32 devices in a mesh: dp: 4 (over z), ctx: 4 (over y, core), fsdp: 2 (over x).
Axes of the slice: x: 2, y: 2, z: 4, core: 2. Of those that a mesh axis runs over, the one named last changes fastest.
Arguments:
- tokens: bfloat16 [8, 1024, 2048], P(('dp', 'fsdp'), 'ctx'), may hold values from -6 to 6
- segment_ids: int32 [8, 1024], P(('dp', 'fsdp'), 'ctx'), may hold values from 0 to 2, as said below
- cotangent: bfloat16 [8, 1024, 2048], P(('dp', 'fsdp'), 'ctx'), may hold values from -6 to 6
- ln1_gain: bfloat16 [2048], P(('dp', 'fsdp')), may hold values from 0.5 to 1.5
- ln1_bias: bfloat16 [2048], P(('dp', 'fsdp')), may hold values from -1.796875 to 1.796875
- w_qkv: bfloat16 [2048, 6144], P(('dp', 'fsdp')), may hold values from -0.125 to 0.125
- b_qkv: bfloat16 [6144], P(('dp', 'fsdp')), may hold values from -3 to 3
- w_out: bfloat16 [2048, 2048], P(('dp', 'fsdp')), may hold values from -2 to 2
- ln2_gain: bfloat16 [2048], P(('dp', 'fsdp')), may hold values from 0.29882812 to 3
- ln2_bias: bfloat16 [2048], P(('dp', 'fsdp')), may hold values from -1.796875 to 1.796875
- w_gate_up: bfloat16 [2048, 11264], P(('dp', 'fsdp')), may hold values from -0.125 to 0.125
- w_down: bfloat16 [5632, 2048], P(('dp', 'fsdp')), may hold values from -0.078125 to 0.078125
Outputs:
- mixed: bfloat16 [8, 1024, 2048], P(('dp', 'fsdp'), 'ctx')
- input_grad: float32 [8, 1024, 2048], P(('dp', 'fsdp'), 'ctx')
- ln1_gain_grad: float32 [2048], P(('dp', 'fsdp'))
- ln1_bias_grad: float32 [2048], P(('dp', 'fsdp'))
- w_qkv_grad: float32 [2048, 6144], P(('dp', 'fsdp'))
- b_qkv_grad: float32 [6144], P(('dp', 'fsdp'))
- w_out_grad: float32 [2048, 2048], P(('dp', 'fsdp'))
- ln2_gain_grad: float32 [2048], P(('dp', 'fsdp'))
- ln2_bias_grad: float32 [2048], P(('dp', 'fsdp'))
- w_gate_up_grad: float32 [2048, 11264], P(('dp', 'fsdp'))
- w_down_grad: float32 [5632, 2048], P(('dp', 'fsdp'))
The draws below stay inside these ranges and needn't reach their ends.
Inputs may be any that keep to these rules, and one draw needn't show every extreme that they name: `segment_ids`: in every row the ids never fall and the row holds exactly three nonempty documents, numbered 0, 1 and 2 in order.
All inputs are finite; a program needn't handle non-finite values.
Results may differ from the reference program's by a relative error of at most 0.02.
Values may be sent and summed in bfloat16 or wider, within the bound.
No kernel may reach another device: no remote copies, remote signals or barrier semaphores. Data moves between devices by JAX's collectives and lax.ppermute only.
A program may use at most 512 MiB of HBM per device.

```python
import math
import jax
import jax.numpy as jnp
from jax import lax

D = 2048
H = 32
E = 64
FF = 5632
ROT = 16
LEN = 1024
TOKS = 256
SEQS = 8


def draw_segment_ids(key, part):
    key = jax.random.fold_in(key, 7)
    first_key, second_key = jax.random.split(key)
    first_cut = jax.random.randint(first_key, (SEQS, 1), 1, TOKS // 2 + 1)
    last_cut = LEN - jax.random.randint(second_key, (SEQS, 1), 1, TOKS // 2 + 1)
    positions = jnp.arange(LEN, dtype=jnp.int32)[None, :]
    return (positions >= first_cut).astype(jnp.int32) + (positions >= last_cut).astype(jnp.int32)


def levels(rng, dims, cuts, low, high):
    gain = 1.0
    for axis_at, parts in cuts:
        draws = jax.random.uniform(jax.random.fold_in(jax.random.fold_in(rng, 6), axis_at), (parts,), jnp.float32, low / len(cuts), high / len(cuts))
        gain = gain * jnp.repeat(jnp.exp(draws), dims[axis_at] // parts).reshape((-1,) + (1,) * (len(dims) - 1 - axis_at))
    return gain


def bell_draw(stream_key, dims, width, bound, cuts=(), kind=jnp.bfloat16):
    loudness = levels(stream_key, dims, cuts, -0.22, 0.18) if cuts else 1.0
    entries = jax.random.normal(stream_key, dims, jnp.float32) * width * loudness
    return jnp.minimum(jnp.maximum(entries, -bound), bound).astype(kind)


def setup_inputs(seed: int = 0) -> dict:
    seeds = jax.random.split(jax.random.key(seed), 13)
    tokens = bell_draw(seeds[0], (SEQS, LEN, D), 1.0, 6.0, ((0, 8), (1, 4)))
    segment_ids = draw_segment_ids(jax.random.fold_in(seeds[12], 71), 0)
    cotangent = bell_draw(seeds[2], (SEQS, LEN, D), 1.0, 6.0, ((0, 8), (1, 4)))
    ln1_gain = jnp.clip(1.0 + 0.1 * jax.random.normal(seeds[3], (D,), jnp.float32), 0.5, 1.5).astype(jnp.bfloat16)
    ln1_bias = bell_draw(seeds[4], (D,), 0.3, 1.796875, ((0, 8),))
    w_qkv = bell_draw(seeds[5], (D, 3 * D), D ** -0.5, 0.125, ((0, 8),))
    b_qkv = bell_draw(seeds[6], (3 * D,), 0.5, 3.0, ((0, 8),))
    w_out = bell_draw(seeds[7], (D, D), (max(1, D // 256)) ** -0.5, 2.0, ((0, 8),))
    ln2_gain = jnp.clip(jnp.exp(math.log(3.0) - 2.306499 * jax.random.uniform(seeds[8], (D,), jnp.float32) ** levels(seeds[8], (D,), ((0, 8),), -0.2, 0.2)), 0.29882812, 3.0).astype(jnp.bfloat16)
    ln2_bias = bell_draw(seeds[9], (D,), 0.3, 1.796875, ((0, 8),))
    w_gate_up = bell_draw(seeds[10], (D, 2 * FF), D ** -0.5, 0.125, ((0, 8),))
    w_down = bell_draw(seeds[11], (FF, D), FF ** -0.5, 0.078125, ((0, 8),))
    return dict(tokens=tokens, segment_ids=segment_ids, cotangent=cotangent, ln1_gain=ln1_gain, ln1_bias=ln1_bias, w_qkv=w_qkv, b_qkv=b_qkv, w_out=w_out, ln2_gain=ln2_gain, ln2_bias=ln2_bias, w_gate_up=w_gate_up, w_down=w_down)


@jax.custom_vjp
def low(v):
    return lax.optimization_barrier(v.astype(jnp.bfloat16)).astype(jnp.float32)

@jax.custom_vjp
def low_back(v):
    return v

def low_keep(v):
    return (low(v), None)

def low_pass(kept, grad):
    return (grad,)

def back_keep(v):
    return (v, None)

def back_low(kept, grad):
    return (low(grad),)
low.defvjp(low_keep, low_pass)
low_back.defvjp(back_keep, back_low)
highest = lax.Precision.HIGHEST
masked_score = -1e+30

def matmul(left, right):
    return jnp.dot(left, right, precision=highest, preferred_element_type=jnp.float32)

def layer_norm(values, scale_gain, shift_bias):
    average = lax.optimization_barrier(jnp.mean(values, axis=-1, keepdims=True))
    centred = values - average
    variance = lax.optimization_barrier(jnp.mean(centred * centred, axis=-1, keepdims=True))
    return centred * lax.rsqrt(variance + 1e-05) * scale_gain + shift_bias

def rotate(values, positions):
    half = ROT // 2
    freqs = 10000.0 ** (-jnp.arange(half, dtype=jnp.float32) * 2.0 / ROT)
    angles = positions.astype(jnp.float32)[:, None] * freqs[None, :]
    cosine = jnp.cos(angles)[:, None, :]
    sine = jnp.sin(angles)[:, None, :]
    first = values[..., :half]
    second = values[..., half:ROT]
    return jnp.concatenate([first * cosine - second * sine, second * cosine + first * sine, values[..., ROT:]], axis=-1)

def attend(queries, keys, values, segments):
    length = queries.shape[0]
    block = math.gcd(length, 512)
    count = length // block
    positions = jnp.arange(length, dtype=jnp.int32)
    scale = E ** (-0.5)

    def one_block(items):
        query_blk, query_pos, query_seg = items
        scores = low_back(jnp.einsum('qhe,khe->hqk', query_blk, keys, precision=highest) * scale)
        allowed = (positions[None, :] <= query_pos[:, None]) & (segments[None, :] == query_seg[:, None])
        weights = jax.nn.softmax(jnp.where(allowed[None], scores, masked_score), axis=-1)
        return jnp.einsum('hqk,khe->qhe', low(weights), values, precision=highest)
    pieces = lax.map(jax.checkpoint(one_block), (queries.reshape(count, block, H, E), positions.reshape(count, block), segments.reshape(count, block)))
    return pieces.reshape(length, H * E)

def forward(inputs, params, segments):
    ln1_gain, ln1_bias, w_qkv, b_qkv, w_out, ln2_gain, ln2_bias, w_gate_up, w_down = params
    length = inputs.shape[0]
    positions = jnp.arange(length, dtype=jnp.int32)
    normed_one = low(layer_norm(inputs, ln1_gain, ln1_bias))
    projected = low_back(matmul(normed_one, w_qkv) + b_qkv)
    queries = low(rotate(projected[:, :D].reshape(length, H, E), positions))
    keys = low(rotate(projected[:, D:2 * D].reshape(length, H, E), positions))
    values = low(projected[:, 2 * D:].reshape(length, H, E))
    attended = low(low_back(attend(queries, keys, values, segments)))
    attn_branch = low_back(matmul(attended, w_out))
    hidden = inputs + attn_branch
    normed_two = low(layer_norm(hidden, ln2_gain, ln2_bias))
    gate_up = low_back(matmul(normed_two, w_gate_up))
    activ = low(jax.nn.silu(gate_up[:, :FF]) * gate_up[:, FF:])
    mlp_branch = low_back(matmul(activ, w_down))
    return hidden + mlp_branch

def reference(tokens, segment_ids, cotangent, ln1_gain, ln1_bias, w_qkv, b_qkv, w_out, ln2_gain, ln2_bias, w_gate_up, w_down):
    params = tuple((weight_arg.astype(jnp.float32) for weight_arg in (ln1_gain, ln1_bias, w_qkv, b_qkv, w_out, ln2_gain, ln2_bias, w_gate_up, w_down)))

    def one_sequence(grad_sums, items):
        seq_tokens, seq_segments, seq_cotangent = items

        def apply_block(inputs, *weights):
            return forward(inputs, weights, seq_segments)
        output, pullback = jax.vjp(apply_block, seq_tokens.astype(jnp.float32), *params)
        grads = pullback(seq_cotangent.astype(jnp.float32))
        new_sums = tuple((running + fresh for running, fresh in zip(grad_sums, grads[1:])))
        return (new_sums, (output.astype(jnp.bfloat16), grads[0]))
    zero_sums = tuple((jnp.zeros(param.shape, jnp.float32) for param in params))
    sums, (outputs, input_grads) = lax.scan(one_sequence, zero_sums, (tokens, segment_ids, cotangent))
    return (outputs, input_grads, sums[0], sums[1], sums[2], sums[3], sums[4], sums[5], sums[6], sums[7], sums[8])
```

```python
import jax
import jax.numpy as jnp
from jax import lax
from jax.sharding import PartitionSpec as P

D = 2048
H = 32
E = 64
FF = 5632
ROT = 16

epsilon = 1e-05
masked_score = -1e30
scale = E ** (-0.5)


def swap(block, axis, bit):
    count = lax.axis_size(axis)
    return lax.ppermute(block, axis, [(i, i ^ bit) for i in range(count)])


def tie(value, *others):
    return lax.optimization_barrier((value, *others))[0]


def shard_index():
    return lax.axis_index("dp") * lax.axis_size("fsdp") + lax.axis_index("fsdp")


def gather_shards(block):
    near = [block] + [swap(block, "dp", r) for r in range(1, lax.axis_size("dp"))]
    blocks = []
    for part in near:
        blocks.append(part)
        for r in range(1, lax.axis_size("fsdp")):
            blocks.append(swap(part, "fsdp", r))
    return blocks


def scatter_shards(blocks):
    far = lax.axis_size("dp")
    wide = lax.axis_size("fsdp")
    parts = blocks.reshape((far, wide) + blocks.shape[1:])
    total = parts[:, 0]
    for r in range(1, wide):
        total = total + swap(parts[:, r].astype(jnp.bfloat16), "fsdp", r).astype(jnp.float32)
    mine = total[0]
    for r in range(1, far):
        mine = mine + swap(total[r].astype(jnp.bfloat16), "dp", r).astype(jnp.float32)
    return mine


def ctx_gather(block):
    count = lax.axis_size("ctx")
    found = {0: block}
    bit = count // 2
    while bit >= 1:
        for r in list(found):
            found[r | bit] = swap(found[r], "ctx", bit)
        bit //= 2
    return [found[r] for r in range(count)]


def ctx_scatter(rows):
    count = lax.axis_size("ctx")
    size = rows.shape[0] // count
    parts = {r: rows[r * size : (r + 1) * size] for r in range(count)}
    bit = 1
    while bit < count:
        parts = {
            r: parts[r]
            + swap(parts[r | bit].astype(jnp.bfloat16), "ctx", bit).astype(jnp.float32)
            for r in parts
            if not r & bit
        }
        bit *= 2
    return parts[0]


def reorder(array, index, axis):
    count = array.shape[axis]
    bit = 1
    while bit < count:
        shape = array.shape[:axis] + (count // (2 * bit), 2, bit) + array.shape[axis + 1 :]
        split = array.reshape(shape)
        first = lax.index_in_dim(split, 0, axis + 1, keepdims=True)
        second = lax.index_in_dim(split, 1, axis + 1, keepdims=True)
        flip = (index & bit) != 0
        split = jnp.concatenate(
            [jnp.where(flip, second, first), jnp.where(flip, first, second)], axis=axis + 1
        )
        array = split.reshape(array.shape)
        bit *= 2
    return array


def layer_stats(values):
    average = jnp.mean(values, axis=-1, keepdims=True)
    centred = values - average
    variance = jnp.mean(centred * centred, axis=-1, keepdims=True)
    inverse = lax.rsqrt(variance + epsilon)
    return (centred * inverse, inverse)


def layer_norm_back(grad_normed, normal, inverse, scale_gain):
    grad_scaled = grad_normed * scale_gain
    first_mean = jnp.mean(grad_scaled, axis=-1, keepdims=True)
    second_mean = jnp.mean(grad_scaled * normal, axis=-1, keepdims=True)
    return inverse * (grad_scaled - first_mean - normal * second_mean)


def rotary_tables(positions):
    half = ROT // 2
    freqs = 10000.0 ** (-jnp.arange(half, dtype=jnp.float32) * 2.0 / ROT)
    angles = positions.astype(jnp.float32)[:, None] * freqs[None, :]
    return (jnp.cos(angles)[:, None, :], jnp.sin(angles)[:, None, :])


def rotate(values, cosine, sine):
    half = ROT // 2
    first = values[..., :half]
    second = values[..., half:ROT]
    return jnp.concatenate(
        [first * cosine - second * sine, second * cosine + first * sine, values[..., ROT:]], axis=-1
    )


def mul(left, right):
    return jnp.dot(left, right, preferred_element_type=jnp.float32)


def contract_rows(left, right):
    return lax.dot_general(
        left, right, (((0,), (0,)), ((), ())), preferred_element_type=jnp.float32
    )


def contract_cols(left, right):
    return lax.dot_general(
        left, right, (((1,), (1,)), ((), ())), preferred_element_type=jnp.float32
    )


def pick(array, index, axis):
    return lax.dynamic_index_in_dim(array, index, axis, keepdims=False)


def body(
    tokens,
    segment_ids,
    cotangent,
    ln1_gain,
    ln1_bias,
    w_qkv,
    b_qkv,
    w_out,
    ln2_gain,
    ln2_bias,
    w_gate_up,
    w_down,
):
    rows = tokens.shape[1]
    count = lax.axis_size("ctx")
    ctx = lax.axis_index("ctx")
    shards = lax.axis_size("dp") * lax.axis_size("fsdp")
    shard = shard_index()
    length = rows * count
    depth = D // shards
    heads = H // count
    even = (H // shards) % count == 0

    if even:
        qkv_mine = pick(w_qkv.reshape(depth, 3, shards, count, -1), ctx, 3).reshape(depth, -1)
        out_mine = pick(w_out.reshape(count, -1, D), ctx, 0)
    else:
        qkv_mine = pick(w_qkv.reshape(depth, 3, count, -1), ctx, 2).reshape(depth, -1)
        out_mine = w_out
    gate_up_mine = pick(w_gate_up.reshape(depth, 2, shards, count, -1), ctx, 3).reshape(depth, -1)
    down_mine = pick(w_down.reshape(count, -1, D), ctx, 0)

    small = jnp.concatenate([ln1_gain, ln1_bias, ln2_gain, ln2_bias, b_qkv])
    small_all = reorder(jnp.stack(gather_shards(small)), shard, 0).astype(jnp.float32)
    gain_one = small_all[:, :depth].reshape(D)
    bias_one = small_all[:, depth : 2 * depth].reshape(D)
    gain_two = small_all[:, 2 * depth : 3 * depth].reshape(D)
    bias_two = small_all[:, 3 * depth : 4 * depth].reshape(D)
    qkv_bias = small_all[:, 4 * depth :].reshape(3 * D)
    if even:
        bias_mine = pick(qkv_bias.reshape(3, shards, count, -1), ctx, 2).reshape(-1)
    else:
        bias_mine = pick(qkv_bias.reshape(3, count, -1), ctx, 1).reshape(-1)

    token_rows = jnp.concatenate(ctx_gather(tokens[0]), axis=0)
    segments = jnp.concatenate(ctx_gather(segment_ids), axis=1)[0]
    positions = jnp.concatenate(
        [(ctx ^ r) * rows + jnp.arange(rows, dtype=jnp.int32) for r in range(count)]
    )
    cosine, sine = rotary_tables(positions)

    qkv_all = jnp.concatenate(gather_shards(qkv_mine), axis=0)
    out_all = jnp.stack(gather_shards(tie(out_mine, qkv_all)))
    out_all = reorder(out_all, shard, 0).reshape(-1, D)
    if not even:
        out_all = pick(out_all.reshape(count, -1, D), ctx, 0)
    gate_up_all = jnp.concatenate(gather_shards(tie(gate_up_mine, qkv_all)), axis=0)
    cot_rows = jnp.concatenate(ctx_gather(tie(cotangent[0], token_rows)), axis=0)
    down_all = jnp.stack(gather_shards(tie(down_mine, gate_up_all)))
    down_all = reorder(down_all, shard, 0).reshape(-1, D)

    def to_shard_order(array):
        n = array.shape[0]
        return reorder(array.reshape(n, shards, depth), shard, 1).reshape(n, D)

    normal_one, inverse_one = layer_stats(token_rows.astype(jnp.float32))
    normed_one = to_shard_order((normal_one * gain_one + bias_one).astype(jnp.bfloat16))
    projected = mul(normed_one, qkv_all) + bias_mine
    width = heads * E
    queries = rotate(projected[:, :width].reshape(length, heads, E), cosine, sine).astype(
        jnp.bfloat16
    )
    keys = rotate(projected[:, width : 2 * width].reshape(length, heads, E), cosine, sine).astype(
        jnp.bfloat16
    )
    values = projected[:, 2 * width :].reshape(length, heads, E).astype(jnp.bfloat16)
    allowed = (positions[None, :] <= positions[:, None]) & (segments[None, :] == segments[:, None])
    scores = jnp.einsum("qhe,khe->hqk", queries, keys, preferred_element_type=jnp.float32) * scale
    scores = jnp.where(allowed[None], scores, masked_score)
    top = jnp.max(scores, axis=-1, keepdims=True)
    weights = jnp.exp(scores - top)
    weights = weights / jnp.sum(weights, axis=-1, keepdims=True)
    low_weights = weights.astype(jnp.bfloat16)
    attended_f = jnp.einsum("hqk,khe->qhe", low_weights, values, preferred_element_type=jnp.float32)
    attended = attended_f.reshape(length, width).astype(jnp.bfloat16)

    hidden = tokens[0].astype(jnp.float32) + ctx_scatter(mul(attended, out_all))
    normal_two, inverse_two = layer_stats(hidden)
    normed_two = to_shard_order((normal_two * gain_two + bias_two).astype(jnp.bfloat16))
    normed_two = jnp.concatenate(ctx_gather(normed_two), axis=0)
    gate_up = mul(normed_two, gate_up_all)
    units = FF // count
    gate = gate_up[:, :units]
    upward = gate_up[:, units:]
    sigma = jax.nn.sigmoid(gate)
    swish = gate * sigma
    activ = (swish * upward).astype(jnp.bfloat16)
    mixed = hidden + ctx_scatter(mul(activ, down_all))

    grad_activ = contract_cols(cot_rows, down_all)
    grad_gate = grad_activ * upward * sigma * (1.0 + gate * (1.0 - sigma))
    grad_up = grad_activ * swish
    grad_gate_up = jnp.concatenate([grad_gate, grad_up], axis=1).astype(jnp.bfloat16)
    down_part = contract_rows(activ, cot_rows).reshape(shards, -1, D)
    down_grad = scatter_shards(reorder(down_part, shard, 0))
    gate_up_part = contract_rows(normed_two, grad_gate_up).reshape(shards, depth, 2 * units)
    gate_up_grad = scatter_shards(tie(gate_up_part, down_grad))

    grad_normed_two = ctx_scatter(contract_cols(grad_gate_up, gate_up_all))
    grad_normed_two = to_shard_order(grad_normed_two)
    gain_two_grad = jnp.sum(grad_normed_two * normal_two, axis=0)
    bias_two_grad = jnp.sum(grad_normed_two, axis=0)
    grad_hidden = cotangent[0].astype(jnp.float32) + layer_norm_back(
        grad_normed_two, normal_two, inverse_two, gain_two
    )
    grad_branch = jnp.concatenate(ctx_gather(grad_hidden.astype(jnp.bfloat16)), axis=0)

    grad_attended = contract_cols(grad_branch, out_all).astype(jnp.bfloat16)
    out_part = contract_rows(attended, grad_branch)
    grad_heads = grad_attended.reshape(length, heads, E)
    grad_weights = jnp.einsum("qhe,khe->hqk", grad_heads, values, preferred_element_type=jnp.float32)
    delta = jnp.sum(weights * grad_weights, axis=-1, keepdims=True)
    grad_scores = (weights * (grad_weights - delta)).astype(jnp.bfloat16)
    grad_queries = (
        jnp.einsum("hqk,khe->qhe", grad_scores, keys, preferred_element_type=jnp.float32) * scale
    )
    grad_keys = (
        jnp.einsum("hqk,qhe->khe", grad_scores, queries, preferred_element_type=jnp.float32) * scale
    )
    grad_values = jnp.einsum(
        "hqk,qhe->khe", low_weights, grad_heads, preferred_element_type=jnp.float32
    )
    grad_qkv = jnp.concatenate(
        [
            rotate(grad_queries, cosine, -sine).reshape(length, width),
            rotate(grad_keys, cosine, -sine).reshape(length, width),
            grad_values.reshape(length, width),
        ],
        axis=1,
    ).astype(jnp.bfloat16)
    qkv_bias_part = jnp.sum(grad_qkv.astype(jnp.float32), axis=0)
    qkv_part = contract_rows(normed_one, grad_qkv).reshape(shards, depth, 3 * width)

    grad_normed_one = to_shard_order(ctx_scatter(contract_cols(grad_qkv, qkv_all)))
    normal_mine = normal_one[:rows]
    gain_one_grad = jnp.sum(grad_normed_one * normal_mine, axis=0)
    bias_one_grad = jnp.sum(grad_normed_one, axis=0)
    input_grad = grad_hidden + layer_norm_back(
        grad_normed_one, normal_mine, inverse_one[:rows], gain_one
    )

    qkv_grad = scatter_shards(tie(qkv_part, gate_up_grad))

    def ctx_blocks(block):
        found = jnp.stack(ctx_gather(block.astype(jnp.bfloat16)))
        return reorder(found, ctx, 0).astype(jnp.float32)

    down_out = ctx_blocks(down_grad).reshape(-1, D)
    gate_up_out = ctx_blocks(gate_up_grad).reshape(count, depth, 2, shards, -1)
    gate_up_out = gate_up_out.transpose(1, 2, 3, 0, 4).reshape(depth, 2 * FF)
    if even:
        out_part = out_part.reshape(shards, -1, D)
        out_out = ctx_blocks(scatter_shards(reorder(out_part, shard, 0))).reshape(-1, D)
        qkv_out = ctx_blocks(qkv_grad).reshape(count, depth, 3, shards, -1)
        qkv_out = qkv_out.transpose(1, 2, 3, 0, 4).reshape(depth, 3 * D)
        qkv_bias_rows = ctx_blocks(qkv_bias_part).reshape(count, 3, shards, -1)
        qkv_bias_rows = qkv_bias_rows.transpose(1, 2, 0, 3).reshape(shards, -1)
    else:
        spread = jnp.zeros((count,) + out_part.shape, jnp.float32)
        spread = lax.dynamic_update_index_in_dim(spread, out_part, ctx, 0)
        out_part = spread.reshape(shards, depth, D)
        out_out = scatter_shards(reorder(out_part, shard, 0))
        out_out = lax.psum(out_out.astype(jnp.bfloat16), "ctx").astype(jnp.float32)
        qkv_out = ctx_blocks(qkv_grad).reshape(count, depth, 3, -1)
        qkv_out = qkv_out.transpose(1, 2, 0, 3).reshape(depth, 3 * D)
        qkv_bias_rows = ctx_blocks(qkv_bias_part).reshape(count, 3, -1)
        qkv_bias_rows = qkv_bias_rows.transpose(1, 0, 2).reshape(shards, -1)

    norm_parts = jnp.concatenate(
        [
            part.reshape(shards, depth)
            for part in (gain_one_grad, bias_one_grad, gain_two_grad, bias_two_grad)
        ],
        axis=1,
    )
    bit = 1
    while bit < count:
        norm_parts = norm_parts + swap(norm_parts, "ctx", bit)
        bit *= 2
    small_parts = jnp.concatenate([norm_parts, qkv_bias_rows], axis=1)
    small_grad = scatter_shards(reorder(small_parts, shard, 0))

    return (
        mixed.astype(jnp.bfloat16)[None],
        input_grad[None],
        small_grad[:depth],
        small_grad[depth : 2 * depth],
        qkv_out,
        small_grad[4 * depth :],
        out_out,
        small_grad[2 * depth : 3 * depth],
        small_grad[3 * depth : 4 * depth],
        gate_up_out,
        down_out,
    )


def solution(mesh):
    shards = ("dp", "fsdp")
    row = P(shards, "ctx", None)
    vector = P(shards)
    matrix = P(shards, None)
    return jax.shard_map(
        body,
        mesh=mesh,
        in_specs=(
            row,
            P(shards, "ctx"),
            row,
            vector,
            vector,
            matrix,
            vector,
            matrix,
            vector,
            vector,
            matrix,
            matrix,
        ),
        out_specs=(
            row,
            row,
            vector,
            vector,
            matrix,
            vector,
            matrix,
            vector,
            vector,
            matrix,
            matrix,
        ),
        check_vma=False,
    )
```

```python
import math

import jax
import jax.numpy as jnp
from jax import lax
from jax.experimental import pallas as pl
from jax.experimental.pallas import tpu as pltpu
from jax.sharding import PartitionSpec as P

D = 2048
H = 32
E = 64
FF = 5632
ROT = 16

epsilon = 1e-05
masked_score = -1e30
scale = E ** (-0.5)


def swap(block, axis, bit):
    count = lax.axis_size(axis)
    return lax.ppermute(block, axis, [(i, i ^ bit) for i in range(count)])


def tie(value, *others):
    return lax.optimization_barrier((value, *others))[0]


def shard_index():
    return lax.axis_index("dp") * lax.axis_size("fsdp") + lax.axis_index("fsdp")


def gather_shards(block):
    near = [block] + [swap(block, "dp", r) for r in range(1, lax.axis_size("dp"))]
    blocks = []
    for part in near:
        blocks.append(part)
        for r in range(1, lax.axis_size("fsdp")):
            blocks.append(swap(part, "fsdp", r))
    return blocks


def scatter_shards(blocks):
    far = lax.axis_size("dp")
    wide = lax.axis_size("fsdp")
    parts = blocks.reshape((far, wide) + blocks.shape[1:])
    total = parts[:, 0]
    for r in range(1, wide):
        total = total + swap(parts[:, r].astype(jnp.bfloat16), "fsdp", r).astype(jnp.float32)
    mine = total[0]
    for r in range(1, far):
        mine = mine + swap(total[r].astype(jnp.bfloat16), "dp", r).astype(jnp.float32)
    return mine


def ctx_gather(block):
    count = lax.axis_size("ctx")
    found = {0: block}
    bit = count // 2
    while bit >= 1:
        for r in list(found):
            found[r | bit] = swap(found[r], "ctx", bit)
        bit //= 2
    return [found[r] for r in range(count)]


def ctx_scatter(rows):
    count = lax.axis_size("ctx")
    size = rows.shape[0] // count
    parts = {r: rows[r * size : (r + 1) * size] for r in range(count)}
    bit = 1
    while bit < count:
        parts = {
            r: parts[r]
            + swap(parts[r | bit].astype(jnp.bfloat16), "ctx", bit).astype(jnp.float32)
            for r in parts
            if not r & bit
        }
        bit *= 2
    return parts[0]


def reorder(array, index, axis):
    count = array.shape[axis]
    bit = 1
    while bit < count:
        shape = array.shape[:axis] + (count // (2 * bit), 2, bit) + array.shape[axis + 1 :]
        split = array.reshape(shape)
        first = lax.index_in_dim(split, 0, axis + 1, keepdims=True)
        second = lax.index_in_dim(split, 1, axis + 1, keepdims=True)
        flip = (index & bit) != 0
        split = jnp.concatenate(
            [jnp.where(flip, second, first), jnp.where(flip, first, second)], axis=axis + 1
        )
        array = split.reshape(array.shape)
        bit *= 2
    return array


def layer_stats(values):
    average = jnp.mean(values, axis=-1, keepdims=True)
    centred = values - average
    variance = jnp.mean(centred * centred, axis=-1, keepdims=True)
    inverse = lax.rsqrt(variance + epsilon)
    return (centred * inverse, inverse)


def layer_norm_back(grad_normed, normal, inverse, scale_gain):
    grad_scaled = grad_normed * scale_gain
    first_mean = jnp.mean(grad_scaled, axis=-1, keepdims=True)
    second_mean = jnp.mean(grad_scaled * normal, axis=-1, keepdims=True)
    return inverse * (grad_scaled - first_mean - normal * second_mean)


def rotary_tables(positions):
    half = ROT // 2
    freqs = 10000.0 ** (-jnp.arange(half, dtype=jnp.float32) * 2.0 / ROT)
    angles = positions.astype(jnp.float32)[:, None] * freqs[None, :]
    return (jnp.cos(angles)[:, None, :], jnp.sin(angles)[:, None, :])


def rotate(values, cosine, sine):
    half = ROT // 2
    first = values[..., :half]
    second = values[..., half:ROT]
    return jnp.concatenate(
        [first * cosine - second * sine, second * cosine + first * sine, values[..., ROT:]], axis=-1
    )


def mul(left, right):
    return jnp.dot(left, right, preferred_element_type=jnp.float32)


def contract_rows(left, right):
    return lax.dot_general(
        left, right, (((0,), (0,)), ((), ())), preferred_element_type=jnp.float32
    )


def contract_cols(left, right):
    return lax.dot_general(
        left, right, (((1,), (1,)), ((), ())), preferred_element_type=jnp.float32
    )


def pick(array, index, axis):
    return lax.dynamic_index_in_dim(array, index, axis, keepdims=False)


def body(
    tokens,
    segment_ids,
    cotangent,
    ln1_gain,
    ln1_bias,
    w_qkv,
    b_qkv,
    w_out,
    ln2_gain,
    ln2_bias,
    w_gate_up,
    w_down,
):
    rows = tokens.shape[1]
    count = lax.axis_size("ctx")
    ctx = lax.axis_index("ctx")
    shards = lax.axis_size("dp") * lax.axis_size("fsdp")
    shard = shard_index()
    length = rows * count
    depth = D // shards
    heads = H // count
    even = (H // shards) % count == 0

    if even:
        qkv_mine = pick(w_qkv.reshape(depth, 3, shards, count, -1), ctx, 3).reshape(depth, -1)
        out_mine = pick(w_out.reshape(count, -1, D), ctx, 0)
    else:
        qkv_mine = pick(w_qkv.reshape(depth, 3, count, -1), ctx, 2).reshape(depth, -1)
        out_mine = w_out
    gate_up_mine = pick(w_gate_up.reshape(depth, 2, shards, count, -1), ctx, 3).reshape(depth, -1)
    down_mine = pick(w_down.reshape(count, -1, D), ctx, 0)

    small = jnp.concatenate([ln1_gain, ln1_bias, ln2_gain, ln2_bias, b_qkv])
    small_all = reorder(jnp.stack(gather_shards(small)), shard, 0).astype(jnp.float32)
    gain_one = small_all[:, :depth].reshape(D)
    bias_one = small_all[:, depth : 2 * depth].reshape(D)
    gain_two = small_all[:, 2 * depth : 3 * depth].reshape(D)
    bias_two = small_all[:, 3 * depth : 4 * depth].reshape(D)
    qkv_bias = small_all[:, 4 * depth :].reshape(3 * D)
    if even:
        bias_mine = pick(qkv_bias.reshape(3, shards, count, -1), ctx, 2).reshape(-1)
    else:
        bias_mine = pick(qkv_bias.reshape(3, count, -1), ctx, 1).reshape(-1)

    token_rows = jnp.concatenate(ctx_gather(tokens[0]), axis=0)
    segments = jnp.concatenate(ctx_gather(segment_ids), axis=1)[0]
    positions = jnp.concatenate(
        [(ctx ^ r) * rows + jnp.arange(rows, dtype=jnp.int32) for r in range(count)]
    )
    cosine, sine = rotary_tables(positions)

    qkv_all = jnp.concatenate(gather_shards(qkv_mine), axis=0)
    out_all = jnp.stack(gather_shards(tie(out_mine, qkv_all)))
    out_all = reorder(out_all, shard, 0).reshape(-1, D)
    if not even:
        out_all = pick(out_all.reshape(count, -1, D), ctx, 0)
    gate_up_all = jnp.concatenate(gather_shards(tie(gate_up_mine, qkv_all)), axis=0)
    cot_rows = jnp.concatenate(ctx_gather(tie(cotangent[0], token_rows)), axis=0)
    down_all = jnp.stack(gather_shards(tie(down_mine, gate_up_all)))
    down_all = reorder(down_all, shard, 0).reshape(-1, D)

    def to_shard_order(array):
        n = array.shape[0]
        return reorder(array.reshape(n, shards, depth), shard, 1).reshape(n, D)

    normal_one, inverse_one = layer_stats(token_rows.astype(jnp.float32))
    normed_one = to_shard_order((normal_one * gain_one + bias_one).astype(jnp.bfloat16))
    projected = mul(normed_one, qkv_all) + bias_mine
    width = heads * E
    queries = rotate(projected[:, :width].reshape(length, heads, E), cosine, sine).astype(
        jnp.bfloat16
    )
    keys = rotate(projected[:, width : 2 * width].reshape(length, heads, E), cosine, sine).astype(
        jnp.bfloat16
    )
    values = projected[:, 2 * width :].reshape(length, heads, E).astype(jnp.bfloat16)
    allowed = (positions[None, :] <= positions[:, None]) & (segments[None, :] == segments[:, None])
    scores = jnp.einsum("qhe,khe->hqk", queries, keys, preferred_element_type=jnp.float32) * scale
    scores = jnp.where(allowed[None], scores, masked_score)
    top = jnp.max(scores, axis=-1, keepdims=True)
    weights = jnp.exp(scores - top)
    weights = weights / jnp.sum(weights, axis=-1, keepdims=True)
    low_weights = weights.astype(jnp.bfloat16)
    attended_f = jnp.einsum("hqk,khe->qhe", low_weights, values, preferred_element_type=jnp.float32)
    attended = attended_f.reshape(length, width).astype(jnp.bfloat16)

    hidden = tokens[0].astype(jnp.float32) + ctx_scatter(mul(attended, out_all))
    normal_two, inverse_two = layer_stats(hidden)
    normed_two = to_shard_order((normal_two * gain_two + bias_two).astype(jnp.bfloat16))
    normed_two = jnp.concatenate(ctx_gather(normed_two), axis=0)
    gate_up = mul(normed_two, gate_up_all)
    units = FF // count
    gate = gate_up[:, :units]
    upward = gate_up[:, units:]
    sigma = jax.nn.sigmoid(gate)
    swish = gate * sigma
    activ = (swish * upward).astype(jnp.bfloat16)
    mixed = hidden + ctx_scatter(mul(activ, down_all))

    grad_activ = contract_cols(cot_rows, down_all)
    grad_gate = grad_activ * upward * sigma * (1.0 + gate * (1.0 - sigma))
    grad_up = grad_activ * swish
    grad_gate_up = jnp.concatenate([grad_gate, grad_up], axis=1).astype(jnp.bfloat16)
    down_part = contract_rows(activ, cot_rows).reshape(shards, -1, D)
    down_grad = scatter_shards(reorder(down_part, shard, 0))
    gate_up_part = contract_rows(normed_two, grad_gate_up).reshape(shards, depth, 2 * units)
    gate_up_grad = scatter_shards(tie(gate_up_part, down_grad))

    grad_normed_two = ctx_scatter(contract_cols(grad_gate_up, gate_up_all))
    grad_normed_two = to_shard_order(grad_normed_two)
    gain_two_grad = jnp.sum(grad_normed_two * normal_two, axis=0)
    bias_two_grad = jnp.sum(grad_normed_two, axis=0)
    grad_hidden = cotangent[0].astype(jnp.float32) + layer_norm_back(
        grad_normed_two, normal_two, inverse_two, gain_two
    )
    grad_branch = jnp.concatenate(ctx_gather(grad_hidden.astype(jnp.bfloat16)), axis=0)

    grad_attended = contract_cols(grad_branch, out_all).astype(jnp.bfloat16)
    out_part = contract_rows(attended, grad_branch)
    grad_heads = grad_attended.reshape(length, heads, E)
    grad_weights = jnp.einsum("qhe,khe->hqk", grad_heads, values, preferred_element_type=jnp.float32)
    delta = jnp.sum(weights * grad_weights, axis=-1, keepdims=True)
    grad_scores = (weights * (grad_weights - delta)).astype(jnp.bfloat16)
    grad_queries = (
        jnp.einsum("hqk,khe->qhe", grad_scores, keys, preferred_element_type=jnp.float32) * scale
    )
    grad_keys = (
        jnp.einsum("hqk,qhe->khe", grad_scores, queries, preferred_element_type=jnp.float32) * scale
    )
    grad_values = jnp.einsum(
        "hqk,qhe->khe", low_weights, grad_heads, preferred_element_type=jnp.float32
    )
    grad_qkv = jnp.concatenate(
        [
            rotate(grad_queries, cosine, -sine).reshape(length, width),
            rotate(grad_keys, cosine, -sine).reshape(length, width),
            grad_values.reshape(length, width),
        ],
        axis=1,
    ).astype(jnp.bfloat16)
    qkv_bias_part = jnp.sum(grad_qkv.astype(jnp.float32), axis=0)
    qkv_part = contract_rows(normed_one, grad_qkv).reshape(shards, depth, 3 * width)

    grad_normed_one = to_shard_order(ctx_scatter(contract_cols(grad_qkv, qkv_all)))
    normal_mine = normal_one[:rows]
    gain_one_grad = jnp.sum(grad_normed_one * normal_mine, axis=0)
    bias_one_grad = jnp.sum(grad_normed_one, axis=0)
    input_grad = grad_hidden + layer_norm_back(
        grad_normed_one, normal_mine, inverse_one[:rows], gain_one
    )

    qkv_grad = scatter_shards(tie(qkv_part, gate_up_grad))

    def ctx_blocks(block):
        found = jnp.stack(ctx_gather(block.astype(jnp.bfloat16)))
        return reorder(found, ctx, 0).astype(jnp.float32)

    down_out = ctx_blocks(down_grad).reshape(-1, D)
    gate_up_out = ctx_blocks(gate_up_grad).reshape(count, depth, 2, shards, -1)
    gate_up_out = gate_up_out.transpose(1, 2, 3, 0, 4).reshape(depth, 2 * FF)
    if even:
        out_part = out_part.reshape(shards, -1, D)
        out_out = ctx_blocks(scatter_shards(reorder(out_part, shard, 0))).reshape(-1, D)
        qkv_out = ctx_blocks(qkv_grad).reshape(count, depth, 3, shards, -1)
        qkv_out = qkv_out.transpose(1, 2, 3, 0, 4).reshape(depth, 3 * D)
        qkv_bias_rows = ctx_blocks(qkv_bias_part).reshape(count, 3, shards, -1)
        qkv_bias_rows = qkv_bias_rows.transpose(1, 2, 0, 3).reshape(shards, -1)
    else:
        spread = jnp.zeros((count,) + out_part.shape, jnp.float32)
        spread = lax.dynamic_update_index_in_dim(spread, out_part, ctx, 0)
        out_part = spread.reshape(shards, depth, D)
        out_out = scatter_shards(reorder(out_part, shard, 0))
        out_out = lax.psum(out_out.astype(jnp.bfloat16), "ctx").astype(jnp.float32)
        qkv_out = ctx_blocks(qkv_grad).reshape(count, depth, 3, -1)
        qkv_out = qkv_out.transpose(1, 2, 0, 3).reshape(depth, 3 * D)
        qkv_bias_rows = ctx_blocks(qkv_bias_part).reshape(count, 3, -1)
        qkv_bias_rows = qkv_bias_rows.transpose(1, 0, 2).reshape(shards, -1)

    norm_parts = jnp.concatenate(
        [
            part.reshape(shards, depth)
            for part in (gain_one_grad, bias_one_grad, gain_two_grad, bias_two_grad)
        ],
        axis=1,
    )
    bit = 1
    while bit < count:
        norm_parts = norm_parts + swap(norm_parts, "ctx", bit)
        bit *= 2
    small_parts = jnp.concatenate([norm_parts, qkv_bias_rows], axis=1)
    small_grad = scatter_shards(reorder(small_parts, shard, 0))

    return (
        mixed.astype(jnp.bfloat16)[None],
        input_grad[None],
        small_grad[:depth],
        small_grad[depth : 2 * depth],
        qkv_out,
        small_grad[4 * depth :],
        out_out,
        small_grad[2 * depth : 3 * depth],
        small_grad[3 * depth : 4 * depth],
        gate_up_out,
        down_out,
    )


def call(kernel, grid, in_specs, out_specs, out_shape, scratch=(), limit=48):
    return pl.pallas_call(
        kernel,
        grid=grid,
        in_specs=in_specs,
        out_specs=out_specs,
        out_shape=out_shape,
        scratch_shapes=list(scratch),
        compiler_params=pltpu.CompilerParams(vmem_limit_bytes=limit * 1024 * 1024),
        cost_estimate=pl.CostEstimate(flops=1, bytes_accessed=1, transcendentals=0),
    )


def sds(shape, dtype):
    return jax.ShapeDtypeStruct(shape, dtype)


def smem():
    return pl.BlockSpec(memory_space=pltpu.SMEM)


def whole(array):
    zeros = (0,) * array.ndim
    return pl.BlockSpec(array.shape, lambda *_: zeros)


def take_columns(places, w, count, shards, groups, pad):
    depth = w.shape[0]
    each = w.shape[1] // groups
    unit = each // (shards * count)
    tile = depth // 4

    def kernel(places_ref, w_ref, o_ref):
        for i in range(count):

            @pl.when(places_ref[0] == i)
            def _():
                o_ref[...] = jnp.concatenate(
                    [
                        w_ref[:, (s * count + i) * unit : (s * count + i + 1) * unit]
                        for s in range(shards)
                    ],
                    axis=1,
                )

    return call(
        kernel,
        (groups, 4),
        [smem(), pl.BlockSpec((tile, each), lambda g, m: (m, g))],
        pl.BlockSpec((tile, each // count), lambda g, m: (m, g)),
        sds((depth + pad, w.shape[1] // count), jnp.bfloat16),
    )(places, w)


def spread_columns(places, near, far, count, shards, groups):
    depth = near.shape[1]
    each = near.shape[2] // groups
    unit = each // shards
    half = count // 2
    tile = depth // 8

    def kernel(places_ref, near_ref, far_ref, o_ref):
        blocks = []
        for i in range(count):
            at = places_ref[1 + i]
            block = jnp.where(
                at < half, near_ref[jnp.minimum(at, half - 1)], far_ref[jnp.maximum(at - half, 0)]
            )
            blocks.append(block.astype(jnp.float32))
        for s in range(shards):
            o_ref[:, s * count * unit : (s + 1) * count * unit] = jnp.concatenate(
                [block[:, s * unit : (s + 1) * unit] for block in blocks], axis=1
            )

    spec = pl.BlockSpec((half, tile, each), lambda g, m: (0, m, g))
    return call(
        kernel,
        (groups, 8),
        [smem(), spec, spec],
        pl.BlockSpec((tile, each * count), lambda g, m: (m, g)),
        sds((depth, groups * each * count), jnp.float32),
    )(places, near, far)


def spread_rows(places, near, far, count):
    half, size, width = near.shape

    def kernel(places_ref, near_ref, far_ref, o_ref):
        at = places_ref[1 + pl.program_id(0)]
        block = jnp.where(
            at < half, near_ref[jnp.minimum(at, half - 1)], far_ref[jnp.maximum(at - half, 0)]
        )
        o_ref[...] = block.astype(jnp.float32)

    return call(
        kernel,
        (count,),
        [smem(), whole(near), whole(far)],
        pl.BlockSpec((size, width), lambda m: (m, 0)),
        sds((count * size, width), jnp.float32),
    )(places, near, far)


def norm_stats(values):
    average = jnp.mean(values, axis=-1, keepdims=True)
    centred = values - average
    inverse = lax.rsqrt(jnp.mean(centred * centred, axis=-1, keepdims=True) + epsilon)
    return centred * inverse, inverse


def norm_columns(places_ref, first, gain_ref, bias_ref, normal, o_ref, plain_ref):
    shards, depth = gain_ref.shape
    plain_ref[...] = normal
    for r in range(shards):
        start = pl.multiple_of(places_ref[first + r] * depth, depth)
        block = plain_ref[:, pl.ds(start, depth)]
        o_ref[:, r * depth : (r + 1) * depth] = (
            block * gain_ref[r : r + 1] + bias_ref[r : r + 1]
        ).astype(jnp.bfloat16)


def norm_tokens(places, tokens, gain, bias, count):
    rows = tokens.shape[0]
    tile = rows // 8

    def kernel(places_ref, x_ref, gain_ref, bias_ref, o_ref, plain_ref):
        normal, _ = norm_stats(x_ref[...].astype(jnp.float32))
        norm_columns(places_ref, 1 + count, gain_ref, bias_ref, normal, o_ref, plain_ref)

    spec = pl.BlockSpec((tile, D), lambda m: (m, 0))
    return call(
        kernel,
        (8,),
        [smem(), spec, whole(gain), whole(bias)],
        spec,
        sds((rows, D), jnp.bfloat16),
        [pltpu.VMEM((tile, D), jnp.float32)],
    )(places, tokens, gain, bias)


def norm_hidden(places, tokens, pieces, gain, bias, count):
    rows = tokens.shape[0]
    tile = rows // 4

    def kernel(places_ref, x_ref, *refs):
        piece_refs = refs[: len(pieces)]
        gain_ref, bias_ref, hidden_ref, o_ref, plain_ref = refs[len(pieces) :]
        hidden = x_ref[...].astype(jnp.float32)
        for ref in piece_refs:
            hidden = hidden + ref[...].astype(jnp.float32)
        hidden_ref[...] = hidden
        normal, _ = norm_stats(hidden)
        norm_columns(places_ref, 1 + count, gain_ref, bias_ref, normal, o_ref, plain_ref)

    spec = pl.BlockSpec((tile, D), lambda m: (m, 0))
    return call(
        kernel,
        (4,),
        [smem()] + [spec] * (1 + len(pieces)) + [whole(gain), whole(bias)],
        [spec, spec],
        [sds((rows, D), jnp.float32), sds((rows, D), jnp.bfloat16)],
        [pltpu.VMEM((tile, D), jnp.float32)],
    )(places, tokens, *pieces, gain, bias)


def norm_back(places, source, pieces, gain, added, count, low):
    rows = source.shape[0]
    tile = rows // 4
    shards, depth = gain.shape

    def kernel(places_ref, x_ref, added_ref, gain_ref, *refs):
        piece_refs = refs[: len(pieces)]
        out_refs = refs[len(pieces) : -2]
        sums_ref = out_refs[-1]
        grad_ref, gain_plain = refs[-2:]
        for r in range(shards):
            start = pl.multiple_of(places_ref[1 + count + r] * depth, depth)
            at = slice(r * depth, (r + 1) * depth)
            block = piece_refs[0][:, at].astype(jnp.float32)
            for ref in piece_refs[1:]:
                block = block + ref[:, at].astype(jnp.float32)
            grad_ref[:, pl.ds(start, depth)] = block
            gain_plain[:, pl.ds(start, depth)] = jnp.broadcast_to(
                gain_ref[r : r + 1], (8, depth)
            )
        normal, inverse = norm_stats(x_ref[...].astype(jnp.float32))
        grad = grad_ref[...]

        @pl.when(pl.program_id(0) == 0)
        def _():
            sums_ref[...] = jnp.zeros_like(sums_ref)

        sums_ref[0:1] += jnp.sum(grad * normal, axis=0, keepdims=True)
        sums_ref[1:2] += jnp.sum(grad, axis=0, keepdims=True)
        scaled = grad * gain_plain[0:1]
        first = jnp.mean(scaled, axis=-1, keepdims=True)
        second = jnp.mean(scaled * normal, axis=-1, keepdims=True)
        total = added_ref[...].astype(jnp.float32) + inverse * (scaled - first - normal * second)
        out_refs[0][...] = total
        if low:
            out_refs[1][...] = total.astype(jnp.bfloat16)

    spec = pl.BlockSpec((tile, D), lambda m: (m, 0))
    sums = pl.BlockSpec((2, D), lambda m: (0, 0))
    return call(
        kernel,
        (4,),
        [smem(), spec, spec, whole(gain)] + [spec] * len(pieces),
        [spec] + [spec] * low + [sums],
        [sds((rows, D), jnp.float32)]
        + [sds((rows, D), jnp.bfloat16)] * low
        + [sds((2, D), jnp.float32)],
        [pltpu.VMEM((tile, D), jnp.float32), pltpu.VMEM((8, D), jnp.float32)],
    )(places, source, added, gain, *pieces)


def column_specs(parts, depth, width, at):
    specs = []
    for part in parts:
        if part.ndim == 2:
            specs.append(pl.BlockSpec((depth, width), lambda *i: (0, at(*i))))
        else:
            lead = part.shape[0]
            specs.append(pl.BlockSpec((lead, depth, width), lambda *i: (0, 0, at(*i))))
    return specs


def times_rows(values, refs, depth):
    total = None
    start = 0
    for ref in refs:
        block = ref[...]
        block = block.reshape(-1, block.shape[-1])
        stop = start + block.shape[0]
        term = jnp.dot(values[:, start:stop], block, preferred_element_type=jnp.float32)
        total = term if total is None else total + term
        start = stop
    return total


def project(normed, parts, bias, tables, depth):
    length = normed.shape[0]
    width = bias.shape[1] // 3
    tile = length // 4

    def kernel(x_ref, a_ref, b_ref, c_ref, d_ref, bias_ref, cos_ref, low_ref, high_ref, o_ref):
        total = times_rows(x_ref[...], (a_ref, b_ref, c_ref, d_ref), depth) + bias_ref[...]

        @pl.when(pl.program_id(0) < 2)
        def _():
            times = width // 128
            cosine = jnp.concatenate([cos_ref[...]] * times, axis=1)
            low = jnp.concatenate([low_ref[...]] * times, axis=1)
            high = jnp.concatenate([high_ref[...]] * times, axis=1)
            turned = (
                total * cosine
                + pltpu.roll(total, width - ROT // 2, 1) * low
                + pltpu.roll(total, ROT // 2, 1) * high
            )
            o_ref[...] = turned.astype(jnp.bfloat16)

        @pl.when(pl.program_id(0) == 2)
        def _():
            o_ref[...] = total.astype(jnp.bfloat16)

    table = pl.BlockSpec((tile, 128), lambda n, m: (m, 0))
    return call(
        kernel,
        (3, 4),
        [pl.BlockSpec((tile, D), lambda n, m: (m, 0))]
        + column_specs(parts, depth, width, lambda n, m: n)
        + [pl.BlockSpec((1, width), lambda n, m: (0, n)), table, table, table],
        pl.BlockSpec((tile, width), lambda n, m: (m, n)),
        sds((length, 3 * width), jnp.bfloat16),
    )(normed, *parts, bias, *tables)


def head_lanes(values, head):
    lanes = lax.broadcasted_iota(jnp.int32, values.shape, 1)
    return jnp.where((lanes >= head * E) & (lanes < (head + 1) * E), values, jnp.zeros_like(values))


def to_plain_rows(places_ref, source_ref, target_ref, count):
    rows = target_ref.shape[0] // count
    for b in range(count):
        start = pl.multiple_of(places_ref[1 + b] * rows, rows)
        target_ref[b * rows : (b + 1) * rows] = source_ref[pl.ds(start, rows)]


def masked(scores, keys_seg, query_seg, first):
    ks = lax.broadcasted_iota(jnp.int32, scores.shape, 0)
    qs = lax.broadcasted_iota(jnp.int32, scores.shape, 1) + first
    return (ks <= qs) & (keys_seg == query_seg)


def attend(places, qkv, seg_col, seg_row, count, heads):
    length = qkv.shape[0]
    pairs = heads // 2
    step = math.gcd(length, 256)
    rows = length // count

    def kernel(places_ref, q_ref, k_ref, v_ref, col_ref, row_ref, o_ref, log_ref, qs, ks, vt, os):
        to_plain_rows(places_ref, q_ref, qs, count)
        to_plain_rows(places_ref, k_ref, ks, count)
        to_plain_rows(places_ref, v_ref, os, count)
        vt[...] = jnp.transpose(os[...].astype(jnp.float32)).astype(jnp.bfloat16)
        for a in range(length // step):
            n = (a + 1) * step
            halves = []
            for h in range(2):
                query = head_lanes(qs[a * step : n], h)
                scores = lax.dot_general(
                    ks[0:n], query, (((1,), (1,)), ((), ())), preferred_element_type=jnp.float32
                )
                allowed = masked(scores, col_ref[0:n], row_ref[:, a * step : n], a * step)
                scores = jnp.where(allowed, scores * scale, masked_score)
                top = jnp.max(scores, axis=0, keepdims=True)
                weights = jnp.exp(scores - top)
                total = jnp.sum(weights, axis=0, keepdims=True)
                out = jnp.dot(
                    vt[h * E : (h + 1) * E, 0:n],
                    weights.astype(jnp.bfloat16),
                    preferred_element_type=jnp.float32,
                )
                halves.append(out / total)
                log_ref[0, h : h + 1, a * step : n] = top + jnp.log(total)
            os[a * step : n] = jnp.transpose(jnp.concatenate(halves, axis=0)).astype(jnp.bfloat16)
        for b in range(count):
            start = pl.multiple_of(places_ref[1 + b] * rows, rows)
            o_ref[pl.ds(start, rows)] = os[b * rows : (b + 1) * rows]

    def columns(group):
        return pl.BlockSpec((length, 128), lambda p: (0, group * pairs + p))

    scratch = pltpu.VMEM((length, 128), jnp.bfloat16)
    return call(
        kernel,
        (pairs,),
        [smem(), columns(0), columns(1), columns(2), whole(seg_col), whole(seg_row)],
        [columns(0), pl.BlockSpec((1, 2, length), lambda p: (p, 0, 0))],
        [
            sds((length, heads * E), jnp.bfloat16),
            sds((pairs, 2, length), jnp.float32),
        ],
        [scratch, scratch, pltpu.VMEM((128, length), jnp.bfloat16), scratch],
    )(places, qkv, qkv, qkv, seg_col, seg_row)


def attend_back(places, qkv, grad_attended, logs, seg_col, seg_row, tables, count, heads):
    length = qkv.shape[0]
    pairs = heads // 2
    step = math.gcd(length, 256)
    rows = length // count

    def kernel(
        places_ref,
        q_ref,
        k_ref,
        v_ref,
        g_ref,
        log_ref,
        col_ref,
        row_ref,
        cos_ref,
        low_ref,
        high_ref,
        dq_ref,
        dk_ref,
        dv_ref,
        sums_ref,
        qs,
        ks,
        vs,
        gs,
        kt,
        dq,
        dk,
        dv,
    ):
        to_plain_rows(places_ref, q_ref, qs, count)
        to_plain_rows(places_ref, k_ref, ks, count)
        to_plain_rows(places_ref, v_ref, vs, count)
        to_plain_rows(places_ref, g_ref, gs, count)
        kt[...] = jnp.transpose(ks[...].astype(jnp.float32)).astype(jnp.bfloat16)
        dk[...] = jnp.zeros_like(dk)
        dv[...] = jnp.zeros_like(dv)
        for a in range(length // step):
            n = (a + 1) * step
            halves = []
            for h in range(2):
                query = head_lanes(qs[a * step : n], h)
                grad = head_lanes(gs[a * step : n], h)
                scores = lax.dot_general(
                    ks[0:n], query, (((1,), (1,)), ((), ())), preferred_element_type=jnp.float32
                )
                allowed = masked(scores, col_ref[0:n], row_ref[:, a * step : n], a * step)
                log = log_ref[0, h : h + 1, a * step : n]
                weights = jnp.exp(jnp.where(allowed, scores * scale - log, masked_score))
                grad_weights = lax.dot_general(
                    vs[0:n], grad, (((1,), (1,)), ((), ())), preferred_element_type=jnp.float32
                )
                product = weights * grad_weights
                delta = jnp.sum(product, axis=0, keepdims=True)
                grad_scores = (product - weights * delta).astype(jnp.bfloat16)
                dv[0:n] += jnp.dot(
                    weights.astype(jnp.bfloat16), grad, preferred_element_type=jnp.float32
                )
                dk[0:n] += jnp.dot(grad_scores, query, preferred_element_type=jnp.float32)
                halves.append(
                    jnp.dot(
                        kt[h * E : (h + 1) * E, 0:n],
                        grad_scores,
                        preferred_element_type=jnp.float32,
                    )
                )
            dq[a * step : n] = jnp.transpose(jnp.concatenate(halves, axis=0))

        sums = [jnp.zeros((1, 128), jnp.float32)] * 3
        for b in range(count):
            start = pl.multiple_of(places_ref[1 + b] * rows, rows)
            cosine = cos_ref[pl.ds(start, rows)]
            low = low_ref[pl.ds(start, rows)]
            high = high_ref[pl.ds(start, rows)]
            for i, (part, out_ref) in enumerate(((dq, dq_ref), (dk, dk_ref), (dv, dv_ref))):
                block = part[b * rows : (b + 1) * rows]
                if i < 2:
                    block = block * scale
                    block = (
                        block * cosine
                        - pltpu.roll(block, 128 - ROT // 2, 1) * low
                        - pltpu.roll(block, ROT // 2, 1) * high
                    )
                block = block.astype(jnp.bfloat16)
                sums[i] = sums[i] + jnp.sum(block.astype(jnp.float32), axis=0, keepdims=True)
                out_ref[pl.ds(start, rows)] = block
        for i in range(3):
            sums_ref[i] = sums[i]

    def columns(group):
        return pl.BlockSpec((length, 128), lambda p: (0, group * pairs + p))

    low_scratch = pltpu.VMEM((length, 128), jnp.bfloat16)
    scratch = pltpu.VMEM((length, 128), jnp.float32)
    width = heads * E
    return call(
        kernel,
        (pairs,),
        [
            smem(),
            columns(0),
            columns(1),
            columns(2),
            columns(0),
            pl.BlockSpec((1, 2, length), lambda p: (p, 0, 0)),
            whole(seg_col),
            whole(seg_row),
            whole(tables[0]),
            whole(tables[1]),
            whole(tables[2]),
        ],
        [columns(0)] * 3 + [pl.BlockSpec((3, 1, 128), lambda p: (0, 0, p))],
        [sds((length, width), jnp.bfloat16)] * 3 + [sds((3, 1, width), jnp.float32)],
        [low_scratch] * 4
        + [pltpu.VMEM((128, length), jnp.bfloat16), scratch, scratch, scratch],
    )(places, qkv, qkv, qkv, grad_attended, logs, seg_col, seg_row, *tables)


def join_rows(places_ref, first, refs, joined):
    size = refs[0].shape[0]
    r = 0
    for ref in refs:
        if len(ref.shape) == 2:
            blocks = [ref[...]]
        else:
            blocks = [ref[i] for i in range(ref.shape[0])]
        for block in blocks:
            start = pl.multiple_of(places_ref[first + r] * size, size)
            joined[pl.ds(start, size)] = block
            r += 1


def halves_specs(tiles, tile, width):
    half = tiles // 2
    rows = pl.BlockSpec((tile, width), lambda m: (lax.rem(m + half, tiles), 0))
    far = pl.BlockSpec((tile, D), lambda m: (jnp.minimum(m, half - 1), 0))
    near = pl.BlockSpec((tile, D), lambda m: (jnp.maximum(m - half, 0), 0))
    return rows, near, far


def store_half(value, near_ref, far_ref, half):
    @pl.when(pl.program_id(0) < half)
    def _():
        far_ref[...] = value

    @pl.when(pl.program_id(0) >= half)
    def _():
        near_ref[...] = value


def out_product(places, left, parts, count):
    length, depth = left.shape
    tile = length // 4
    rows, near, far = halves_specs(4, tile, depth)

    def kernel(places_ref, x_ref, a_ref, b_ref, c_ref, d_ref, near_ref, far_ref, joined):
        @pl.when(pl.program_id(0) == 0)
        def _():
            join_rows(places_ref, 1 + count, (a_ref, b_ref, c_ref, d_ref), joined)

        total = jnp.dot(x_ref[...], joined[...], preferred_element_type=jnp.float32)
        store_half(total.astype(jnp.bfloat16), near_ref, far_ref, 2)

    shape = sds((length // 2, D), jnp.bfloat16)
    return call(
        kernel,
        (4,),
        [smem(), rows] + [whole(part) for part in parts],
        [near, far],
        [shape, shape],
        [pltpu.VMEM((depth, D), jnp.bfloat16)],
    )(places, left, *parts)


def grad_out(places, grad, parts, count):
    length = grad.shape[0]
    width = parts[0].shape[0] * 2 * (1 + parts[1].shape[0])
    tile = length // 4

    def kernel(places_ref, x_ref, a_ref, b_ref, c_ref, d_ref, o_ref, joined):
        @pl.when(pl.program_id(0) == 0)
        def _():
            join_rows(places_ref, 1 + count, (a_ref, b_ref, c_ref, d_ref), joined)

        o_ref[...] = lax.dot_general(
            x_ref[...], joined[...], (((1,), (1,)), ((), ())), preferred_element_type=jnp.float32
        ).astype(jnp.bfloat16)

    return call(
        kernel,
        (4,),
        [smem(), pl.BlockSpec((tile, D), lambda m: (m, 0))] + [whole(part) for part in parts],
        pl.BlockSpec((tile, width), lambda m: (m, 0)),
        sds((length, width), jnp.bfloat16),
        [pltpu.VMEM((width, D), jnp.bfloat16)],
    )(places, grad, *parts)


def gate_product(normed, parts, depth):
    length = normed.shape[0]
    width = parts[0].shape[1]
    units = width // 2
    tile = length // 4

    def kernel(x_ref, a_ref, b_ref, c_ref, d_ref, both_ref, activ_ref):
        both = times_rows(x_ref[...], (a_ref, b_ref, c_ref, d_ref), depth)
        gate = both[:, :units]
        both_ref[...] = both.astype(jnp.bfloat16)
        activ_ref[...] = (gate * jax.nn.sigmoid(gate) * both[:, units:]).astype(jnp.bfloat16)

    return call(
        kernel,
        (4,),
        [pl.BlockSpec((tile, D), lambda m: (m, 0))]
        + column_specs(parts, depth, width, lambda m: 0),
        [
            pl.BlockSpec((tile, width), lambda m: (m, 0)),
            pl.BlockSpec((tile, units), lambda m: (m, 0)),
        ],
        [sds((length, width), jnp.bfloat16), sds((length, units), jnp.bfloat16)],
        limit=60,
    )(normed, *parts)


def gate_back(places, cotangent, parts, both, count):
    length = cotangent.shape[0]
    width = both.shape[1]
    units = width // 2
    tile = length // 4

    def kernel(places_ref, x_ref, a_ref, b_ref, c_ref, d_ref, both_ref, o_ref, joined):
        @pl.when(pl.program_id(0) == 0)
        def _():
            join_rows(places_ref, 1 + count, (a_ref, b_ref, c_ref, d_ref), joined)

        grad = lax.dot_general(
            x_ref[...], joined[...], (((1,), (1,)), ((), ())), preferred_element_type=jnp.float32
        )
        gate = both_ref[:, :units].astype(jnp.float32)
        upward = both_ref[:, units:].astype(jnp.float32)
        sigma = jax.nn.sigmoid(gate)
        o_ref[:, :units] = (grad * upward * sigma * (1.0 + gate * (1.0 - sigma))).astype(
            jnp.bfloat16
        )
        o_ref[:, units:] = (grad * (gate * sigma)).astype(jnp.bfloat16)

    spec = pl.BlockSpec((tile, width), lambda m: (m, 0))
    return call(
        kernel,
        (4,),
        [smem(), pl.BlockSpec((tile, D), lambda m: (m, 0))]
        + [whole(part) for part in parts]
        + [spec],
        spec,
        sds((length, width), jnp.bfloat16),
        [pltpu.VMEM((units, D), jnp.bfloat16)],
        limit=60,
    )(places, cotangent, *parts, both)


def normed_grad(lefts, parts, depth):
    length = lefts[0].shape[0]
    width = sum(left.shape[1] for left in lefts)
    tile = length // 4
    rows, near, far = halves_specs(4, tile, width)

    def kernel(*refs):
        left_refs = refs[: len(lefts)]
        part_refs = refs[len(lefts) : len(lefts) + 4]
        near_ref, far_ref = refs[-2:]
        left = jnp.concatenate([ref[...] for ref in left_refs], axis=1)
        blocks = []
        for ref in part_refs:
            block = ref[...]
            block = block.reshape(-1, block.shape[-1])
            blocks.append(
                lax.dot_general(
                    left, block, (((1,), (1,)), ((), ())), preferred_element_type=jnp.float32
                ).astype(jnp.bfloat16)
            )
        store_half(jnp.concatenate(blocks, axis=1), near_ref, far_ref, 2)

    shape = sds((length // 2, D), jnp.bfloat16)
    return call(
        kernel,
        (4,),
        [pl.BlockSpec((tile, left.shape[1]), rows.index_map) for left in lefts]
        + column_specs(parts, depth, width, lambda m: 0),
        [near, far],
        [shape, shape],
        limit=60,
    )(*lefts, *parts)


def line_gather(block):
    count = lax.axis_size("dp")
    here = lax.axis_index("dp")
    ups, downs = [block], [block]
    for k in range(1, count):
        ups.append(lax.ppermute(ups[-1], "dp", [(i, i + 1) for i in range(k - 1, count - 1)]))
        downs.append(lax.ppermute(downs[-1], "dp", [(i, i - 1) for i in range(1, count - k + 1)]))
    rest = jnp.stack(
        [jnp.where(here + j < count, downs[j], ups[count - j]) for j in range(1, count)]
    )
    return rest, (ups[-1], downs[-1])


def line_scatter(block_at):
    count = lax.axis_size("dp")
    up = down = None
    for k in range(count - 1, 0, -1):
        up_load, down_load = block_at(k), block_at(-k)
        if up is not None:
            up_load = (up_load.astype(jnp.float32) + up.astype(jnp.float32)).astype(jnp.bfloat16)
            down_load = (down_load.astype(jnp.float32) + down.astype(jnp.float32)).astype(
                jnp.bfloat16
            )
        up = lax.ppermute(up_load, "dp", [(i, i + 1) for i in range(count - k)])
        down = lax.ppermute(down_load, "dp", [(i, i - 1) for i in range(k, count)])
    total = block_at(0).astype(jnp.float32) + up.astype(jnp.float32) + down.astype(jnp.float32)
    return total.astype(jnp.bfloat16)


def rows_gather(block):
    bit = lax.axis_size("ctx") // 2
    while bit >= 1:
        block = jnp.concatenate([block, swap(block, "ctx", bit)], axis=0)
        bit //= 2
    return block


def rows_scatter(near, far):
    count = lax.axis_size("ctx")
    pieces = [near, swap(far, "ctx", 1)]
    bit = 2
    while bit < count:
        half = pieces[0].shape[0] // 2
        load = sum(piece[half:].astype(jnp.float32) for piece in pieces).astype(jnp.bfloat16)
        pieces = [piece[:half] for piece in pieces] + [swap(load, "ctx", bit)]
        bit *= 2
    return pieces


def blocks_gather(block):
    near = block[None]
    bit = lax.axis_size("ctx") // 2
    while bit >= 2:
        near = jnp.concatenate([near, swap(near, "ctx", bit)], axis=0)
        bit //= 2
    return near, swap(near, "ctx", 1)


def fast_body(
    tokens,
    segment_ids,
    cotangent,
    ln1_gain,
    ln1_bias,
    w_qkv,
    b_qkv,
    w_out,
    ln2_gain,
    ln2_bias,
    w_gate_up,
    w_down,
):
    rows = tokens.shape[1]
    count = lax.axis_size("ctx")
    ctx = lax.axis_index("ctx")
    far_count = lax.axis_size("dp")
    here = lax.axis_index("dp")
    side = lax.axis_index("fsdp")
    shards = 2 * far_count
    depth = D // shards
    heads = H // count
    width = heads * E
    length = rows * count

    def reversed_bits(value):
        result = 0
        bit, top = 1, count // 2
        while bit < count:
            result = result + jnp.where((value & bit) != 0, top, 0)
            bit, top = bit * 2, top // 2
        return result

    row_places = [reversed_bits(b ^ ctx) for b in range(count)]
    shard_of = [
        ((here + j) % far_count) * 2 + (side ^ r) for r in range(2) for j in range(far_count)
    ]
    places = jnp.stack([ctx] + row_places + shard_of).astype(jnp.int32)

    small = jnp.concatenate([ln1_gain, ln1_bias, ln2_gain, ln2_bias, b_qkv])
    pad = 16
    qkv_mine = take_columns(places, w_qkv, count, shards, 3, pad)
    lead = jnp.zeros((pad, 3 * width), jnp.bfloat16)
    lead = lax.dynamic_update_slice(lead, small[None, : 3 * width], (0, 0))
    lead = lax.dynamic_update_slice(lead, small[None, 3 * width :], (1, 0))
    qkv_mine = lax.dynamic_update_slice(qkv_mine, lead, (depth, 0))
    out_mine = pick(w_out.reshape(count, -1, D), ctx, 0)
    gate_mine = take_columns(places, w_gate_up, count, shards, 2, 0)
    down_mine = pick(w_down.reshape(count, -1, D), ctx, 0)

    def weight(block, rest):
        return (block, rest, swap(block, "fsdp", 1), swap(rest, "fsdp", 1))

    token_rows = rows_gather(tokens[0])
    qkv_rest, last = line_gather(qkv_mine)
    qkv_parts = weight(qkv_mine, qkv_rest)
    out_rest, last = line_gather(tie(out_mine, *last))
    out_parts = weight(out_mine, out_rest)
    gate_rest, last = line_gather(tie(gate_mine, *last))
    gate_parts = weight(gate_mine, gate_rest)
    down_rest, last = line_gather(tie(down_mine, *last))
    down_parts = weight(down_mine, down_rest)
    segments = rows_gather(segment_ids)
    cot_rows = rows_gather(tie(cotangent[0], token_rows))

    segments = sum(
        jnp.where(place == jnp.arange(count)[:, None], segments, 0).sum(0)[None, :]
        * (jnp.arange(count)[:, None] == b)
        for b, place in enumerate(row_places)
    )
    seg_row = segments.reshape(1, length)
    seg_col = segments.reshape(length, 1)
    base = jnp.stack([reversed_bits(jnp.int32(p)) ^ ctx for p in range(count)]) * rows
    positions = (base[:, None] + jnp.arange(rows, dtype=jnp.int32)[None, :]).reshape(length)
    half = ROT // 2
    freqs = 10000.0 ** (-jnp.arange(half, dtype=jnp.float32) * 2.0 / ROT)
    angles = positions.astype(jnp.float32)[:, None] * freqs[None, :]
    cosine, sine = jnp.cos(angles), jnp.sin(angles)
    rest_zero = jnp.zeros((length, E - ROT), jnp.float32)
    zero = jnp.zeros((length, half), jnp.float32)
    tables = (
        jnp.concatenate([cosine, cosine, rest_zero + 1.0] * 2, axis=1),
        jnp.concatenate([-sine, zero, rest_zero] * 2, axis=1),
        jnp.concatenate([zero, sine, rest_zero] * 2, axis=1),
    )

    small_rows = [part.reshape(-1, depth + pad, 3 * width)[:, depth : depth + 2] for part in qkv_parts]
    small_all = jnp.concatenate(small_rows, axis=0).reshape(shards, -1)[:, : small.shape[0]]
    small_all = small_all.astype(jnp.float32)
    gain_one, bias_one, gain_two, bias_two = (
        small_all[:, i * depth : (i + 1) * depth] for i in range(4)
    )
    bias_rows = small_all[:, 4 * depth :]
    bias_plain = sum(
        (jnp.arange(shards)[:, None] == shard_of[r]) * bias_rows[r][None, :] for r in range(shards)
    )
    bias_mine = pick(bias_plain.reshape(3, shards, count, E), ctx, 2).reshape(1, 3 * width)

    normed_one = norm_tokens(places, token_rows, gain_one, bias_one, count)
    qkv = project(normed_one, qkv_parts, bias_mine, tables, depth)
    attended, logs = attend(places, qkv, seg_col, seg_row, count, heads)
    pieces = rows_scatter(*out_product(places, attended, out_parts, count))
    hidden, normed_two = norm_hidden(places, tokens[0], pieces, gain_two, bias_two, count)
    normed_two = rows_gather(normed_two)
    both, activ = gate_product(normed_two, gate_parts, depth)

    def row_grad(left, right):
        part = contract_rows(left, right).astype(jnp.bfloat16).reshape(far_count, 2, -1, D)
        arrived = swap(pick(part, 1 - side, 1), "fsdp", 1)
        total = (pick(part, side, 1).astype(jnp.float32) + arrived.astype(jnp.float32)).astype(
            jnp.bfloat16
        )

        def block_at(step):
            return pick(total, jnp.clip(here + step, 0, far_count - 1), 0)

        return line_scatter(block_at)

    def column_grad(normed, right):
        load = contract_rows(normed[:, D // 2 :], right).astype(jnp.bfloat16)
        arrived = swap(load, "fsdp", 1)
        total = contract_rows(normed[:, : D // 2], right) + arrived.astype(jnp.float32)
        total = total.astype(jnp.bfloat16).reshape(far_count, depth, -1)
        return line_scatter(lambda step: total[step % far_count])

    down_grad = row_grad(activ, cot_rows)
    grad_both = gate_back(places, cot_rows, down_parts, both, count)
    gate_grad = column_grad(normed_two, grad_both)
    pieces = rows_scatter(*normed_grad([grad_both], gate_parts, depth))
    grad_hidden, grad_branch, sums_two = norm_back(
        places, hidden, pieces, gain_two, cotangent[0], count, True
    )
    grad_branch = rows_gather(grad_branch)
    grad_attended = grad_out(places, grad_branch, out_parts, count)
    out_grad = row_grad(attended, grad_branch)
    grad_q, grad_k, grad_v, bias_sums = attend_back(
        places, qkv, grad_attended, logs, seg_col, seg_row, tables, count, heads
    )
    qkv_grad = column_grad(normed_one, jnp.concatenate([grad_q, grad_k, grad_v], axis=1))
    pieces = rows_scatter(*normed_grad([grad_q, grad_k, grad_v], qkv_parts, depth))
    input_grad, sums_one = norm_back(
        places, tokens[0], pieces, gain_one, grad_hidden, count, False
    )

    mixed_pieces = rows_scatter(*out_product(places, tie(activ, grad_branch), down_parts, count))
    mixed = hidden + sum(piece[:rows].astype(jnp.float32) for piece in mixed_pieces)

    down_out = spread_rows(places, *blocks_gather(down_grad), count)
    gate_out = spread_columns(places, *blocks_gather(gate_grad), count, shards, 2)
    out_out = spread_rows(places, *blocks_gather(out_grad), count)
    qkv_out = spread_columns(places, *blocks_gather(qkv_grad), count, shards, 3)

    bias_part = jnp.where(
        jnp.arange(count)[None, None, :, None] == ctx, bias_sums.reshape(3, shards, 1, E), 0.0
    ).reshape(shards, 3 * depth)
    small_part = jnp.concatenate(
        [part.reshape(shards, depth) for part in (*sums_one, *sums_two)] + [bias_part], axis=1
    ).reshape(far_count, 2, -1)
    load = pick(small_part, 1 - side, 1).astype(jnp.bfloat16)
    total = pick(small_part, side, 1) + swap(load, "fsdp", 1).astype(jnp.float32)
    mine = pick(total, here, 0)
    low_total = total.astype(jnp.bfloat16)
    for r in range(1, far_count):
        mine = mine + swap(pick(low_total, here ^ r, 0), "dp", r).astype(jnp.float32)
    bit = count // 2
    while bit >= 1:
        mine = mine + swap(mine, "ctx", bit)
        bit //= 2

    return (
        mixed.astype(jnp.bfloat16)[None],
        input_grad[None],
        mine[:depth],
        mine[depth : 2 * depth],
        qkv_out,
        mine[4 * depth :],
        out_out,
        mine[2 * depth : 3 * depth],
        mine[3 * depth : 4 * depth],
        gate_out,
        down_out,
    )


def fits(mesh):
    count, shards = mesh.shape["ctx"], mesh.shape["dp"] * mesh.shape["fsdp"]
    return (
        mesh.shape["fsdp"] == 2
        and count > 1
        and count & (count - 1) == 0
        and (H // shards) == count
        and (FF // shards) % (16 * count) == 0
        and (FF // count) % 128 == 0
        and (H // count) % 2 == 0
    )


def solution(mesh):
    shards = ("dp", "fsdp")
    row = P(shards, "ctx", None)
    vector = P(shards)
    matrix = P(shards, None)
    return jax.shard_map(
        fast_body if fits(mesh) else body,
        mesh=mesh,
        in_specs=(
            row,
            P(shards, "ctx"),
            row,
            vector,
            vector,
            matrix,
            vector,
            matrix,
            vector,
            vector,
            matrix,
            matrix,
        ),
        out_specs=(
            row,
            row,
            vector,
            vector,
            matrix,
            vector,
            matrix,
            vector,
            vector,
            matrix,
            matrix,
        ),
        check_vma=False,
    )
```

```python
import math

import jax
import jax.numpy as jnp
import numpy as np
from jax import lax
from jax.experimental import pallas as pl
from jax.experimental.pallas import tpu as pltpu
from jax.sharding import PartitionSpec as P

D = 2048
H = 32
E = 64
FF = 5632
ROT = 16

epsilon = 1e-05
masked_score = -1e30
scale = E ** (-0.5)


def swap(block, axis, bit):
    count = lax.axis_size(axis)
    return lax.ppermute(block, axis, [(i, i ^ bit) for i in range(count)])


def tie(value, *others):
    return lax.optimization_barrier((value, *others))[0]


def shard_index():
    return lax.axis_index("dp") * lax.axis_size("fsdp") + lax.axis_index("fsdp")


def gather_shards(block):
    near = [block] + [swap(block, "dp", r) for r in range(1, lax.axis_size("dp"))]
    blocks = []
    for part in near:
        blocks.append(part)
        for r in range(1, lax.axis_size("fsdp")):
            blocks.append(swap(part, "fsdp", r))
    return blocks


def scatter_shards(blocks):
    far = lax.axis_size("dp")
    wide = lax.axis_size("fsdp")
    parts = blocks.reshape((far, wide) + blocks.shape[1:])
    total = parts[:, 0]
    for r in range(1, wide):
        total = total + swap(parts[:, r].astype(jnp.bfloat16), "fsdp", r).astype(jnp.float32)
    mine = total[0]
    for r in range(1, far):
        mine = mine + swap(total[r].astype(jnp.bfloat16), "dp", r).astype(jnp.float32)
    return mine


def ctx_gather(block):
    count = lax.axis_size("ctx")
    found = {0: block}
    bit = count // 2
    while bit >= 1:
        for r in list(found):
            found[r | bit] = swap(found[r], "ctx", bit)
        bit //= 2
    return [found[r] for r in range(count)]


def ctx_scatter(rows):
    count = lax.axis_size("ctx")
    size = rows.shape[0] // count
    parts = {r: rows[r * size : (r + 1) * size] for r in range(count)}
    bit = 1
    while bit < count:
        parts = {
            r: parts[r]
            + swap(parts[r | bit].astype(jnp.bfloat16), "ctx", bit).astype(jnp.float32)
            for r in parts
            if not r & bit
        }
        bit *= 2
    return parts[0]


def reorder(array, index, axis):
    count = array.shape[axis]
    bit = 1
    while bit < count:
        shape = array.shape[:axis] + (count // (2 * bit), 2, bit) + array.shape[axis + 1 :]
        split = array.reshape(shape)
        first = lax.index_in_dim(split, 0, axis + 1, keepdims=True)
        second = lax.index_in_dim(split, 1, axis + 1, keepdims=True)
        flip = (index & bit) != 0
        split = jnp.concatenate(
            [jnp.where(flip, second, first), jnp.where(flip, first, second)], axis=axis + 1
        )
        array = split.reshape(array.shape)
        bit *= 2
    return array


def layer_stats(values):
    average = jnp.mean(values, axis=-1, keepdims=True)
    centred = values - average
    variance = jnp.mean(centred * centred, axis=-1, keepdims=True)
    inverse = lax.rsqrt(variance + epsilon)
    return (centred * inverse, inverse)


def layer_norm_back(grad_normed, normal, inverse, scale_gain):
    grad_scaled = grad_normed * scale_gain
    first_mean = jnp.mean(grad_scaled, axis=-1, keepdims=True)
    second_mean = jnp.mean(grad_scaled * normal, axis=-1, keepdims=True)
    return inverse * (grad_scaled - first_mean - normal * second_mean)


def rotary_tables(positions):
    half = ROT // 2
    freqs = 10000.0 ** (-jnp.arange(half, dtype=jnp.float32) * 2.0 / ROT)
    angles = positions.astype(jnp.float32)[:, None] * freqs[None, :]
    return (jnp.cos(angles)[:, None, :], jnp.sin(angles)[:, None, :])


def rotate(values, cosine, sine):
    half = ROT // 2
    first = values[..., :half]
    second = values[..., half:ROT]
    return jnp.concatenate(
        [first * cosine - second * sine, second * cosine + first * sine, values[..., ROT:]], axis=-1
    )


def mul(left, right):
    return jnp.dot(left, right, preferred_element_type=jnp.float32)


def contract_rows(left, right):
    return lax.dot_general(
        left, right, (((0,), (0,)), ((), ())), preferred_element_type=jnp.float32
    )


def contract_cols(left, right):
    return lax.dot_general(
        left, right, (((1,), (1,)), ((), ())), preferred_element_type=jnp.float32
    )


def pick(array, index, axis):
    return lax.dynamic_index_in_dim(array, index, axis, keepdims=False)


def body(
    tokens,
    segment_ids,
    cotangent,
    ln1_gain,
    ln1_bias,
    w_qkv,
    b_qkv,
    w_out,
    ln2_gain,
    ln2_bias,
    w_gate_up,
    w_down,
):
    rows = tokens.shape[1]
    count = lax.axis_size("ctx")
    ctx = lax.axis_index("ctx")
    shards = lax.axis_size("dp") * lax.axis_size("fsdp")
    shard = shard_index()
    length = rows * count
    depth = D // shards
    heads = H // count
    even = (H // shards) % count == 0

    if even:
        qkv_mine = pick(w_qkv.reshape(depth, 3, shards, count, -1), ctx, 3).reshape(depth, -1)
        out_mine = pick(w_out.reshape(count, -1, D), ctx, 0)
    else:
        qkv_mine = pick(w_qkv.reshape(depth, 3, count, -1), ctx, 2).reshape(depth, -1)
        out_mine = w_out
    gate_up_mine = pick(w_gate_up.reshape(depth, 2, shards, count, -1), ctx, 3).reshape(depth, -1)
    down_mine = pick(w_down.reshape(count, -1, D), ctx, 0)

    small = jnp.concatenate([ln1_gain, ln1_bias, ln2_gain, ln2_bias, b_qkv])
    small_all = reorder(jnp.stack(gather_shards(small)), shard, 0).astype(jnp.float32)
    gain_one = small_all[:, :depth].reshape(D)
    bias_one = small_all[:, depth : 2 * depth].reshape(D)
    gain_two = small_all[:, 2 * depth : 3 * depth].reshape(D)
    bias_two = small_all[:, 3 * depth : 4 * depth].reshape(D)
    qkv_bias = small_all[:, 4 * depth :].reshape(3 * D)
    if even:
        bias_mine = pick(qkv_bias.reshape(3, shards, count, -1), ctx, 2).reshape(-1)
    else:
        bias_mine = pick(qkv_bias.reshape(3, count, -1), ctx, 1).reshape(-1)

    token_rows = jnp.concatenate(ctx_gather(tokens[0]), axis=0)
    segments = jnp.concatenate(ctx_gather(segment_ids), axis=1)[0]
    positions = jnp.concatenate(
        [(ctx ^ r) * rows + jnp.arange(rows, dtype=jnp.int32) for r in range(count)]
    )
    cosine, sine = rotary_tables(positions)

    qkv_all = jnp.concatenate(gather_shards(qkv_mine), axis=0)
    out_all = jnp.stack(gather_shards(tie(out_mine, qkv_all)))
    out_all = reorder(out_all, shard, 0).reshape(-1, D)
    if not even:
        out_all = pick(out_all.reshape(count, -1, D), ctx, 0)
    gate_up_all = jnp.concatenate(gather_shards(tie(gate_up_mine, qkv_all)), axis=0)
    cot_rows = jnp.concatenate(ctx_gather(tie(cotangent[0], token_rows)), axis=0)
    down_all = jnp.stack(gather_shards(tie(down_mine, gate_up_all)))
    down_all = reorder(down_all, shard, 0).reshape(-1, D)

    def to_shard_order(array):
        n = array.shape[0]
        return reorder(array.reshape(n, shards, depth), shard, 1).reshape(n, D)

    normal_one, inverse_one = layer_stats(token_rows.astype(jnp.float32))
    normed_one = to_shard_order((normal_one * gain_one + bias_one).astype(jnp.bfloat16))
    projected = mul(normed_one, qkv_all) + bias_mine
    width = heads * E
    queries = rotate(projected[:, :width].reshape(length, heads, E), cosine, sine).astype(
        jnp.bfloat16
    )
    keys = rotate(projected[:, width : 2 * width].reshape(length, heads, E), cosine, sine).astype(
        jnp.bfloat16
    )
    values = projected[:, 2 * width :].reshape(length, heads, E).astype(jnp.bfloat16)
    allowed = (positions[None, :] <= positions[:, None]) & (segments[None, :] == segments[:, None])
    scores = jnp.einsum("qhe,khe->hqk", queries, keys, preferred_element_type=jnp.float32) * scale
    scores = jnp.where(allowed[None], scores, masked_score)
    top = jnp.max(scores, axis=-1, keepdims=True)
    weights = jnp.exp(scores - top)
    weights = weights / jnp.sum(weights, axis=-1, keepdims=True)
    low_weights = weights.astype(jnp.bfloat16)
    attended_f = jnp.einsum("hqk,khe->qhe", low_weights, values, preferred_element_type=jnp.float32)
    attended = attended_f.reshape(length, width).astype(jnp.bfloat16)

    hidden = tokens[0].astype(jnp.float32) + ctx_scatter(mul(attended, out_all))
    normal_two, inverse_two = layer_stats(hidden)
    normed_two = to_shard_order((normal_two * gain_two + bias_two).astype(jnp.bfloat16))
    normed_two = jnp.concatenate(ctx_gather(normed_two), axis=0)
    gate_up = mul(normed_two, gate_up_all)
    units = FF // count
    gate = gate_up[:, :units]
    upward = gate_up[:, units:]
    sigma = jax.nn.sigmoid(gate)
    swish = gate * sigma
    activ = (swish * upward).astype(jnp.bfloat16)
    mixed = hidden + ctx_scatter(mul(activ, down_all))

    grad_activ = contract_cols(cot_rows, down_all)
    grad_gate = grad_activ * upward * sigma * (1.0 + gate * (1.0 - sigma))
    grad_up = grad_activ * swish
    grad_gate_up = jnp.concatenate([grad_gate, grad_up], axis=1).astype(jnp.bfloat16)
    down_part = contract_rows(activ, cot_rows).reshape(shards, -1, D)
    down_grad = scatter_shards(reorder(down_part, shard, 0))
    gate_up_part = contract_rows(normed_two, grad_gate_up).reshape(shards, depth, 2 * units)
    gate_up_grad = scatter_shards(tie(gate_up_part, down_grad))

    grad_normed_two = ctx_scatter(contract_cols(grad_gate_up, gate_up_all))
    grad_normed_two = to_shard_order(grad_normed_two)
    gain_two_grad = jnp.sum(grad_normed_two * normal_two, axis=0)
    bias_two_grad = jnp.sum(grad_normed_two, axis=0)
    grad_hidden = cotangent[0].astype(jnp.float32) + layer_norm_back(
        grad_normed_two, normal_two, inverse_two, gain_two
    )
    grad_branch = jnp.concatenate(ctx_gather(grad_hidden.astype(jnp.bfloat16)), axis=0)

    grad_attended = contract_cols(grad_branch, out_all).astype(jnp.bfloat16)
    out_part = contract_rows(attended, grad_branch)
    grad_heads = grad_attended.reshape(length, heads, E)
    grad_weights = jnp.einsum("qhe,khe->hqk", grad_heads, values, preferred_element_type=jnp.float32)
    delta = jnp.sum(weights * grad_weights, axis=-1, keepdims=True)
    grad_scores = (weights * (grad_weights - delta)).astype(jnp.bfloat16)
    grad_queries = (
        jnp.einsum("hqk,khe->qhe", grad_scores, keys, preferred_element_type=jnp.float32) * scale
    )
    grad_keys = (
        jnp.einsum("hqk,qhe->khe", grad_scores, queries, preferred_element_type=jnp.float32) * scale
    )
    grad_values = jnp.einsum(
        "hqk,qhe->khe", low_weights, grad_heads, preferred_element_type=jnp.float32
    )
    grad_qkv = jnp.concatenate(
        [
            rotate(grad_queries, cosine, -sine).reshape(length, width),
            rotate(grad_keys, cosine, -sine).reshape(length, width),
            grad_values.reshape(length, width),
        ],
        axis=1,
    ).astype(jnp.bfloat16)
    qkv_bias_part = jnp.sum(grad_qkv.astype(jnp.float32), axis=0)
    qkv_part = contract_rows(normed_one, grad_qkv).reshape(shards, depth, 3 * width)

    grad_normed_one = to_shard_order(ctx_scatter(contract_cols(grad_qkv, qkv_all)))
    normal_mine = normal_one[:rows]
    gain_one_grad = jnp.sum(grad_normed_one * normal_mine, axis=0)
    bias_one_grad = jnp.sum(grad_normed_one, axis=0)
    input_grad = grad_hidden + layer_norm_back(
        grad_normed_one, normal_mine, inverse_one[:rows], gain_one
    )

    qkv_grad = scatter_shards(tie(qkv_part, gate_up_grad))

    def ctx_blocks(block):
        found = jnp.stack(ctx_gather(block.astype(jnp.bfloat16)))
        return reorder(found, ctx, 0).astype(jnp.float32)

    down_out = ctx_blocks(down_grad).reshape(-1, D)
    gate_up_out = ctx_blocks(gate_up_grad).reshape(count, depth, 2, shards, -1)
    gate_up_out = gate_up_out.transpose(1, 2, 3, 0, 4).reshape(depth, 2 * FF)
    if even:
        out_part = out_part.reshape(shards, -1, D)
        out_out = ctx_blocks(scatter_shards(reorder(out_part, shard, 0))).reshape(-1, D)
        qkv_out = ctx_blocks(qkv_grad).reshape(count, depth, 3, shards, -1)
        qkv_out = qkv_out.transpose(1, 2, 3, 0, 4).reshape(depth, 3 * D)
        qkv_bias_rows = ctx_blocks(qkv_bias_part).reshape(count, 3, shards, -1)
        qkv_bias_rows = qkv_bias_rows.transpose(1, 2, 0, 3).reshape(shards, -1)
    else:
        spread = jnp.zeros((count,) + out_part.shape, jnp.float32)
        spread = lax.dynamic_update_index_in_dim(spread, out_part, ctx, 0)
        out_part = spread.reshape(shards, depth, D)
        out_out = scatter_shards(reorder(out_part, shard, 0))
        out_out = lax.psum(out_out.astype(jnp.bfloat16), "ctx").astype(jnp.float32)
        qkv_out = ctx_blocks(qkv_grad).reshape(count, depth, 3, -1)
        qkv_out = qkv_out.transpose(1, 2, 0, 3).reshape(depth, 3 * D)
        qkv_bias_rows = ctx_blocks(qkv_bias_part).reshape(count, 3, -1)
        qkv_bias_rows = qkv_bias_rows.transpose(1, 0, 2).reshape(shards, -1)

    norm_parts = jnp.concatenate(
        [
            part.reshape(shards, depth)
            for part in (gain_one_grad, bias_one_grad, gain_two_grad, bias_two_grad)
        ],
        axis=1,
    )
    bit = 1
    while bit < count:
        norm_parts = norm_parts + swap(norm_parts, "ctx", bit)
        bit *= 2
    small_parts = jnp.concatenate([norm_parts, qkv_bias_rows], axis=1)
    small_grad = scatter_shards(reorder(small_parts, shard, 0))

    return (
        mixed.astype(jnp.bfloat16)[None],
        input_grad[None],
        small_grad[:depth],
        small_grad[depth : 2 * depth],
        qkv_out,
        small_grad[4 * depth :],
        out_out,
        small_grad[2 * depth : 3 * depth],
        small_grad[3 * depth : 4 * depth],
        gate_up_out,
        down_out,
    )


def call(kernel, grid, in_specs, out_specs, out_shape, scratch=(), limit=48, after=(), aliases=()):
    inputs = len(in_specs)

    def body_of(places_ref, *refs):
        kernel(places_ref, *refs[:inputs], *refs[inputs + len(after) :])

    run = pl.pallas_call(
        body_of,
        grid_spec=pltpu.PrefetchScalarGridSpec(
            num_scalar_prefetch=1,
            grid=grid,
            in_specs=in_specs + [anywhere()] * len(after),
            out_specs=out_specs,
            scratch_shapes=list(scratch),
        ),
        out_shape=out_shape,
        input_output_aliases=dict(aliases),
        compiler_params=pltpu.CompilerParams(vmem_limit_bytes=limit * 1024 * 1024),
        cost_estimate=pl.CostEstimate(flops=1, bytes_accessed=1, transcendentals=0),
    )
    return lambda *operands: run(*operands, *after)


def anywhere():
    return pl.BlockSpec(memory_space=pl.ANY)


def hold(places, value, *after):
    def kernel(places_ref, value_ref, o_ref):
        pass

    return call(
        kernel,
        (1,),
        [anywhere()],
        anywhere(),
        sds(value.shape, value.dtype),
        limit=1,
        after=after,
        aliases=((1, 0),),
    )(places, value)


def sds(shape, dtype):
    return jax.ShapeDtypeStruct(shape, dtype)


def whole(array):
    zeros = (0,) * array.ndim
    return pl.BlockSpec(array.shape, lambda *_: zeros)


def quarters(shape):
    if shape[0] % 64 == 0:
        return (shape[0] // 4, shape[1]), lambda m: (m, 0)
    return (shape[0], shape[1] // 4), lambda m: (0, m)


def add(places, terms, after=()):
    shape = terms[0][0].shape[len(terms[0][1]) :]
    steps = 4 if shape[0] % 64 == 0 else 1
    tile = shape[0] // steps

    def spec(at):
        return pl.BlockSpec((None,) * len(at) + (tile, shape[1]), lambda m, _: at + (m, 0))

    def kernel(places_ref, *refs):
        total = refs[0][...].astype(jnp.float32)
        for ref in refs[1:-1]:
            total = total + ref[...].astype(jnp.float32)
        refs[-1][...] = total.astype(jnp.bfloat16)

    return call(
        kernel,
        (steps,),
        [spec(at) for _, at in terms],
        spec(()),
        sds(shape, jnp.bfloat16),
        after=after,
    )(places, *[array for array, _ in terms])


def contract(left, right):
    return lax.dot_general(
        left, right, (((0,), (0,)), ((), ())), preferred_element_type=jnp.float32
    )


def take_columns(places, w, count, shards, groups, group, copies, pad, after=()):
    depth = w.shape[0]
    each = w.shape[1] // groups
    unit = each // (shards * count)
    tile = depth // 4

    def kernel(places_ref, w_ref, o_ref):
        for i in range(count):

            @pl.when(places_ref[0] == i)
            def _():
                block = jnp.concatenate(
                    [
                        w_ref[:, (s * count + i) * unit : (s * count + i + 1) * unit]
                        for s in range(shards)
                    ],
                    axis=1,
                )
                for copy in range(copies):
                    o_ref[copy] = block

    return call(
        kernel,
        (4,),
        [pl.BlockSpec((tile, each), lambda m, _: (m, group))],
        pl.BlockSpec((copies, tile, each // count), lambda m, _: (0, m, 0)),
        sds((copies, depth + pad, each // count), jnp.bfloat16),
        after=after,
    )(places, w)


def take_pairs(places, w, count, shards, after=()):
    depth = w.shape[0]
    each = w.shape[1] // 2
    unit = each // (shards * count)
    tile = depth // 4

    def kernel(places_ref, gate_ref, up_ref, o_ref):
        for i in range(count):

            @pl.when(places_ref[0] == i)
            def _():
                for part, ref in enumerate((gate_ref, up_ref)):
                    block = jnp.concatenate(
                        [
                            ref[:, (s * count + i) * unit : (s * count + i + 1) * unit]
                            for s in range(shards)
                        ],
                        axis=1,
                    )
                    for n in range(each // count // 128):
                        at = (2 * n + part) * 128
                        o_ref[:, at : at + 128] = block[:, n * 128 : (n + 1) * 128]

    return call(
        kernel,
        (4,),
        [
            pl.BlockSpec((tile, each), lambda m, _: (m, 0)),
            pl.BlockSpec((tile, each), lambda m, _: (m, 1)),
        ],
        pl.BlockSpec((tile, 2 * each // count), lambda m, _: (m, 0)),
        sds((depth, 2 * each // count), jnp.bfloat16),
        after=after,
    )(places, w, w)


def interleave(blocks, shards):
    unit = blocks[0].shape[1] // shards
    return [
        jnp.concatenate([block[:, s * unit : (s + 1) * unit] for block in blocks], axis=1)
        for s in range(shards)
    ]


def spread_pairs(places, gathered, count, shards, after=()):
    depth = gathered.shape[0] // count
    width = gathered.shape[1]
    each = width // 2
    unit = each // shards * count
    tile = depth // 8

    def kernel(places_ref, x_ref, o_ref):
        for part in range(2):
            blocks = []
            for i in range(count):
                tiles = [
                    x_ref[i][:, (2 * n + part) * 128 : (2 * n + part + 1) * 128]
                    for n in range(each // 128)
                ]
                blocks.append(jnp.concatenate(tiles, axis=1).astype(jnp.float32))
            for s, block in enumerate(interleave(blocks, shards)):
                at = part * each * count + s * unit
                o_ref[:, at : at + unit] = block

    return call(
        kernel,
        (8,),
        [pl.BlockSpec((count, tile, width), lambda m, _: (0, m, 0))],
        pl.BlockSpec((tile, width * count), lambda m, _: (m, 0)),
        sds((depth, width * count), jnp.float32),
        after=after,
    )(places, gathered.reshape(count, depth, width))


def spread_columns(places, pieces, count, shards, after=()):
    groups = len(pieces)
    depth, each = pieces[0][0].shape
    unit = each // shards * count
    tile = depth // 4
    flat = [piece for group in pieces for piece in group]

    def kernel(places_ref, *refs):
        o_ref = refs[-1]
        for g in range(groups):
            values = [refs[g * count + p][...].astype(jnp.float32) for p in range(count)]
            blocks = []
            for i in range(count):
                block = values[0]
                for p in range(1, count):
                    block = jnp.where(places_ref[1 + i] == p, values[p], block)
                blocks.append(block)
            for s, block in enumerate(interleave(blocks, shards)):
                at = g * each * count + s * unit
                o_ref[:, at : at + unit] = block

    spec = pl.BlockSpec((tile, each), lambda m, _: (m, 0))
    return call(
        kernel,
        (4,),
        [spec] * len(flat),
        pl.BlockSpec((tile, groups * each * count), lambda m, _: (m, 0)),
        sds((depth, groups * each * count), jnp.float32),
        after=after,
    )(places, *flat)


def norm_stats(values):
    average = jnp.mean(values, axis=-1, keepdims=True)
    centred = values - average
    inverse = lax.rsqrt(jnp.mean(centred * centred, axis=-1, keepdims=True) + epsilon)
    return centred * inverse, inverse


def norm_tokens(places, tokens, gain, bias, count, after=()):
    length = tokens.shape[0]
    tile = length // count // 2
    shards, depth = gain.shape

    def kernel(places_ref, x_ref, gain_ref, bias_ref, o_ref, plain_ref):
        plain_ref[...], _ = norm_stats(x_ref[...].astype(jnp.float32))
        for r in range(shards):
            start = pl.multiple_of(places_ref[1 + count + r] * depth, depth)
            block = plain_ref[:, pl.ds(start, depth)]
            o_ref[:, r * depth : (r + 1) * depth] = (
                block * gain_ref[r : r + 1] + bias_ref[r : r + 1]
            ).astype(jnp.bfloat16)

    return call(
        kernel,
        (count, 2),
        [
            pl.BlockSpec((tile, D), lambda b, h, p: (p[1 + b] * 2 + h, 0)),
            whole(gain),
            whole(bias),
        ],
        pl.BlockSpec((tile, D), lambda b, h, _: (b * 2 + h, 0)),
        sds((length, D), jnp.bfloat16),
        [pltpu.VMEM((tile, D), jnp.float32)],
        after=after,
    )(places, tokens, gain, bias)


def norm_hidden(places, tokens, pieces, gain, bias, after=()):
    rows = tokens.shape[0]
    tile = rows // 4

    def kernel(places_ref, x_ref, *refs):
        gain_ref, bias_ref, hidden_ref, o_ref = refs[-4:]
        hidden = x_ref[...].astype(jnp.float32)
        for ref in refs[:-4]:
            hidden = hidden + ref[...].astype(jnp.float32)
        hidden_ref[...] = hidden
        normal, _ = norm_stats(hidden)
        o_ref[...] = (normal * gain_ref[...] + bias_ref[...]).astype(jnp.bfloat16)

    spec = pl.BlockSpec((tile, D), lambda m, _: (m, 0))
    return call(
        kernel,
        (4,),
        [spec] * (1 + len(pieces)) + [whole(gain), whole(bias)],
        [spec, spec],
        [sds((rows, D), jnp.float32), sds((rows, D), jnp.bfloat16)],
        after=after,
    )(places, tokens, *pieces, gain, bias)


def norm_back(places, source, pieces, gain, added, first, low, after=()):
    rows = source.shape[0]
    tile = rows // 4
    shards, depth = gain.shape

    def kernel(places_ref, x_ref, added_ref, gain_ref, *refs):
        piece_refs = refs[: len(pieces)]
        out_refs = refs[len(pieces) : -2]
        sums_ref = out_refs[-1]
        grad_ref, gain_plain = refs[-2:]
        for r in range(shards):
            start = pl.multiple_of(places_ref[first + r] * depth, depth) if shards > 1 else 0
            at = slice(r * depth, (r + 1) * depth)
            block = piece_refs[0][:, at].astype(jnp.float32)
            for ref in piece_refs[1:]:
                block = block + ref[:, at].astype(jnp.float32)
            grad_ref[:, pl.ds(start, depth)] = block
            gain_plain[:, pl.ds(start, depth)] = jnp.broadcast_to(gain_ref[r : r + 1], (8, depth))
        normal, inverse = norm_stats(x_ref[...].astype(jnp.float32))
        grad = grad_ref[...]

        @pl.when(pl.program_id(0) == 0)
        def _():
            sums_ref[...] = jnp.zeros_like(sums_ref)

        sums_ref[0:1] += jnp.sum(grad * normal, axis=0, keepdims=True)
        sums_ref[1:2] += jnp.sum(grad, axis=0, keepdims=True)
        scaled = grad * gain_plain[0:1]
        mean = jnp.mean(scaled, axis=-1, keepdims=True)
        second = jnp.mean(scaled * normal, axis=-1, keepdims=True)
        total = added_ref[...].astype(jnp.float32) + inverse * (scaled - mean - normal * second)
        out_refs[0][...] = total
        if low:
            out_refs[1][...] = total.astype(jnp.bfloat16)

    spec = pl.BlockSpec((tile, D), lambda m, _: (m, 0))
    sums = pl.BlockSpec((2, D), lambda m, _: (0, 0))
    return call(
        kernel,
        (4,),
        [spec, spec, whole(gain)] + [spec] * len(pieces),
        [spec] + [spec] * low + [sums],
        [sds((rows, D), jnp.float32)]
        + [sds((rows, D), jnp.bfloat16)] * low
        + [sds((2, D), jnp.float32)],
        [pltpu.VMEM((tile, D), jnp.float32), pltpu.VMEM((8, D), jnp.float32)],
        after=after,
    )(places, source, added, gain, *pieces)


def project(places, normed, near, far, bias, tables, after=()):
    length = normed.shape[0]
    width = bias.shape[1]
    tile = min(width, 256)
    blocks = near.shape[0]
    depth = D // blocks // 2

    def kernel(places_ref, x_ref, near_ref, far_ref, bias_ref, *refs):
        o_ref = refs[-1]
        total = bias_ref[...]
        for i, ref in enumerate((near_ref, far_ref)):
            weight = ref[...].reshape(D // 2, tile)
            left = x_ref[:, i * (D // 2) : (i + 1) * (D // 2)]
            total = total + jnp.dot(left, weight, preferred_element_type=jnp.float32)
        if tables:
            cosine, low, high = (
                jnp.concatenate([ref[...]] * (tile // 128), axis=1) for ref in refs[:3]
            )
            total = (
                total * cosine
                + pltpu.roll(total, tile - ROT // 2, 1) * low
                + pltpu.roll(total, ROT // 2, 1) * high
            )
        o_ref[...] = total.astype(jnp.bfloat16)

    weight = pl.BlockSpec((blocks, depth, tile), lambda n, _: (0, 0, n))
    return call(
        kernel,
        (width // tile,),
        [whole(normed), weight, weight, pl.BlockSpec((1, tile), lambda n, _: (0, n))]
        + [whole(table) for table in tables],
        pl.BlockSpec((length, tile), lambda n, _: (0, n)),
        sds((length, width), jnp.bfloat16),
        after=after,
    )(places, normed, near, far, bias, *tables)


def head_lanes(values, head):
    lanes = lax.broadcasted_iota(jnp.int32, values.shape, 1)
    return jnp.where((lanes >= head * E) & (lanes < (head + 1) * E), values, jnp.zeros_like(values))


def to_plain_rows(places_ref, source_ref, target_ref, count):
    rows = target_ref.shape[0] // count
    for b in range(count):
        start = pl.multiple_of(places_ref[1 + b] * rows, rows)
        target_ref[b * rows : (b + 1) * rows] = source_ref[pl.ds(start, rows)]


def masked(scores, keys_seg, query_seg, first):
    ks = lax.broadcasted_iota(jnp.int32, scores.shape, 0)
    qs = lax.broadcasted_iota(jnp.int32, scores.shape, 1) + first
    return (ks <= qs) & (keys_seg == query_seg)


def attend(places, qkv, seg_col, seg_row, count, heads, after=()):
    length = qkv[0].shape[0]
    pairs = heads // 2
    step = math.gcd(length, 256)
    rows = length // count

    def kernel(places_ref, q_ref, k_ref, v_ref, col_ref, row_ref, o_ref, log_ref, vt, os):
        vt[...] = jnp.transpose(v_ref[...].astype(jnp.float32)).astype(jnp.bfloat16)
        for a in range(length // step):
            n = (a + 1) * step
            halves = []
            for h in range(2):
                query = head_lanes(q_ref[a * step : n], h)
                scores = lax.dot_general(
                    k_ref[0:n], query, (((1,), (1,)), ((), ())), preferred_element_type=jnp.float32
                )
                allowed = masked(scores, col_ref[0:n], row_ref[:, a * step : n], a * step)
                scores = jnp.where(allowed, scores * scale, masked_score)
                top = jnp.max(scores, axis=0, keepdims=True)
                weights = jnp.exp(scores - top)
                total = jnp.sum(weights, axis=0, keepdims=True)
                out = jnp.dot(
                    vt[h * E : (h + 1) * E, 0:n],
                    weights.astype(jnp.bfloat16),
                    preferred_element_type=jnp.float32,
                )
                halves.append(out / total)
                log_ref[0, h : h + 1, a * step : n] = top + jnp.log(total)
            os[a * step : n] = jnp.transpose(jnp.concatenate(halves, axis=0)).astype(jnp.bfloat16)
        for b in range(count):
            start = pl.multiple_of(places_ref[1 + b] * rows, rows)
            o_ref[pl.ds(start, rows)] = os[b * rows : (b + 1) * rows]

    def columns(group):
        return pl.BlockSpec((length, 128), lambda p, _: (0, group * pairs + p))

    scratch = pltpu.VMEM((length, 128), jnp.bfloat16)
    return call(
        kernel,
        (pairs,),
        [columns(0), columns(0), columns(0), whole(seg_col), whole(seg_row)],
        [columns(0), pl.BlockSpec((1, 2, length), lambda p, _: (p, 0, 0))],
        [
            sds((length, heads * E), jnp.bfloat16),
            sds((pairs, 2, length), jnp.float32),
        ],
        [pltpu.VMEM((128, length), jnp.bfloat16), scratch],
        after=after,
    )(places, *qkv, seg_col, seg_row)


def attend_back(
    places, qkv, grad_attended, logs, seg_col, seg_row, tables, count, heads, after=()
):
    length = qkv[0].shape[0]
    pairs = heads // 2
    step = math.gcd(length, 256)
    rows = length // count

    def kernel(
        places_ref,
        q_ref,
        k_ref,
        v_ref,
        g_ref,
        log_ref,
        col_ref,
        row_ref,
        cos_ref,
        low_ref,
        high_ref,
        dq_ref,
        dk_ref,
        dv_ref,
        sums_ref,
        gs,
        kt,
        dq,
        dk,
        dv,
    ):
        to_plain_rows(places_ref, g_ref, gs, count)
        kt[...] = jnp.transpose(k_ref[...].astype(jnp.float32)).astype(jnp.bfloat16)
        dk[...] = jnp.zeros_like(dk)
        dv[...] = jnp.zeros_like(dv)
        for a in range(length // step):
            n = (a + 1) * step
            halves = []
            for h in range(2):
                query = head_lanes(q_ref[a * step : n], h)
                grad = head_lanes(gs[a * step : n], h)
                scores = lax.dot_general(
                    k_ref[0:n], query, (((1,), (1,)), ((), ())), preferred_element_type=jnp.float32
                )
                allowed = masked(scores, col_ref[0:n], row_ref[:, a * step : n], a * step)
                log = log_ref[0, h : h + 1, a * step : n]
                weights = jnp.exp(jnp.where(allowed, scores * scale - log, masked_score))
                grad_weights = lax.dot_general(
                    v_ref[0:n], grad, (((1,), (1,)), ((), ())), preferred_element_type=jnp.float32
                )
                product = weights * grad_weights
                delta = jnp.sum(product, axis=0, keepdims=True)
                grad_scores = (product - weights * delta).astype(jnp.bfloat16)
                dv[0:n] += jnp.dot(
                    weights.astype(jnp.bfloat16), grad, preferred_element_type=jnp.float32
                )
                dk[0:n] += jnp.dot(grad_scores, query, preferred_element_type=jnp.float32)
                halves.append(
                    jnp.dot(
                        kt[h * E : (h + 1) * E, 0:n],
                        grad_scores,
                        preferred_element_type=jnp.float32,
                    )
                )
            dq[a * step : n] = jnp.transpose(jnp.concatenate(halves, axis=0))

        sums = [jnp.zeros((1, 128), jnp.float32)] * 3
        for b in range(count):
            at = slice(b * rows, (b + 1) * rows)
            cosine, low, high = cos_ref[at], low_ref[at], high_ref[at]
            for i, (part, out_ref) in enumerate(((dq, dq_ref), (dk, dk_ref), (dv, dv_ref))):
                block = part[at]
                if i < 2:
                    block = block * scale
                    block = (
                        block * cosine
                        - pltpu.roll(block, 128 - ROT // 2, 1) * low
                        - pltpu.roll(block, ROT // 2, 1) * high
                    )
                block = block.astype(jnp.bfloat16)
                sums[i] = sums[i] + jnp.sum(block.astype(jnp.float32), axis=0, keepdims=True)
                out_ref[at] = block
        for i in range(3):
            sums_ref[i] = sums[i]

    def columns(group):
        return pl.BlockSpec((length, 128), lambda p, _: (0, group * pairs + p))

    low_scratch = pltpu.VMEM((length, 128), jnp.bfloat16)
    scratch = pltpu.VMEM((length, 128), jnp.float32)
    width = heads * E
    return call(
        kernel,
        (pairs,),
        [
            columns(0),
            columns(0),
            columns(0),
            columns(0),
            pl.BlockSpec((1, 2, length), lambda p, _: (p, 0, 0)),
            whole(seg_col),
            whole(seg_row),
            whole(tables[0]),
            whole(tables[1]),
            whole(tables[2]),
        ],
        [columns(0)] * 3 + [pl.BlockSpec((3, 1, 128), lambda p, _: (0, 0, p))],
        [sds((length, width), jnp.bfloat16)] * 3 + [sds((3, 1, width), jnp.float32)],
        [low_scratch]
        + [pltpu.VMEM((128, length), jnp.bfloat16), scratch, scratch, scratch],
        after=after,
    )(places, *qkv, grad_attended, logs, seg_col, seg_row, *tables)


def join_rows(places_ref, first, refs, joined):
    r = 0
    for ref in refs:
        blocks, size, _ = ref.shape
        for i in range(blocks):
            start = pl.multiple_of(places_ref[first + r] * size, size)
            joined[pl.ds(start, size)] = ref[i]
            r += 1


def row_product(places, left, near, far, count, after=()):
    length, depth = left.shape
    tile = D // 4

    def kernel(places_ref, x_ref, a_ref, b_ref, near_ref, far_ref, joined):
        @pl.when(pl.program_id(0) == 0)
        def _():
            join_rows(places_ref, 1 + count, (a_ref, b_ref), joined)

        start = pl.multiple_of(pl.program_id(0) * tile, tile)
        total = jnp.dot(
            x_ref[...], joined[:, pl.ds(start, tile)], preferred_element_type=jnp.float32
        ).astype(jnp.bfloat16)
        near_ref[...] = total[: length // 2]
        far_ref[...] = total[length // 2 :]

    spec = pl.BlockSpec((length // 2, tile), lambda n, _: (0, n))
    shape = sds((length // 2, D), jnp.bfloat16)
    return call(
        kernel,
        (4,),
        [whole(left), whole(near), whole(far)],
        [spec, spec],
        [shape, shape],
        [pltpu.VMEM((depth, D), jnp.bfloat16)],
        after=after,
    )(places, left, near, far)


def grad_out(places, pieces, near, far, count, after=()):
    rows = pieces[0].shape[0]
    width = near.shape[0] * near.shape[1] * 2
    tile = rows

    def kernel(places_ref, *refs):
        piece_refs = refs[:count]
        a_ref, b_ref, o_ref, all_ref, joined = refs[count:]

        @pl.when(pl.program_id(0) == 0)
        def _():
            join_rows(places_ref, 1 + count, (a_ref, b_ref), joined)

        for p, ref in enumerate(piece_refs):

            @pl.when(pl.program_id(0) == p)
            def _():
                all_ref[...] = ref[...]
                o_ref[...] = lax.dot_general(
                    ref[...],
                    joined[...],
                    (((1,), (1,)), ((), ())),
                    preferred_element_type=jnp.float32,
                ).astype(jnp.bfloat16)

    return call(
        kernel,
        (count,),
        [whole(piece) for piece in pieces] + [whole(near), whole(far)],
        [
            pl.BlockSpec((tile, width), lambda m, _: (m, 0)),
            pl.BlockSpec((tile, D), lambda m, _: (m, 0)),
        ],
        [sds((rows * count, width), jnp.bfloat16), sds((rows * count, D), jnp.bfloat16)],
        [pltpu.VMEM((width, D), jnp.bfloat16)],
        after=after,
    )(places, *pieces, near, far)


def gate_product(places, pieces, weight, after=()):
    rows = pieces[0].shape[0]
    length = rows * len(pieces)
    width = weight.shape[1]

    def kernel(places_ref, *refs):
        *piece_refs, w_ref, all_ref, both_ref, activ_ref = refs

        @pl.when(pl.program_id(0) == 0)
        def _():
            for p, ref in enumerate(piece_refs):
                all_ref[p * rows : (p + 1) * rows] = ref[...]

        both = jnp.dot(all_ref[...], w_ref[...], preferred_element_type=jnp.float32)
        gate = both[:, :128]
        both_ref[...] = both.astype(jnp.bfloat16)
        activ_ref[...] = (gate * jax.nn.sigmoid(gate) * both[:, 128:]).astype(jnp.bfloat16)

    return call(
        kernel,
        (width // 256,),
        [whole(piece) for piece in pieces] + [pl.BlockSpec((D, 256), lambda n, _: (0, n))],
        [
            pl.BlockSpec((length, D), lambda n, _: (0, 0)),
            pl.BlockSpec((length, 256), lambda n, _: (0, n)),
            pl.BlockSpec((length, 128), lambda n, _: (0, n)),
        ],
        [
            sds((length, D), jnp.bfloat16),
            sds((length, width), jnp.bfloat16),
            sds((length, width // 2), jnp.bfloat16),
        ],
        limit=56,
        after=after,
    )(places, *pieces, weight)


def gate_back(places, cotangent, near, far, both, count, after=()):
    length, width = both.shape
    units = width // 2
    steps = -(-units // 256)

    def kernel(places_ref, x_ref, a_ref, b_ref, both_ref, o_ref, joined):
        @pl.when(pl.program_id(0) == 0)
        def _():
            join_rows(places_ref, 1 + count, (a_ref, b_ref), joined)

        start = pl.multiple_of(pl.program_id(0) * 256, 256)
        grad = lax.dot_general(
            x_ref[...],
            joined[pl.ds(start, 256)],
            (((1,), (1,)), ((), ())),
            preferred_element_type=jnp.float32,
        )
        for i in range(2):
            part = grad[:, i * 128 : (i + 1) * 128]
            gate = both_ref[:, i * 256 : i * 256 + 128].astype(jnp.float32)
            upward = both_ref[:, i * 256 + 128 : (i + 1) * 256].astype(jnp.float32)
            sigma = jax.nn.sigmoid(gate)
            grad_gate = part * upward * sigma * (1.0 + gate * (1.0 - sigma))
            o_ref[:, i * 256 : i * 256 + 128] = grad_gate.astype(jnp.bfloat16)
            o_ref[:, i * 256 + 128 : (i + 1) * 256] = (part * (gate * sigma)).astype(jnp.bfloat16)

    spec = pl.BlockSpec((length, 512), lambda n, _: (0, n))
    return call(
        kernel,
        (steps,),
        [whole(cotangent), whole(near), whole(far), spec],
        spec,
        sds((length, width), jnp.bfloat16),
        [pltpu.VMEM((steps * 256, D), jnp.bfloat16)],
        limit=56,
        after=after,
    )(places, cotangent, near, far, both)


def normed_grad(places, left, weight, after=()):
    length, width = left.shape

    def kernel(places_ref, x_ref, w_ref, near_ref, far_ref):
        total = lax.dot_general(
            x_ref[...], w_ref[...], (((1,), (1,)), ((), ())), preferred_element_type=jnp.float32
        ).astype(jnp.bfloat16)
        near_ref[...] = total[: length // 2]
        far_ref[...] = total[length // 2 :]

    spec = pl.BlockSpec((length // 2, 256), lambda n, _: (0, n))
    shape = sds((length // 2, D), jnp.bfloat16)
    return call(
        kernel,
        (D // 256,),
        [whole(left), pl.BlockSpec((256, width), lambda n, _: (n, 0))],
        [spec, spec],
        [shape, shape],
        limit=56,
        after=after,
    )(places, left, weight)


def normed_grad_parts(places, lefts, parts, count, after=()):
    length, width = lefts[0].shape
    rows = length // count
    blocks, depth = parts[0][0].shape[0], D // parts[0][0].shape[0] // 2
    total_width = width * len(lefts)

    def kernel(places_ref, *refs):
        left_refs = refs[: len(lefts)]
        near_refs = refs[len(lefts) : 2 * len(lefts)]
        far_refs = refs[2 * len(lefts) : 3 * len(lefts)]
        near_ref, far_ref, joined = refs[3 * len(lefts) :]

        @pl.when(pl.program_id(0) == 0)
        def _():
            for b in range(count):
                start = pl.multiple_of(places_ref[1 + b] * rows, rows)
                for i, ref in enumerate(left_refs):
                    joined[pl.ds(start, rows), i * width : (i + 1) * width] = ref[
                        b * rows : (b + 1) * rows
                    ]

        def run(weight_refs):
            weight = jnp.concatenate([ref[0] for ref in weight_refs], axis=1)
            total = lax.dot_general(
                joined[...], weight, (((1,), (1,)), ((), ())), preferred_element_type=jnp.float32
            ).astype(jnp.bfloat16)
            near_ref[...] = total[: length // 2]
            far_ref[...] = total[length // 2 :]

        @pl.when(pl.program_id(0) < blocks)
        def _():
            run(near_refs)

        @pl.when(pl.program_id(0) >= blocks)
        def _():
            run(far_refs)

    near_spec = pl.BlockSpec((1, depth, width), lambda n, _: (jnp.minimum(n, blocks - 1), 0, 0))
    far_spec = pl.BlockSpec((1, depth, width), lambda n, _: (jnp.maximum(n - blocks, 0), 0, 0))
    spec = pl.BlockSpec((length // 2, depth), lambda n, _: (0, n))
    shape = sds((length // 2, D), jnp.bfloat16)
    return call(
        kernel,
        (2 * blocks,),
        [whole(left) for left in lefts] + [near_spec] * len(lefts) + [far_spec] * len(lefts),
        [spec, spec],
        [shape, shape],
        [pltpu.VMEM((length, total_width), jnp.bfloat16)],
        after=after,
    )(places, *lefts, *[near for near, _ in parts], *[far for _, far in parts])


def turn(source_ref, first, columns, target_ref):
    step = math.gcd(columns, 256)
    for at in range(0, columns, step):
        block = source_ref[:, first + at : first + at + step].astype(jnp.float32)
        target_ref[at : at + step] = jnp.transpose(block).astype(jnp.bfloat16)


def pairs_grad(places, normed, right, after=()):
    length, width = right.shape

    def kernel(places_ref, x_ref, g_ref, o_ref, turned):
        @pl.when(pl.program_id(0) == 0)
        def _():
            turn(x_ref, 0, D, turned)

        o_ref[...] = jnp.dot(
            turned[...], g_ref[...], preferred_element_type=jnp.float32
        ).astype(jnp.bfloat16)

    return call(
        kernel,
        (width // 256,),
        [whole(normed), pl.BlockSpec((length, 256), lambda n, _: (0, n))],
        pl.BlockSpec((D, 256), lambda n, _: (0, n)),
        sds((D, width), jnp.bfloat16),
        [pltpu.VMEM((D, length), jnp.bfloat16)],
        after=after,
    )(places, normed, right)


def column_loads(places, normed, rights, after=()):
    length, width = rights[0].shape
    count = len(rights)
    rows = D // 2

    def kernel(places_ref, x_ref, *refs):
        right_refs, out_refs = refs[:count], refs[count : 2 * count]
        turned_ref, turned = refs[2 * count :]
        step = pl.program_id(0)

        @pl.when(step == 0)
        def _():
            turn(x_ref, rows, rows, turned)

        for i in range(count):

            @pl.when(step == i)
            def _():
                out_refs[i][...] = jnp.dot(
                    turned[...], right_refs[i][...], preferred_element_type=jnp.float32
                ).astype(jnp.bfloat16)

        @pl.when(step == count - 1)
        def _():
            turn(x_ref, 0, rows, turned_ref)

    shape = sds((rows, width), jnp.bfloat16)
    own = sds((rows, length), jnp.bfloat16)
    return call(
        kernel,
        (count,),
        [whole(normed)] + [whole(right) for right in rights],
        [whole(shape)] * count + [whole(own)],
        [shape] * count + [own],
        [pltpu.VMEM((rows, length), jnp.bfloat16)],
        after=after,
    )(places, normed, *rights)


def column_keep(places, turned, right, arrived, after=()):
    rows, length = turned.shape
    width = right.shape[1]
    tile = width // 2

    def kernel(places_ref, x_ref, g_ref, arrived_ref, o_ref):
        total = jnp.dot(x_ref[...], g_ref[...], preferred_element_type=jnp.float32)
        o_ref[...] = (total + arrived_ref[...].astype(jnp.float32)).astype(jnp.bfloat16)

    spec = pl.BlockSpec((rows, tile), lambda n, _: (0, n))
    return call(
        kernel,
        (2,),
        [whole(turned), pl.BlockSpec((length, tile), lambda n, _: (0, n)), spec],
        spec,
        sds((rows, width), jnp.bfloat16),
        after=after,
    )(places, turned, right, arrived)


def row_grad(places, left, right, size, count, stacked, after=()):
    length, width = left.shape
    tile = D // 4
    blocks = width // size // 2

    def kernel(places_ref, x_ref, g_ref, *refs):
        total_ref = refs[-1]
        total_ref[...] = contract(x_ref[...], g_ref[...])
        for side in range(2):
            for r in range(blocks):
                place = places_ref[1 + count + side * blocks + r]
                start = pl.multiple_of(place * size, size)
                refs[side][r] = total_ref[pl.ds(start, size)].astype(jnp.bfloat16)

    block = (blocks, size, tile)
    if stacked:
        spec = pl.BlockSpec(block, lambda n, _: (0, n, 0))
        shape = sds((blocks, 4 * size, tile), jnp.bfloat16)
    else:
        spec = pl.BlockSpec(block, lambda n, _: (0, 0, n))
        shape = sds((blocks, size, D), jnp.bfloat16)
    return call(
        kernel,
        (4,),
        [whole(left), pl.BlockSpec((length, tile), lambda n, _: (0, n))],
        [spec, spec],
        [shape, shape],
        [pltpu.VMEM((width, tile), jnp.float32)],
        after=after,
    )(places, left, right)


def to_line(blocks):
    return lax.all_to_all(blocks, "dp", split_axis=0, concat_axis=0)


def rows_gather(own):
    pieces = [own]
    bit = lax.axis_size("ctx") // 2
    while bit >= 1:
        pieces = pieces + [swap(piece, "ctx", bit) for piece in pieces]
        bit //= 2
    return pieces


def rows_scatter(places, near, far, after=()):
    count = lax.axis_size("ctx")
    pieces = [near, swap(far, "ctx", 1)]
    bit = 2
    while bit < count:
        pieces = [piece.reshape(2, -1, D) for piece in pieces]
        load = add(places, [(piece, (1,)) for piece in pieces], after if 2 * bit == count else ())
        pieces = [piece[0] for piece in pieces] if 2 * bit < count else [
            piece.reshape(-1, D) for piece in pieces
        ]
        pieces.append(swap(load, "ctx", bit))
        bit *= 2
    return pieces


def fast_body(
    tokens,
    segment_ids,
    cotangent,
    ln1_gain,
    ln1_bias,
    w_qkv,
    b_qkv,
    w_out,
    ln2_gain,
    ln2_bias,
    w_gate_up,
    w_down,
):
    rows = tokens.shape[1]
    count = lax.axis_size("ctx")
    ctx = lax.axis_index("ctx")
    line = lax.axis_size("dp")
    here = lax.axis_index("dp")
    side = lax.axis_index("fsdp")
    shards = 2 * line
    depth = D // shards
    heads = H // count
    width = heads * E
    length = rows * count

    def reversed_bits(value):
        return sum(
            jnp.where((value >> i) & 1, count >> (i + 1), 0) for i in range(count.bit_length() - 1)
        )

    row_places = [reversed_bits(b ^ ctx) for b in range(count)]
    shard_of = [(r % line) * 2 + (side ^ (r // line)) for r in range(shards)]
    places = jnp.stack([jnp.asarray(i, jnp.int32) for i in [ctx] + row_places + shard_of])

    small = jnp.concatenate([ln1_gain, ln1_bias, ln2_gain, ln2_bias, b_qkv])
    pad = 16
    q_mine = take_columns(places, w_qkv, count, shards, 3, 0, line, pad)
    lines = -(-small.shape[0] // width)
    lead = jnp.pad(small, (0, pad * width - small.shape[0])).reshape(1, pad, width)
    q_mine = lax.dynamic_update_slice(
        q_mine, jnp.broadcast_to(lead, (line, pad, width)), (0, depth, 0)
    )

    def weight(blocks):
        near = to_line(blocks)
        return near, swap(near, "fsdp", 1)

    def row_copies(w, *after):
        block = hold(places, pick(w.reshape(count, -1, D), ctx, 0), *after)
        return jnp.broadcast_to(block[None], (line,) + block.shape)

    token_rows = jnp.concatenate(rows_gather(tokens[0]), axis=0)
    cot_rows = jnp.concatenate(
        rows_gather(hold(places, cotangent[0], token_rows)), axis=0
    )
    q_parts = weight(q_mine)
    k_mine = take_columns(
        places, w_qkv, count, shards, 3, 1, line, 0, q_parts[:1]
    )
    k_parts = weight(k_mine)
    gate_mine = take_pairs(places, w_gate_up, count, shards, (k_parts[0], token_rows))
    gate_up = lax.all_gather(gate_mine, ("dp", "fsdp"), axis=0, tiled=True)
    v_mine = take_columns(
        places, w_qkv, count, shards, 3, 2, line, 0, (k_parts[0], q_parts[1], token_rows)
    )
    v_parts = weight(v_mine)
    qkv_parts = [q_parts, k_parts, v_parts]
    out_parts = weight(row_copies(w_out, v_parts[0], k_parts[1], cot_rows))
    seg_row = lax.all_gather(segment_ids, "ctx", axis=1, tiled=True)
    seg_col = seg_row.reshape(length, 1)

    half = ROT // 2
    angles = np.arange(length)[:, None] * 10000.0 ** (-np.arange(half) * 2.0 / ROT)[None, :]
    cosine, sine = np.cos(angles), np.sin(angles)
    flat = np.zeros((length, E - ROT))
    zero = np.zeros((length, half))
    tables = [
        jnp.asarray(np.concatenate(parts * 2, axis=1), jnp.float32)
        for parts in ([cosine, cosine, flat + 1.0], [-sine, zero, flat], [zero, sine, flat])
    ]

    small_rows = [part[:, depth : depth + lines] for part in qkv_parts[0]]
    small_all = jnp.concatenate(small_rows, axis=0).reshape(shards, -1)[:, : small.shape[0]]
    small_all = small_all.astype(jnp.float32)
    small_plain = sum(
        (jnp.arange(shards)[:, None] == shard_of[r]) * small_all[r][None, :] for r in range(shards)
    )
    gain_one, bias_one = small_all[:, :depth], small_all[:, depth : 2 * depth]
    gain_two = small_plain[:, 2 * depth : 3 * depth].reshape(1, D)
    bias_two = small_plain[:, 3 * depth : 4 * depth].reshape(1, D)
    bias_plain = small_plain[:, 4 * depth :]
    bias_mine = pick(bias_plain.reshape(3, shards, count, E), ctx, 2).reshape(3, 1, width)

    normed_one = norm_tokens(places, token_rows, gain_one, bias_one, count, (seg_row,))
    qkv = []
    for i, parts in enumerate(qkv_parts):
        turns = tables if i < 2 else []
        qkv.append(project(places, normed_one, *parts, bias_mine[i], turns, qkv[-1:]))
    down_near = to_line(row_copies(w_down, out_parts[0], qkv[2]))
    attended, logs = attend(places, qkv, seg_col, seg_row, count, heads)
    pieces = rows_scatter(places, *row_product(places, attended, *out_parts, count))
    hidden, normed_two = norm_hidden(places, tokens[0], pieces, gain_two, bias_two)
    down_near = hold(places, down_near, hidden)
    down_parts = (down_near, swap(down_near, "fsdp", 1))
    normed_two, both, activ = gate_product(places, rows_gather(normed_two), gate_up)

    def line_sum(blocks, after=()):
        arrived = to_line(blocks).reshape(line, -1, blocks.shape[-1])
        return add(places, [(arrived, (i,)) for i in range(line)], after)

    def both_sides(kept, arrived):
        return (kept.astype(jnp.float32) + arrived.astype(jnp.float32)).astype(jnp.bfloat16)

    down_keep, down_load = row_grad(
        places, activ, cot_rows, down_parts[0].shape[1], count, False
    )
    down_arrived = swap(down_load, "fsdp", 1)
    grad_both = gate_back(places, cot_rows, *down_parts, both, count, (down_load,))
    gate_part = pairs_grad(places, normed_two, grad_both)
    gate_grad = lax.psum_scatter(gate_part, ("dp", "fsdp"), scatter_dimension=0, tiled=True)
    pieces = rows_scatter(places, *normed_grad(places, grad_both, gate_up, (gate_part,)))
    down_total = both_sides(down_keep, hold(places, down_arrived, pieces[1]))
    down_pieces = row_product(places, activ, *down_parts, count, (down_total,))
    grad_hidden, grad_branch, sums_two = norm_back(
        places, hidden, pieces, gain_two, cotangent[0], 0, True, (down_pieces[0],)
    )
    down_pieces = rows_scatter(places, *down_pieces, (grad_branch,))
    grad_attended, grad_branch = grad_out(places, rows_gather(grad_branch), *out_parts, count)
    out_keep, out_load = row_grad(places, attended, grad_branch, out_parts[0].shape[1], count, True)
    out_arrived = swap(out_load, "fsdp", 1)
    grads = attend_back(
        places, qkv, grad_attended, logs, seg_col, seg_row, tables, count, heads, (out_load,)
    )
    grads, bias_sums = grads[:3], grads[3]
    *loads, turned = column_loads(places, normed_one, grads)
    arrivals = [swap(load, "fsdp", 1) for load in loads]
    mixed = hidden + sum(piece[:rows].astype(jnp.float32) for piece in down_pieces)
    mixed = mixed.astype(jnp.bfloat16)
    down_grad = line_sum(down_total, (loads[2],))

    def ctx_rows(block):
        return lax.all_gather(block, "ctx", axis=0, tiled=True)

    def keep(i, *after):
        total = column_keep(places, turned, grads[i], arrivals[i], after)
        return total.reshape(line, depth, width)

    out_total = both_sides(out_keep, out_arrived)
    totals = [jnp.concatenate([keep(0, down_grad), out_total], axis=1)]
    near, far = normed_grad_parts(places, grads, qkv_parts, count, (totals[0],))
    gate_out = spread_pairs(places, ctx_rows(gate_grad), count, shards)
    down_out = ctx_rows(down_grad).astype(jnp.float32)
    totals.append(keep(1, gate_out))
    pieces = rows_scatter(places, near, far, (totals[1],))
    q_sum = line_sum(totals[0], (mixed,))
    totals.append(keep(2, down_out))
    input_grad, sums_one = norm_back(
        places, tokens[0], pieces, gain_one, grad_hidden, 1 + count, False, (totals[2],)
    )
    out_out = ctx_rows(q_sum[depth:]).reshape(count, 4, -1, D // 4)
    out_out = out_out.transpose(0, 2, 1, 3).reshape(-1, D).astype(jnp.float32)
    sums = [q_sum[:depth], line_sum(totals[1]), line_sum(totals[2], (out_out,))]
    qkv_grads = [rows_gather(total) for total in sums]
    qkv_out = spread_columns(places, qkv_grads, count, shards)

    bias_part = jnp.where(
        jnp.arange(count)[None, None, :, None] == ctx, bias_sums.reshape(3, shards, 1, E), 0.0
    ).reshape(shards, 3 * depth)
    small_part = jnp.concatenate(
        [part.reshape(shards, depth) for part in (*sums_one, *sums_two)] + [bias_part], axis=1
    ).reshape(line, 2, -1)
    load = pick(small_part, 1 - side, 1).astype(jnp.bfloat16)
    total = pick(small_part, side, 1) + swap(load, "fsdp", 1).astype(jnp.float32)
    low_total = total.astype(jnp.bfloat16)
    mine = pick(total, here, 0)
    for r in range(1, line):
        mine = mine + swap(pick(low_total, here ^ r, 0), "dp", r).astype(jnp.float32)
    bit = count // 2
    while bit >= 1:
        mine = mine + swap(mine, "ctx", bit)
        bit //= 2

    return (
        mixed[None],
        input_grad[None],
        mine[:depth],
        mine[depth : 2 * depth],
        qkv_out,
        mine[4 * depth :],
        out_out,
        mine[2 * depth : 3 * depth],
        mine[3 * depth : 4 * depth],
        gate_out,
        down_out,
    )


def fits(mesh):
    count, shards = mesh.shape["ctx"], mesh.shape["dp"] * mesh.shape["fsdp"]
    return (
        mesh.shape["fsdp"] == 2
        and count > 1
        and count & (count - 1) == 0
        and (H // shards) == count
        and (FF // shards) % (16 * count) == 0
        and (FF // count) % 128 == 0
        and (H // count) % 2 == 0
    )


def solution(mesh):
    shards = ("dp", "fsdp")
    row = P(shards, "ctx", None)
    vector = P(shards)
    matrix = P(shards, None)
    return jax.shard_map(
        fast_body if fits(mesh) else body,
        mesh=mesh,
        in_specs=(
            row,
            P(shards, "ctx"),
            row,
            vector,
            vector,
            matrix,
            vector,
            matrix,
            vector,
            vector,
            matrix,
            matrix,
        ),
        out_specs=(
            row,
            row,
            vector,
            vector,
            matrix,
            vector,
            matrix,
            vector,
            vector,
            matrix,
            matrix,
        ),
        check_vma=False,
    )
```

```python
import math

import jax
import jax.numpy as jnp
import numpy as np
from jax import lax
from jax.experimental import pallas as pl
from jax.experimental.pallas import tpu as pltpu
from jax.sharding import PartitionSpec as P

D = 2048
H = 32
E = 64
FF = 5632
ROT = 16

epsilon = 1e-05
masked_score = -1e30
scale = E ** (-0.5)


def swap(block, axis, bit):
    count = lax.axis_size(axis)
    return lax.ppermute(block, axis, [(i, i ^ bit) for i in range(count)])


def tie(value, *others):
    return lax.optimization_barrier((value, *others))[0]


def shard_index():
    return lax.axis_index("dp") * lax.axis_size("fsdp") + lax.axis_index("fsdp")


def gather_shards(block):
    near = [block] + [swap(block, "dp", r) for r in range(1, lax.axis_size("dp"))]
    blocks = []
    for part in near:
        blocks.append(part)
        for r in range(1, lax.axis_size("fsdp")):
            blocks.append(swap(part, "fsdp", r))
    return blocks


def scatter_shards(blocks):
    far = lax.axis_size("dp")
    wide = lax.axis_size("fsdp")
    parts = blocks.reshape((far, wide) + blocks.shape[1:])
    total = parts[:, 0]
    for r in range(1, wide):
        total = total + swap(parts[:, r].astype(jnp.bfloat16), "fsdp", r).astype(jnp.float32)
    mine = total[0]
    for r in range(1, far):
        mine = mine + swap(total[r].astype(jnp.bfloat16), "dp", r).astype(jnp.float32)
    return mine


def ctx_gather(block):
    count = lax.axis_size("ctx")
    found = {0: block}
    bit = count // 2
    while bit >= 1:
        for r in list(found):
            found[r | bit] = swap(found[r], "ctx", bit)
        bit //= 2
    return [found[r] for r in range(count)]


def ctx_scatter(rows):
    count = lax.axis_size("ctx")
    size = rows.shape[0] // count
    parts = {r: rows[r * size : (r + 1) * size] for r in range(count)}
    bit = 1
    while bit < count:
        parts = {
            r: parts[r]
            + swap(parts[r | bit].astype(jnp.bfloat16), "ctx", bit).astype(jnp.float32)
            for r in parts
            if not r & bit
        }
        bit *= 2
    return parts[0]


def reorder(array, index, axis):
    count = array.shape[axis]
    bit = 1
    while bit < count:
        shape = array.shape[:axis] + (count // (2 * bit), 2, bit) + array.shape[axis + 1 :]
        split = array.reshape(shape)
        first = lax.index_in_dim(split, 0, axis + 1, keepdims=True)
        second = lax.index_in_dim(split, 1, axis + 1, keepdims=True)
        flip = (index & bit) != 0
        split = jnp.concatenate(
            [jnp.where(flip, second, first), jnp.where(flip, first, second)], axis=axis + 1
        )
        array = split.reshape(array.shape)
        bit *= 2
    return array


def layer_stats(values):
    average = jnp.mean(values, axis=-1, keepdims=True)
    centred = values - average
    variance = jnp.mean(centred * centred, axis=-1, keepdims=True)
    inverse = lax.rsqrt(variance + epsilon)
    return (centred * inverse, inverse)


def layer_norm_back(grad_normed, normal, inverse, scale_gain):
    grad_scaled = grad_normed * scale_gain
    first_mean = jnp.mean(grad_scaled, axis=-1, keepdims=True)
    second_mean = jnp.mean(grad_scaled * normal, axis=-1, keepdims=True)
    return inverse * (grad_scaled - first_mean - normal * second_mean)


def rotary_tables(positions):
    half = ROT // 2
    freqs = 10000.0 ** (-jnp.arange(half, dtype=jnp.float32) * 2.0 / ROT)
    angles = positions.astype(jnp.float32)[:, None] * freqs[None, :]
    return (jnp.cos(angles)[:, None, :], jnp.sin(angles)[:, None, :])


def rotate(values, cosine, sine):
    half = ROT // 2
    first = values[..., :half]
    second = values[..., half:ROT]
    return jnp.concatenate(
        [first * cosine - second * sine, second * cosine + first * sine, values[..., ROT:]], axis=-1
    )


def mul(left, right):
    return jnp.dot(left, right, preferred_element_type=jnp.float32)


def contract_rows(left, right):
    return lax.dot_general(
        left, right, (((0,), (0,)), ((), ())), preferred_element_type=jnp.float32
    )


def contract_cols(left, right):
    return lax.dot_general(
        left, right, (((1,), (1,)), ((), ())), preferred_element_type=jnp.float32
    )


def pick(array, index, axis):
    return lax.dynamic_index_in_dim(array, index, axis, keepdims=False)


def body(
    tokens,
    segment_ids,
    cotangent,
    ln1_gain,
    ln1_bias,
    w_qkv,
    b_qkv,
    w_out,
    ln2_gain,
    ln2_bias,
    w_gate_up,
    w_down,
):
    rows = tokens.shape[1]
    count = lax.axis_size("ctx")
    ctx = lax.axis_index("ctx")
    shards = lax.axis_size("dp") * lax.axis_size("fsdp")
    shard = shard_index()
    length = rows * count
    depth = D // shards
    heads = H // count
    even = (H // shards) % count == 0

    if even:
        qkv_mine = pick(w_qkv.reshape(depth, 3, shards, count, -1), ctx, 3).reshape(depth, -1)
        out_mine = pick(w_out.reshape(count, -1, D), ctx, 0)
    else:
        qkv_mine = pick(w_qkv.reshape(depth, 3, count, -1), ctx, 2).reshape(depth, -1)
        out_mine = w_out
    gate_up_mine = pick(w_gate_up.reshape(depth, 2, shards, count, -1), ctx, 3).reshape(depth, -1)
    down_mine = pick(w_down.reshape(count, -1, D), ctx, 0)

    small = jnp.concatenate([ln1_gain, ln1_bias, ln2_gain, ln2_bias, b_qkv])
    small_all = reorder(jnp.stack(gather_shards(small)), shard, 0).astype(jnp.float32)
    gain_one = small_all[:, :depth].reshape(D)
    bias_one = small_all[:, depth : 2 * depth].reshape(D)
    gain_two = small_all[:, 2 * depth : 3 * depth].reshape(D)
    bias_two = small_all[:, 3 * depth : 4 * depth].reshape(D)
    qkv_bias = small_all[:, 4 * depth :].reshape(3 * D)
    if even:
        bias_mine = pick(qkv_bias.reshape(3, shards, count, -1), ctx, 2).reshape(-1)
    else:
        bias_mine = pick(qkv_bias.reshape(3, count, -1), ctx, 1).reshape(-1)

    token_rows = jnp.concatenate(ctx_gather(tokens[0]), axis=0)
    segments = jnp.concatenate(ctx_gather(segment_ids), axis=1)[0]
    positions = jnp.concatenate(
        [(ctx ^ r) * rows + jnp.arange(rows, dtype=jnp.int32) for r in range(count)]
    )
    cosine, sine = rotary_tables(positions)

    qkv_all = jnp.concatenate(gather_shards(qkv_mine), axis=0)
    out_all = jnp.stack(gather_shards(tie(out_mine, qkv_all)))
    out_all = reorder(out_all, shard, 0).reshape(-1, D)
    if not even:
        out_all = pick(out_all.reshape(count, -1, D), ctx, 0)
    gate_up_all = jnp.concatenate(gather_shards(tie(gate_up_mine, qkv_all)), axis=0)
    cot_rows = jnp.concatenate(ctx_gather(tie(cotangent[0], token_rows)), axis=0)
    down_all = jnp.stack(gather_shards(tie(down_mine, gate_up_all)))
    down_all = reorder(down_all, shard, 0).reshape(-1, D)

    def to_shard_order(array):
        n = array.shape[0]
        return reorder(array.reshape(n, shards, depth), shard, 1).reshape(n, D)

    normal_one, inverse_one = layer_stats(token_rows.astype(jnp.float32))
    normed_one = to_shard_order((normal_one * gain_one + bias_one).astype(jnp.bfloat16))
    projected = mul(normed_one, qkv_all) + bias_mine
    width = heads * E
    queries = rotate(projected[:, :width].reshape(length, heads, E), cosine, sine).astype(
        jnp.bfloat16
    )
    keys = rotate(projected[:, width : 2 * width].reshape(length, heads, E), cosine, sine).astype(
        jnp.bfloat16
    )
    values = projected[:, 2 * width :].reshape(length, heads, E).astype(jnp.bfloat16)
    allowed = (positions[None, :] <= positions[:, None]) & (segments[None, :] == segments[:, None])
    scores = jnp.einsum("qhe,khe->hqk", queries, keys, preferred_element_type=jnp.float32) * scale
    scores = jnp.where(allowed[None], scores, masked_score)
    top = jnp.max(scores, axis=-1, keepdims=True)
    weights = jnp.exp(scores - top)
    weights = weights / jnp.sum(weights, axis=-1, keepdims=True)
    low_weights = weights.astype(jnp.bfloat16)
    attended_f = jnp.einsum("hqk,khe->qhe", low_weights, values, preferred_element_type=jnp.float32)
    attended = attended_f.reshape(length, width).astype(jnp.bfloat16)

    hidden = tokens[0].astype(jnp.float32) + ctx_scatter(mul(attended, out_all))
    normal_two, inverse_two = layer_stats(hidden)
    normed_two = to_shard_order((normal_two * gain_two + bias_two).astype(jnp.bfloat16))
    normed_two = jnp.concatenate(ctx_gather(normed_two), axis=0)
    gate_up = mul(normed_two, gate_up_all)
    units = FF // count
    gate = gate_up[:, :units]
    upward = gate_up[:, units:]
    sigma = jax.nn.sigmoid(gate)
    swish = gate * sigma
    activ = (swish * upward).astype(jnp.bfloat16)
    mixed = hidden + ctx_scatter(mul(activ, down_all))

    grad_activ = contract_cols(cot_rows, down_all)
    grad_gate = grad_activ * upward * sigma * (1.0 + gate * (1.0 - sigma))
    grad_up = grad_activ * swish
    grad_gate_up = jnp.concatenate([grad_gate, grad_up], axis=1).astype(jnp.bfloat16)
    down_part = contract_rows(activ, cot_rows).reshape(shards, -1, D)
    down_grad = scatter_shards(reorder(down_part, shard, 0))
    gate_up_part = contract_rows(normed_two, grad_gate_up).reshape(shards, depth, 2 * units)
    gate_up_grad = scatter_shards(tie(gate_up_part, down_grad))

    grad_normed_two = ctx_scatter(contract_cols(grad_gate_up, gate_up_all))
    grad_normed_two = to_shard_order(grad_normed_two)
    gain_two_grad = jnp.sum(grad_normed_two * normal_two, axis=0)
    bias_two_grad = jnp.sum(grad_normed_two, axis=0)
    grad_hidden = cotangent[0].astype(jnp.float32) + layer_norm_back(
        grad_normed_two, normal_two, inverse_two, gain_two
    )
    grad_branch = jnp.concatenate(ctx_gather(grad_hidden.astype(jnp.bfloat16)), axis=0)

    grad_attended = contract_cols(grad_branch, out_all).astype(jnp.bfloat16)
    out_part = contract_rows(attended, grad_branch)
    grad_heads = grad_attended.reshape(length, heads, E)
    grad_weights = jnp.einsum("qhe,khe->hqk", grad_heads, values, preferred_element_type=jnp.float32)
    delta = jnp.sum(weights * grad_weights, axis=-1, keepdims=True)
    grad_scores = (weights * (grad_weights - delta)).astype(jnp.bfloat16)
    grad_queries = (
        jnp.einsum("hqk,khe->qhe", grad_scores, keys, preferred_element_type=jnp.float32) * scale
    )
    grad_keys = (
        jnp.einsum("hqk,qhe->khe", grad_scores, queries, preferred_element_type=jnp.float32) * scale
    )
    grad_values = jnp.einsum(
        "hqk,qhe->khe", low_weights, grad_heads, preferred_element_type=jnp.float32
    )
    grad_qkv = jnp.concatenate(
        [
            rotate(grad_queries, cosine, -sine).reshape(length, width),
            rotate(grad_keys, cosine, -sine).reshape(length, width),
            grad_values.reshape(length, width),
        ],
        axis=1,
    ).astype(jnp.bfloat16)
    qkv_bias_part = jnp.sum(grad_qkv.astype(jnp.float32), axis=0)
    qkv_part = contract_rows(normed_one, grad_qkv).reshape(shards, depth, 3 * width)

    grad_normed_one = to_shard_order(ctx_scatter(contract_cols(grad_qkv, qkv_all)))
    normal_mine = normal_one[:rows]
    gain_one_grad = jnp.sum(grad_normed_one * normal_mine, axis=0)
    bias_one_grad = jnp.sum(grad_normed_one, axis=0)
    input_grad = grad_hidden + layer_norm_back(
        grad_normed_one, normal_mine, inverse_one[:rows], gain_one
    )

    qkv_grad = scatter_shards(tie(qkv_part, gate_up_grad))

    def ctx_blocks(block):
        found = jnp.stack(ctx_gather(block.astype(jnp.bfloat16)))
        return reorder(found, ctx, 0).astype(jnp.float32)

    down_out = ctx_blocks(down_grad).reshape(-1, D)
    gate_up_out = ctx_blocks(gate_up_grad).reshape(count, depth, 2, shards, -1)
    gate_up_out = gate_up_out.transpose(1, 2, 3, 0, 4).reshape(depth, 2 * FF)
    if even:
        out_part = out_part.reshape(shards, -1, D)
        out_out = ctx_blocks(scatter_shards(reorder(out_part, shard, 0))).reshape(-1, D)
        qkv_out = ctx_blocks(qkv_grad).reshape(count, depth, 3, shards, -1)
        qkv_out = qkv_out.transpose(1, 2, 3, 0, 4).reshape(depth, 3 * D)
        qkv_bias_rows = ctx_blocks(qkv_bias_part).reshape(count, 3, shards, -1)
        qkv_bias_rows = qkv_bias_rows.transpose(1, 2, 0, 3).reshape(shards, -1)
    else:
        spread = jnp.zeros((count,) + out_part.shape, jnp.float32)
        spread = lax.dynamic_update_index_in_dim(spread, out_part, ctx, 0)
        out_part = spread.reshape(shards, depth, D)
        out_out = scatter_shards(reorder(out_part, shard, 0))
        out_out = lax.psum(out_out.astype(jnp.bfloat16), "ctx").astype(jnp.float32)
        qkv_out = ctx_blocks(qkv_grad).reshape(count, depth, 3, -1)
        qkv_out = qkv_out.transpose(1, 2, 0, 3).reshape(depth, 3 * D)
        qkv_bias_rows = ctx_blocks(qkv_bias_part).reshape(count, 3, -1)
        qkv_bias_rows = qkv_bias_rows.transpose(1, 0, 2).reshape(shards, -1)

    norm_parts = jnp.concatenate(
        [
            part.reshape(shards, depth)
            for part in (gain_one_grad, bias_one_grad, gain_two_grad, bias_two_grad)
        ],
        axis=1,
    )
    bit = 1
    while bit < count:
        norm_parts = norm_parts + swap(norm_parts, "ctx", bit)
        bit *= 2
    small_parts = jnp.concatenate([norm_parts, qkv_bias_rows], axis=1)
    small_grad = scatter_shards(reorder(small_parts, shard, 0))

    return (
        mixed.astype(jnp.bfloat16)[None],
        input_grad[None],
        small_grad[:depth],
        small_grad[depth : 2 * depth],
        qkv_out,
        small_grad[4 * depth :],
        out_out,
        small_grad[2 * depth : 3 * depth],
        small_grad[3 * depth : 4 * depth],
        gate_up_out,
        down_out,
    )


def call(kernel, grid, in_specs, out_specs, out_shape, scratch=(), limit=48, after=(), aliases=()):
    inputs = len(in_specs)

    def body_of(places_ref, *refs):
        kernel(places_ref, *refs[:inputs], *refs[inputs + len(after) :])

    run = pl.pallas_call(
        body_of,
        grid_spec=pltpu.PrefetchScalarGridSpec(
            num_scalar_prefetch=1,
            grid=grid,
            in_specs=in_specs + [anywhere()] * len(after),
            out_specs=out_specs,
            scratch_shapes=list(scratch),
        ),
        out_shape=out_shape,
        input_output_aliases=dict(aliases),
        compiler_params=pltpu.CompilerParams(vmem_limit_bytes=limit * 1024 * 1024),
        cost_estimate=pl.CostEstimate(flops=1, bytes_accessed=1, transcendentals=0),
    )
    return lambda *operands: run(*operands, *after)


def anywhere():
    return pl.BlockSpec(memory_space=pl.ANY)


def hold(places, value, *after):
    def kernel(places_ref, value_ref, o_ref):
        pass

    return call(
        kernel,
        (1,),
        [anywhere()],
        anywhere(),
        sds(value.shape, value.dtype),
        limit=1,
        after=after,
        aliases=((1, 0),),
    )(places, value)


def sds(shape, dtype):
    return jax.ShapeDtypeStruct(shape, dtype)


def whole(array):
    zeros = (0,) * array.ndim
    return pl.BlockSpec(array.shape, lambda *_: zeros)


def quarters(shape):
    if shape[0] % 64 == 0:
        return (shape[0] // 4, shape[1]), lambda m: (m, 0)
    return (shape[0], shape[1] // 4), lambda m: (0, m)


def add(places, terms, after=()):
    shape = terms[0][0].shape[len(terms[0][1]) :]
    steps = 4 if shape[0] % 64 == 0 else 1
    tile = shape[0] // steps

    def spec(at):
        return pl.BlockSpec((None,) * len(at) + (tile, shape[1]), lambda m, _: at + (m, 0))

    def kernel(places_ref, *refs):
        total = refs[0][...].astype(jnp.float32)
        for ref in refs[1:-1]:
            total = total + ref[...].astype(jnp.float32)
        refs[-1][...] = total.astype(jnp.bfloat16)

    return call(
        kernel,
        (steps,),
        [spec(at) for _, at in terms],
        spec(()),
        sds(shape, jnp.bfloat16),
        after=after,
    )(places, *[array for array, _ in terms])


def contract(left, right):
    return lax.dot_general(
        left, right, (((0,), (0,)), ((), ())), preferred_element_type=jnp.float32
    )


def take_columns(places, w, count, shards, groups, copies, pad, after=()):
    depth = w.shape[0]
    each = w.shape[1] // groups
    unit = each // (shards * count)
    tile = depth // 4

    def kernel(places_ref, w_ref, o_ref):
        for i in range(count):

            @pl.when(places_ref[0] == i)
            def _():
                block = jnp.concatenate(
                    [
                        w_ref[:, (s * count + i) * unit : (s * count + i + 1) * unit]
                        for s in range(shards)
                    ],
                    axis=1,
                )
                for copy in range(copies):
                    o_ref[copy] = block

    return call(
        kernel,
        (groups, 4),
        [pl.BlockSpec((tile, each), lambda g, m, _: (m, g))],
        pl.BlockSpec((copies, tile, each // count), lambda g, m, _: (0, m, g)),
        sds((copies, depth + pad, w.shape[1] // count), jnp.bfloat16),
        after=after,
    )(places, w)


def take_pairs(places, w, count, shards, after=()):
    depth = w.shape[0]
    each = w.shape[1] // 2
    unit = each // (shards * count)
    tile = depth // 4

    def kernel(places_ref, gate_ref, up_ref, o_ref):
        for i in range(count):

            @pl.when(places_ref[0] == i)
            def _():
                for part, ref in enumerate((gate_ref, up_ref)):
                    block = jnp.concatenate(
                        [
                            ref[:, (s * count + i) * unit : (s * count + i + 1) * unit]
                            for s in range(shards)
                        ],
                        axis=1,
                    )
                    for n in range(each // count // 128):
                        at = (2 * n + part) * 128
                        o_ref[:, at : at + 128] = block[:, n * 128 : (n + 1) * 128]

    return call(
        kernel,
        (4,),
        [
            pl.BlockSpec((tile, each), lambda m, _: (m, 0)),
            pl.BlockSpec((tile, each), lambda m, _: (m, 1)),
        ],
        pl.BlockSpec((tile, 2 * each // count), lambda m, _: (m, 0)),
        sds((depth, 2 * each // count), jnp.bfloat16),
        after=after,
    )(places, w, w)


def interleave(blocks, shards):
    unit = blocks[0].shape[1] // shards
    return [
        jnp.concatenate([block[:, s * unit : (s + 1) * unit] for block in blocks], axis=1)
        for s in range(shards)
    ]


def spread_pairs(places, gathered, count, shards, after=()):
    depth = gathered.shape[0] // count
    width = gathered.shape[1]
    each = width // 2
    unit = each // shards * count
    tile = depth // 8

    def kernel(places_ref, x_ref, o_ref):
        for part in range(2):
            blocks = []
            for i in range(count):
                tiles = [
                    x_ref[i][:, (2 * n + part) * 128 : (2 * n + part + 1) * 128]
                    for n in range(each // 128)
                ]
                blocks.append(jnp.concatenate(tiles, axis=1).astype(jnp.float32))
            for s, block in enumerate(interleave(blocks, shards)):
                at = part * each * count + s * unit
                o_ref[:, at : at + unit] = block

    return call(
        kernel,
        (8,),
        [pl.BlockSpec((count, tile, width), lambda m, _: (0, m, 0))],
        pl.BlockSpec((tile, width * count), lambda m, _: (m, 0)),
        sds((depth, width * count), jnp.float32),
        after=after,
    )(places, gathered.reshape(count, depth, width))


def spread_columns(places, pieces, count, shards, after=()):
    groups = len(pieces)
    depth, each = pieces[0][0].shape
    unit = each // shards * count
    tile = depth // 4
    flat = [piece for group in pieces for piece in group]

    def kernel(places_ref, *refs):
        o_ref = refs[-1]
        for g in range(groups):
            values = [refs[g * count + p][...].astype(jnp.float32) for p in range(count)]
            blocks = []
            for i in range(count):
                block = values[0]
                for p in range(1, count):
                    block = jnp.where(places_ref[1 + i] == p, values[p], block)
                blocks.append(block)
            for s, block in enumerate(interleave(blocks, shards)):
                at = g * each * count + s * unit
                o_ref[:, at : at + unit] = block

    spec = pl.BlockSpec((tile, each), lambda m, _: (m, 0))
    return call(
        kernel,
        (4,),
        [spec] * len(flat),
        pl.BlockSpec((tile, groups * each * count), lambda m, _: (m, 0)),
        sds((depth, groups * each * count), jnp.float32),
        after=after,
    )(places, *flat)


def norm_stats(values):
    average = jnp.mean(values, axis=-1, keepdims=True)
    centred = values - average
    inverse = lax.rsqrt(jnp.mean(centred * centred, axis=-1, keepdims=True) + epsilon)
    return centred * inverse, inverse


def norm_tokens(places, tokens, gain, bias, count, after=()):
    length = tokens.shape[0]
    tile = length // count // 2
    shards, depth = gain.shape

    def kernel(places_ref, x_ref, gain_ref, bias_ref, o_ref, plain_ref):
        plain_ref[...], _ = norm_stats(x_ref[...].astype(jnp.float32))
        for r in range(shards):
            start = pl.multiple_of(places_ref[1 + count + r] * depth, depth)
            block = plain_ref[:, pl.ds(start, depth)]
            o_ref[:, r * depth : (r + 1) * depth] = (
                block * gain_ref[r : r + 1] + bias_ref[r : r + 1]
            ).astype(jnp.bfloat16)

    return call(
        kernel,
        (count, 2),
        [
            pl.BlockSpec((tile, D), lambda b, h, p: (p[1 + b] * 2 + h, 0)),
            whole(gain),
            whole(bias),
        ],
        pl.BlockSpec((tile, D), lambda b, h, _: (b * 2 + h, 0)),
        sds((length, D), jnp.bfloat16),
        [pltpu.VMEM((tile, D), jnp.float32)],
        after=after,
    )(places, tokens, gain, bias)


def norm_hidden(places, tokens, pieces, gain, bias, after=()):
    rows = tokens.shape[0]
    tile = rows // 4

    def kernel(places_ref, x_ref, *refs):
        gain_ref, bias_ref, hidden_ref, o_ref = refs[-4:]
        hidden = x_ref[...].astype(jnp.float32)
        for ref in refs[:-4]:
            hidden = hidden + ref[...].astype(jnp.float32)
        hidden_ref[...] = hidden
        normal, _ = norm_stats(hidden)
        o_ref[...] = (normal * gain_ref[...] + bias_ref[...]).astype(jnp.bfloat16)

    spec = pl.BlockSpec((tile, D), lambda m, _: (m, 0))
    return call(
        kernel,
        (4,),
        [spec] * (1 + len(pieces)) + [whole(gain), whole(bias)],
        [spec, spec],
        [sds((rows, D), jnp.float32), sds((rows, D), jnp.bfloat16)],
        after=after,
    )(places, tokens, *pieces, gain, bias)


def norm_back(places, source, pieces, gain, added, first, low, after=()):
    rows = source.shape[0]
    tile = rows // 4
    shards, depth = gain.shape

    def kernel(places_ref, x_ref, added_ref, gain_ref, *refs):
        piece_refs = refs[: len(pieces)]
        out_refs = refs[len(pieces) : -2]
        sums_ref = out_refs[-1]
        grad_ref, gain_plain = refs[-2:]
        for r in range(shards):
            start = pl.multiple_of(places_ref[first + r] * depth, depth) if shards > 1 else 0
            at = slice(r * depth, (r + 1) * depth)
            block = piece_refs[0][:, at].astype(jnp.float32)
            for ref in piece_refs[1:]:
                block = block + ref[:, at].astype(jnp.float32)
            grad_ref[:, pl.ds(start, depth)] = block
            gain_plain[:, pl.ds(start, depth)] = jnp.broadcast_to(gain_ref[r : r + 1], (8, depth))
        normal, inverse = norm_stats(x_ref[...].astype(jnp.float32))
        grad = grad_ref[...]

        @pl.when(pl.program_id(0) == 0)
        def _():
            sums_ref[...] = jnp.zeros_like(sums_ref)

        sums_ref[0:1] += jnp.sum(grad * normal, axis=0, keepdims=True)
        sums_ref[1:2] += jnp.sum(grad, axis=0, keepdims=True)
        scaled = grad * gain_plain[0:1]
        mean = jnp.mean(scaled, axis=-1, keepdims=True)
        second = jnp.mean(scaled * normal, axis=-1, keepdims=True)
        total = added_ref[...].astype(jnp.float32) + inverse * (scaled - mean - normal * second)
        out_refs[0][...] = total
        if low:
            out_refs[1][...] = total.astype(jnp.bfloat16)

    spec = pl.BlockSpec((tile, D), lambda m, _: (m, 0))
    sums = pl.BlockSpec((2, D), lambda m, _: (0, 0))
    return call(
        kernel,
        (4,),
        [spec, spec, whole(gain)] + [spec] * len(pieces),
        [spec] + [spec] * low + [sums],
        [sds((rows, D), jnp.float32)]
        + [sds((rows, D), jnp.bfloat16)] * low
        + [sds((2, D), jnp.float32)],
        [pltpu.VMEM((tile, D), jnp.float32), pltpu.VMEM((8, D), jnp.float32)],
        after=after,
    )(places, source, added, gain, *pieces)


def project(places, normed, near, far, group, bias, tables, after=()):
    length = normed.shape[0]
    width = bias.shape[1]
    tile = min(width, 256)
    blocks = near.shape[0]
    depth = D // blocks // 2

    def kernel(places_ref, x_ref, near_ref, far_ref, bias_ref, *refs):
        o_ref = refs[-1]
        total = bias_ref[...]
        for i, ref in enumerate((near_ref, far_ref)):
            weight = ref[...].reshape(D // 2, tile)
            left = x_ref[:, i * (D // 2) : (i + 1) * (D // 2)]
            total = total + jnp.dot(left, weight, preferred_element_type=jnp.float32)
        if tables:
            cosine, low, high = (
                jnp.concatenate([ref[...]] * (tile // 128), axis=1) for ref in refs[:3]
            )
            total = (
                total * cosine
                + pltpu.roll(total, tile - ROT // 2, 1) * low
                + pltpu.roll(total, ROT // 2, 1) * high
            )
        o_ref[...] = total.astype(jnp.bfloat16)

    steps = width // tile
    weight = pl.BlockSpec((blocks, depth, tile), lambda n, _: (0, 0, group * steps + n))
    return call(
        kernel,
        (steps,),
        [whole(normed), weight, weight, pl.BlockSpec((1, tile), lambda n, _: (0, n))]
        + [whole(table) for table in tables],
        pl.BlockSpec((length, tile), lambda n, _: (0, n)),
        sds((length, width), jnp.bfloat16),
        after=after,
    )(places, normed, near, far, bias, *tables)


def head_lanes(values, head):
    lanes = lax.broadcasted_iota(jnp.int32, values.shape, 1)
    return jnp.where((lanes >= head * E) & (lanes < (head + 1) * E), values, jnp.zeros_like(values))


def to_plain_rows(places_ref, source_ref, target_ref, count):
    rows = target_ref.shape[0] // count
    for b in range(count):
        start = pl.multiple_of(places_ref[1 + b] * rows, rows)
        target_ref[b * rows : (b + 1) * rows] = source_ref[pl.ds(start, rows)]


def masked(shape, keys_seg, query_seg, first):
    ks = lax.broadcasted_iota(jnp.int32, shape, 0)
    qs = lax.broadcasted_iota(jnp.int32, shape, 1) + first
    return (ks <= qs) & (keys_seg == query_seg)


def attend(places, qkv, seg_col, seg_row, count, heads, after=()):
    length = qkv[0].shape[0]
    pairs = heads // 2
    step = math.gcd(length, 256)
    rows = length // count

    def kernel(places_ref, q_ref, k_ref, v_ref, col_ref, row_ref, o_ref, log_ref, vt, os):
        vt[...] = jnp.transpose(v_ref[...].astype(jnp.float32)).astype(jnp.bfloat16)
        for a in range(length // step):
            n = (a + 1) * step
            halves = []
            allowed = masked((n, step), col_ref[0:n], row_ref[:, a * step : n], a * step)
            for h in range(2):
                query = head_lanes(q_ref[a * step : n], h) * scale
                scores = lax.dot_general(
                    k_ref[0:n], query, (((1,), (1,)), ((), ())), preferred_element_type=jnp.float32
                )
                scores = jnp.where(allowed, scores, masked_score)
                top = jnp.max(scores, axis=0, keepdims=True)
                weights = jnp.exp(scores - top)
                total = jnp.sum(weights, axis=0, keepdims=True)
                out = jnp.dot(
                    vt[h * E : (h + 1) * E, 0:n],
                    weights.astype(jnp.bfloat16),
                    preferred_element_type=jnp.float32,
                )
                halves.append(out / total)
                log_ref[0, h : h + 1, a * step : n] = top + jnp.log(total)
            os[a * step : n] = jnp.transpose(jnp.concatenate(halves, axis=0)).astype(jnp.bfloat16)
        for b in range(count):
            start = pl.multiple_of(places_ref[1 + b] * rows, rows)
            o_ref[pl.ds(start, rows)] = os[b * rows : (b + 1) * rows]

    def columns(group):
        return pl.BlockSpec((length, 128), lambda p, _: (0, group * pairs + p))

    scratch = pltpu.VMEM((length, 128), jnp.bfloat16)
    return call(
        kernel,
        (pairs,),
        [columns(0), columns(0), columns(0), whole(seg_col), whole(seg_row)],
        [columns(0), pl.BlockSpec((1, 2, length), lambda p, _: (p, 0, 0))],
        [
            sds((length, heads * E), jnp.bfloat16),
            sds((pairs, 2, length), jnp.float32),
        ],
        [pltpu.VMEM((128, length), jnp.bfloat16), scratch],
        after=after,
    )(places, *qkv, seg_col, seg_row)


def attend_back(
    places, qkv, grad_attended, logs, seg_col, seg_row, tables, count, heads, after=()
):
    length = qkv[0].shape[0]
    pairs = heads // 2
    step = math.gcd(length, 256)
    rows = length // count

    def kernel(
        places_ref,
        q_ref,
        k_ref,
        v_ref,
        g_ref,
        log_ref,
        col_ref,
        row_ref,
        cos_ref,
        low_ref,
        high_ref,
        dq_ref,
        dk_ref,
        dv_ref,
        sums_ref,
        gs,
        kt,
        dq,
        dk,
        dv,
    ):
        to_plain_rows(places_ref, g_ref, gs, count)
        kt[...] = jnp.transpose(k_ref[...].astype(jnp.float32)).astype(jnp.bfloat16)
        dk[...] = jnp.zeros_like(dk)
        dv[...] = jnp.zeros_like(dv)
        for a in range(length // step):
            n = (a + 1) * step
            halves = []
            allowed = masked((n, step), col_ref[0:n], row_ref[:, a * step : n], a * step)
            for h in range(2):
                query = head_lanes(q_ref[a * step : n], h) * scale
                grad = head_lanes(gs[a * step : n], h)
                scores = lax.dot_general(
                    k_ref[0:n], query, (((1,), (1,)), ((), ())), preferred_element_type=jnp.float32
                )
                log = log_ref[0, h : h + 1, a * step : n]
                weights = jnp.exp(jnp.where(allowed, scores - log, masked_score))
                grad_weights = lax.dot_general(
                    v_ref[0:n], grad, (((1,), (1,)), ((), ())), preferred_element_type=jnp.float32
                )
                product = weights * grad_weights
                delta = jnp.sum(product, axis=0, keepdims=True)
                grad_scores = (product - weights * delta).astype(jnp.bfloat16)
                dv[0:n] += jnp.dot(
                    weights.astype(jnp.bfloat16), grad, preferred_element_type=jnp.float32
                )
                dk[0:n] += jnp.dot(grad_scores, query, preferred_element_type=jnp.float32)
                halves.append(
                    jnp.dot(
                        kt[h * E : (h + 1) * E, 0:n],
                        grad_scores,
                        preferred_element_type=jnp.float32,
                    )
                )
            dq[a * step : n] = jnp.transpose(jnp.concatenate(halves, axis=0))

        sums = [jnp.zeros((1, 128), jnp.float32)] * 3
        for b in range(count):
            at = slice(b * rows, (b + 1) * rows)
            cosine, low, high = cos_ref[at], low_ref[at], high_ref[at]
            for i, (part, out_ref) in enumerate(((dq, dq_ref), (dk, dk_ref), (dv, dv_ref))):
                block = part[at]
                if i == 0:
                    block = block * scale
                if i < 2:
                    block = (
                        block * cosine
                        - pltpu.roll(block, 128 - ROT // 2, 1) * low
                        - pltpu.roll(block, ROT // 2, 1) * high
                    )
                block = block.astype(jnp.bfloat16)
                sums[i] = sums[i] + jnp.sum(block.astype(jnp.float32), axis=0, keepdims=True)
                out_ref[at] = block
        for i in range(3):
            sums_ref[i] = sums[i]

    def columns(group):
        return pl.BlockSpec((length, 128), lambda p, _: (0, group * pairs + p))

    low_scratch = pltpu.VMEM((length, 128), jnp.bfloat16)
    scratch = pltpu.VMEM((length, 128), jnp.float32)
    width = heads * E
    return call(
        kernel,
        (pairs,),
        [
            columns(0),
            columns(0),
            columns(0),
            columns(0),
            pl.BlockSpec((1, 2, length), lambda p, _: (p, 0, 0)),
            whole(seg_col),
            whole(seg_row),
            whole(tables[0]),
            whole(tables[1]),
            whole(tables[2]),
        ],
        [columns(0)] * 3 + [pl.BlockSpec((3, 1, 128), lambda p, _: (0, 0, p))],
        [sds((length, width), jnp.bfloat16)] * 3 + [sds((3, 1, width), jnp.float32)],
        [low_scratch]
        + [pltpu.VMEM((128, length), jnp.bfloat16), scratch, scratch, scratch],
        after=after,
    )(places, *qkv, grad_attended, logs, seg_col, seg_row, *tables)


def join_rows(places_ref, first, refs, joined):
    halves = len(refs) // 2
    width = refs[0].shape[-1]
    for at, ref in enumerate(refs):
        blocks, size, _ = ref.shape
        columns = slice(at % halves * width, (at % halves + 1) * width)
        for i in range(blocks):
            place = places_ref[first + at // halves * blocks + i]
            joined[pl.ds(pl.multiple_of(place * size, size), size), columns] = ref[i]


def row_product(places, left, parts, count, after=()):
    length, depth = left.shape
    tile = D // 4

    def kernel(places_ref, x_ref, *refs):
        near_ref, far_ref, joined = refs[-3:]

        @pl.when(pl.program_id(0) == 0)
        def _():
            join_rows(places_ref, 1 + count, refs[:-3], joined)

        start = pl.multiple_of(pl.program_id(0) * tile, tile)
        total = jnp.dot(
            x_ref[...], joined[:, pl.ds(start, tile)], preferred_element_type=jnp.float32
        ).astype(jnp.bfloat16)
        near_ref[...] = total[: length // 2]
        far_ref[...] = total[length // 2 :]

    spec = pl.BlockSpec((length // 2, tile), lambda n, _: (0, n))
    shape = sds((length // 2, D), jnp.bfloat16)
    return call(
        kernel,
        (4,),
        [whole(left)] + [whole(part) for part in parts],
        [spec, spec],
        [shape, shape],
        [pltpu.VMEM((depth, D), jnp.bfloat16)],
        after=after,
    )(places, left, *parts)


def grad_out(places, pieces, near, far, count, after=()):
    rows = pieces[0].shape[0]
    width = near.shape[0] * near.shape[1] * 2
    tile = rows

    def kernel(places_ref, *refs):
        piece_refs = refs[:count]
        a_ref, b_ref, o_ref, all_ref, joined = refs[count:]

        @pl.when(pl.program_id(0) == 0)
        def _():
            join_rows(places_ref, 1 + count, (a_ref, b_ref), joined)

        for p, ref in enumerate(piece_refs):

            @pl.when(pl.program_id(0) == p)
            def _():
                all_ref[...] = ref[...]
                o_ref[...] = lax.dot_general(
                    ref[...],
                    joined[...],
                    (((1,), (1,)), ((), ())),
                    preferred_element_type=jnp.float32,
                ).astype(jnp.bfloat16)

    return call(
        kernel,
        (count,),
        [whole(piece) for piece in pieces] + [whole(near), whole(far)],
        [
            pl.BlockSpec((tile, width), lambda m, _: (m, 0)),
            pl.BlockSpec((tile, D), lambda m, _: (m, 0)),
        ],
        [sds((rows * count, width), jnp.bfloat16), sds((rows * count, D), jnp.bfloat16)],
        [pltpu.VMEM((width, D), jnp.bfloat16)],
        after=after,
    )(places, *pieces, near, far)


def gate_product(places, pieces, weight, after=()):
    rows = pieces[0].shape[0]
    length = rows * len(pieces)
    width = weight.shape[1]

    def kernel(places_ref, *refs):
        *piece_refs, w_ref, all_ref, both_ref, activ_ref = refs

        @pl.when(pl.program_id(0) == 0)
        def _():
            for p, ref in enumerate(piece_refs):
                all_ref[p * rows : (p + 1) * rows] = ref[...]

        both = jnp.dot(all_ref[...], w_ref[...], preferred_element_type=jnp.float32)
        gate = both[:, :128]
        both_ref[...] = both.astype(jnp.bfloat16)
        activ_ref[...] = (gate * jax.nn.sigmoid(gate) * both[:, 128:]).astype(jnp.bfloat16)

    return call(
        kernel,
        (width // 256,),
        [whole(piece) for piece in pieces] + [pl.BlockSpec((D, 256), lambda n, _: (0, n))],
        [
            pl.BlockSpec((length, D), lambda n, _: (0, 0)),
            pl.BlockSpec((length, 256), lambda n, _: (0, n)),
            pl.BlockSpec((length, 128), lambda n, _: (0, n)),
        ],
        [
            sds((length, D), jnp.bfloat16),
            sds((length, width), jnp.bfloat16),
            sds((length, width // 2), jnp.bfloat16),
        ],
        limit=56,
        after=after,
    )(places, *pieces, weight)


def gate_back(places, cotangent, parts, both, count, after=()):
    length, width = both.shape
    units = width // 2
    steps = -(-units // 256)

    def kernel(places_ref, x_ref, both_ref, *refs):
        o_ref, joined = refs[-2:]

        @pl.when(pl.program_id(0) == 0)
        def _():
            join_rows(places_ref, 1 + count, refs[:-2], joined)

        start = pl.multiple_of(pl.program_id(0) * 256, 256)
        grad = lax.dot_general(
            x_ref[...],
            joined[pl.ds(start, 256)],
            (((1,), (1,)), ((), ())),
            preferred_element_type=jnp.float32,
        )
        for i in range(2):
            part = grad[:, i * 128 : (i + 1) * 128]
            gate = both_ref[:, i * 256 : i * 256 + 128].astype(jnp.float32)
            upward = both_ref[:, i * 256 + 128 : (i + 1) * 256].astype(jnp.float32)
            sigma = jax.nn.sigmoid(gate)
            grad_gate = part * upward * sigma * (1.0 + gate * (1.0 - sigma))
            o_ref[:, i * 256 : i * 256 + 128] = grad_gate.astype(jnp.bfloat16)
            o_ref[:, i * 256 + 128 : (i + 1) * 256] = (part * (gate * sigma)).astype(jnp.bfloat16)

    spec = pl.BlockSpec((length, 512), lambda n, _: (0, n))
    return call(
        kernel,
        (steps,),
        [whole(cotangent), spec] + [whole(part) for part in parts],
        spec,
        sds((length, width), jnp.bfloat16),
        [pltpu.VMEM((steps * 256, D), jnp.bfloat16)],
        limit=56,
        after=after,
    )(places, cotangent, both, *parts)


def normed_grad(places, left, weight, after=()):
    length, width = left.shape

    def kernel(places_ref, x_ref, w_ref, near_ref, far_ref):
        total = lax.dot_general(
            x_ref[...], w_ref[...], (((1,), (1,)), ((), ())), preferred_element_type=jnp.float32
        ).astype(jnp.bfloat16)
        near_ref[...] = total[: length // 2]
        far_ref[...] = total[length // 2 :]

    spec = pl.BlockSpec((length // 2, 256), lambda n, _: (0, n))
    shape = sds((length // 2, D), jnp.bfloat16)
    return call(
        kernel,
        (D // 256,),
        [whole(left), pl.BlockSpec((256, width), lambda n, _: (n, 0))],
        [spec, spec],
        [shape, shape],
        limit=56,
        after=after,
    )(places, left, weight)


def normed_grad_parts(places, lefts, parts, count, after=()):
    length, width = lefts[0].shape
    rows = length // count
    blocks = parts[0].shape[0]
    depth = D // blocks // 2
    total_width = width * len(lefts)

    def kernel(places_ref, *refs):
        left_refs = refs[: len(lefts)]
        near_part, far_part, near_ref, far_ref, joined = refs[len(lefts) :]

        @pl.when(pl.program_id(0) == 0)
        def _():
            for b in range(count):
                start = pl.multiple_of(places_ref[1 + b] * rows, rows)
                for i, ref in enumerate(left_refs):
                    joined[pl.ds(start, rows), i * width : (i + 1) * width] = ref[
                        b * rows : (b + 1) * rows
                    ]

        def run(weight_ref):
            total = lax.dot_general(
                joined[...], weight_ref[0], (((1,), (1,)), ((), ())), preferred_element_type=jnp.float32
            ).astype(jnp.bfloat16)
            near_ref[...] = total[: length // 2]
            far_ref[...] = total[length // 2 :]

        @pl.when(pl.program_id(0) < blocks)
        def _():
            run(near_part)

        @pl.when(pl.program_id(0) >= blocks)
        def _():
            run(far_part)

    near_spec = pl.BlockSpec(
        (1, depth, total_width), lambda n, _: (jnp.minimum(n, blocks - 1), 0, 0)
    )
    far_spec = pl.BlockSpec(
        (1, depth, total_width), lambda n, _: (jnp.maximum(n - blocks, 0), 0, 0)
    )
    spec = pl.BlockSpec((length // 2, depth), lambda n, _: (0, n))
    shape = sds((length // 2, D), jnp.bfloat16)
    return call(
        kernel,
        (2 * blocks,),
        [whole(left) for left in lefts] + [near_spec, far_spec],
        [spec, spec],
        [shape, shape],
        [pltpu.VMEM((length, total_width), jnp.bfloat16)],
        after=after,
    )(places, *lefts, *parts)


def turn(source_ref, first, columns, target_ref):
    step = math.gcd(columns, 256)
    for at in range(0, columns, step):
        block = source_ref[:, first + at : first + at + step].astype(jnp.float32)
        target_ref[at : at + step] = jnp.transpose(block).astype(jnp.bfloat16)


def pairs_grad(places, normed, right, after=()):
    length, width = right.shape

    def kernel(places_ref, x_ref, g_ref, o_ref, turned):
        @pl.when(pl.program_id(0) == 0)
        def _():
            turn(x_ref, 0, D, turned)

        o_ref[...] = jnp.dot(
            turned[...], g_ref[...], preferred_element_type=jnp.float32
        ).astype(jnp.bfloat16)

    return call(
        kernel,
        (width // 256,),
        [whole(normed), pl.BlockSpec((length, 256), lambda n, _: (0, n))],
        pl.BlockSpec((D, 256), lambda n, _: (0, n)),
        sds((D, width), jnp.bfloat16),
        [pltpu.VMEM((D, length), jnp.bfloat16)],
        after=after,
    )(places, normed, right)


def column_loads(places, normed, rights, after=()):
    length, width = rights[0].shape
    count = len(rights)
    rows = D // 2

    def kernel(places_ref, x_ref, *refs):
        right_refs, out_refs = refs[:count], refs[count : 2 * count]
        turned_ref, turned = refs[2 * count :]
        step = pl.program_id(0)

        @pl.when(step == 0)
        def _():
            turn(x_ref, rows, rows, turned)

        for i in range(count):

            @pl.when(step == i)
            def _():
                out_refs[i][...] = jnp.dot(
                    turned[...], right_refs[i][...], preferred_element_type=jnp.float32
                ).astype(jnp.bfloat16)

        @pl.when(step == count - 1)
        def _():
            turn(x_ref, 0, rows, turned_ref)

    shape = sds((rows, width), jnp.bfloat16)
    own = sds((rows, length), jnp.bfloat16)
    return call(
        kernel,
        (count,),
        [whole(normed)] + [whole(right) for right in rights],
        [whole(shape)] * count + [whole(own)],
        [shape] * count + [own],
        [pltpu.VMEM((rows, length), jnp.bfloat16)],
        after=after,
    )(places, normed, *rights)


def column_keep(places, turned, right, arrived, after=()):
    rows, length = turned.shape
    width = right.shape[1]
    tile = width // 2

    def kernel(places_ref, x_ref, g_ref, arrived_ref, o_ref):
        total = jnp.dot(x_ref[...], g_ref[...], preferred_element_type=jnp.float32)
        o_ref[...] = (total + arrived_ref[...].astype(jnp.float32)).astype(jnp.bfloat16)

    spec = pl.BlockSpec((rows, tile), lambda n, _: (0, n))
    return call(
        kernel,
        (2,),
        [whole(turned), pl.BlockSpec((length, tile), lambda n, _: (0, n)), spec],
        spec,
        sds((rows, width), jnp.bfloat16),
        after=after,
    )(places, turned, right, arrived)


def row_grad(places, left, right, size, count, stacked, after=()):
    length, width = left.shape
    tile = D // 4
    blocks = width // size // 2

    def kernel(places_ref, x_ref, g_ref, *refs):
        total_ref = refs[-1]
        total_ref[...] = contract(x_ref[...], g_ref[...])
        halves = 1 if stacked else 2
        for half in range(halves):

            @pl.when(pl.program_id(0) // 2 == half if halves > 1 else pl.program_id(0) >= 0)
            def _():
                for side in range(2):
                    for r in range(blocks):
                        place = places_ref[1 + count + side * blocks + r]
                        start = pl.multiple_of(place * size, size)
                        block = total_ref[pl.ds(start, size)].astype(jnp.bfloat16)
                        refs[side * halves + half][r] = block

    block = (blocks, size, tile)
    if stacked:
        specs = [pl.BlockSpec(block, lambda n, _: (0, n, 0))] * 2
        shapes = [sds((blocks, 4 * size, tile), jnp.bfloat16)] * 2
    else:
        first = pl.BlockSpec(block, lambda n, _: (0, 0, jnp.minimum(n, 1)))
        second = pl.BlockSpec(block, lambda n, _: (0, 0, jnp.maximum(n - 2, 0)))
        specs = [first, second] * 2
        shapes = [sds((blocks, size, D // 2), jnp.bfloat16)] * 4
    return call(
        kernel,
        (4,),
        [whole(left), pl.BlockSpec((length, tile), lambda n, _: (0, n))],
        specs,
        shapes,
        [pltpu.VMEM((width, tile), jnp.float32)],
        after=after,
    )(places, left, right)


def to_line(blocks):
    return lax.all_to_all(blocks, "dp", split_axis=0, concat_axis=0)


def rows_gather(own):
    pieces = [own]
    bit = lax.axis_size("ctx") // 2
    while bit >= 1:
        pieces = pieces + [swap(piece, "ctx", bit) for piece in pieces]
        bit //= 2
    return pieces


def rows_scatter(places, near, far, after=()):
    count = lax.axis_size("ctx")
    pieces = [near, swap(far, "ctx", 1)]
    bit = 2
    while bit < count:
        pieces = [piece.reshape(2, -1, D) for piece in pieces]
        load = add(places, [(piece, (1,)) for piece in pieces], after if 2 * bit == count else ())
        pieces = [piece[0] for piece in pieces] if 2 * bit < count else [
            piece.reshape(-1, D) for piece in pieces
        ]
        pieces.append(swap(load, "ctx", bit))
        bit *= 2
    return pieces


def fast_body(
    tokens,
    segment_ids,
    cotangent,
    ln1_gain,
    ln1_bias,
    w_qkv,
    b_qkv,
    w_out,
    ln2_gain,
    ln2_bias,
    w_gate_up,
    w_down,
):
    rows = tokens.shape[1]
    count = lax.axis_size("ctx")
    ctx = lax.axis_index("ctx")
    line = lax.axis_size("dp")
    here = lax.axis_index("dp")
    side = lax.axis_index("fsdp")
    shards = 2 * line
    depth = D // shards
    heads = H // count
    width = heads * E
    length = rows * count

    def reversed_bits(value):
        return sum(
            ((value >> i) & 1) * (count >> (i + 1)) for i in range(count.bit_length() - 1)
        )

    shard_of = [(r % line) * 2 + (side ^ (r // line)) for r in range(shards)]
    index = jnp.arange(1 + count + shards, dtype=jnp.int32)
    r = jnp.maximum(index - 1 - count, 0)
    places = jnp.where(
        index <= count,
        reversed_bits(jnp.clip(index - 1, 0, count - 1) ^ ctx),
        lax.rem(r, line) * 2 + (side ^ lax.div(r, line)),
    )
    places = jnp.where(index == 0, ctx, places).astype(jnp.int32)

    small = jnp.concatenate([ln1_gain, ln1_bias, ln2_gain, ln2_bias, b_qkv])
    pad = 16
    qkv_mine = take_columns(places, w_qkv, count, shards, 3, line, pad)
    lead = jnp.pad(small, (0, 2 * 3 * width - small.shape[0])).reshape(1, 2, 3 * width)
    lead = jnp.pad(lead, ((0, 0), (0, pad - 2), (0, 0)))
    qkv_mine = lax.dynamic_update_slice(
        qkv_mine, jnp.broadcast_to(lead, (line, pad, 3 * width)), (0, depth, 0)
    )

    def weight(blocks):
        near = to_line(blocks)
        return near, swap(near, "fsdp", 1)

    def row_copies(w, *after):
        block = hold(places, pick(w.reshape(count, -1, D), ctx, 0), *after)
        return jnp.broadcast_to(block[None], (line,) + block.shape)

    token_rows = jnp.concatenate(rows_gather(tokens[0]), axis=0)
    cot_rows = jnp.concatenate(
        rows_gather(hold(places, cotangent[0], token_rows)), axis=0
    )
    qkv_parts = weight(qkv_mine)
    gate_mine = take_pairs(places, w_gate_up, count, shards, (qkv_parts[0], token_rows))
    gate_up = lax.all_gather(gate_mine, ("dp", "fsdp"), axis=0, tiled=True)
    out_parts = weight(row_copies(w_out, qkv_parts[0], cot_rows))
    seg_row = lax.all_gather(segment_ids, "ctx", axis=1, tiled=True)
    seg_col = seg_row.reshape(length, 1)

    half = ROT // 2
    angles = np.arange(length)[:, None] * 10000.0 ** (-np.arange(half) * 2.0 / ROT)[None, :]
    cosine, sine = np.cos(angles), np.sin(angles)
    flat = np.zeros((length, E - ROT))
    zero = np.zeros((length, half))
    tables = [
        jnp.asarray(np.concatenate(parts * 2, axis=1), jnp.float32)
        for parts in ([cosine, cosine, flat + 1.0], [-sine, zero, flat], [zero, sine, flat])
    ]

    small_rows = [part[:, depth : depth + 2] for part in qkv_parts]
    small_all = jnp.concatenate(small_rows, axis=0).reshape(shards, -1)[:, : small.shape[0]]
    small_all = small_all.astype(jnp.float32)
    small_plain = sum(
        (jnp.arange(shards)[:, None] == shard_of[r]) * small_all[r][None, :] for r in range(shards)
    )
    gain_one, bias_one = small_all[:, :depth], small_all[:, depth : 2 * depth]
    gain_two = small_plain[:, 2 * depth : 3 * depth].reshape(1, D)
    bias_two = small_plain[:, 3 * depth : 4 * depth].reshape(1, D)
    bias_plain = small_plain[:, 4 * depth :]
    bias_mine = pick(bias_plain.reshape(3, shards, count, E), ctx, 2).reshape(3, 1, width)

    normed_one = norm_tokens(places, token_rows, gain_one, bias_one, count, (seg_row,))
    qkv = []
    for i in range(3):
        turns = tables if i < 2 else []
        qkv.append(
            project(places, normed_one, *qkv_parts, i, bias_mine[i], turns, qkv[-1:])
        )
    down_copies = row_copies(w_down, out_parts[0])
    size = down_copies.shape[1]
    down_left = to_line(down_copies[..., : D // 2])
    down_right = to_line(hold(places, down_copies[..., D // 2 :], down_left))
    attended, logs = attend(places, qkv, seg_col, seg_row, count, heads)
    product = row_product(places, attended, out_parts, count)
    pieces = rows_scatter(places, *product)
    hidden, normed_two = norm_hidden(places, tokens[0], pieces, gain_two, bias_two)
    normed_pieces = rows_gather(normed_two)
    down_left = hold(places, down_left, product[0])
    down_right = hold(places, down_right, normed_pieces[1])
    down_parts = (
        down_left,
        down_right,
        swap(down_left, "fsdp", 1),
        swap(down_right, "fsdp", 1),
    )
    normed_two, both, activ = gate_product(places, normed_pieces, gate_up)

    def line_sum(blocks, after=()):
        arrived = to_line(blocks).reshape(line, -1, blocks.shape[-1])
        return add(places, [(arrived, (i,)) for i in range(line)], after)

    def both_sides(kept, arrived):
        return (kept.astype(jnp.float32) + arrived.astype(jnp.float32)).astype(jnp.bfloat16)

    keep_left, keep_right, load_left, load_right = row_grad(
        places, activ, cot_rows, size, count, False
    )
    left_arrived = swap(load_left, "fsdp", 1)
    right_arrived = swap(load_right, "fsdp", 1)
    grad_both = gate_back(places, cot_rows, down_parts, both, count, (load_right,))
    gate_part = pairs_grad(places, normed_two, grad_both)
    gate_grad = lax.psum_scatter(gate_part, ("dp", "fsdp"), scatter_dimension=0, tiled=True)
    pieces = rows_scatter(places, *normed_grad(places, grad_both, gate_up, (gate_part,)))
    down_pieces = row_product(places, activ, down_parts, count, (pieces[1],))
    left_total = both_sides(keep_left, hold(places, left_arrived, pieces[1]))
    grad_hidden, grad_branch, sums_two = norm_back(
        places, hidden, pieces, gain_two, cotangent[0], 0, True, (down_pieces[0], left_total,)
    )
    down_pieces = rows_scatter(places, *down_pieces, (grad_branch,))
    branch_pieces = rows_gather(grad_branch)
    down_total = both_sides(keep_right, hold(places, right_arrived, branch_pieces[1]))
    grad_attended, grad_branch = grad_out(
        places, branch_pieces, *out_parts, count, ( down_total,)
    )
    out_keep, out_load = row_grad(
        places, attended, grad_branch, out_parts[0].shape[1], count, True, ()
    )
    out_arrived = swap(out_load, "fsdp", 1)
    grads = attend_back(
        places,
        qkv,
        grad_attended,
        logs,
        seg_col,
        seg_row,
        tables,
        count,
        heads,
        (out_load, down_pieces[-1]),
    )
    grads, bias_sums = grads[:3], grads[3]
    out_total = both_sides(out_keep, out_arrived)
    *loads, turned = column_loads(places, normed_one, grads, ())
    arrivals = [swap(load, "fsdp", 1) for load in loads]
    mixed = hidden + sum(piece[:rows].astype(jnp.float32) for piece in down_pieces)
    mixed = mixed.astype(jnp.bfloat16)
    left_grad = line_sum(left_total, (loads[2],))
    down_grad = jnp.concatenate([left_grad, line_sum(down_total, (loads[2],))], axis=1)

    def ctx_rows(block):
        return lax.all_gather(block, "ctx", axis=0, tiled=True)

    def keep(i, *after):
        total = column_keep(places, turned, grads[i], arrivals[i], after)
        return total.reshape(line, depth, width)

    totals = [jnp.concatenate([keep(0, down_grad), out_total], axis=1)]
    near, far = normed_grad_parts(places, grads, qkv_parts, count, (totals[0],))
    gate_grad = hold(places, gate_grad, loads[0])
    gate_rows = ctx_rows(gate_grad)
    gate_out = spread_pairs(places, gate_rows, count, shards)
    down_out = ctx_rows(hold(places, down_grad, totals[0])).astype(jnp.float32)
    totals.append(keep(1, gate_out))
    pieces = rows_scatter(places, near, far, (totals[0],))
    q_sum = line_sum(totals[0], (mixed,))
    totals.append(keep(2, down_out))
    input_grad, sums_one = norm_back(
        places, tokens[0], pieces, gain_one, grad_hidden, 1 + count, False, ()
    )
    out_out = ctx_rows(q_sum[depth:]).reshape(count, 4, -1, D // 4)
    out_out = out_out.transpose(0, 2, 1, 3).reshape(-1, D).astype(jnp.float32)
    sums = [q_sum[:depth], line_sum(totals[1], ()), line_sum(totals[2], (out_out, down_out, gate_out))]
    qkv_grads = [rows_gather(total) for total in sums]
    qkv_out = spread_columns(places, qkv_grads, count, shards)

    bias_part = jnp.where(
        jnp.arange(count)[None, None, :, None] == ctx, bias_sums.reshape(3, shards, 1, E), 0.0
    ).reshape(shards, 3 * depth)
    small_part = jnp.concatenate(
        [part.reshape(shards, depth) for part in (*sums_one, *sums_two)] + [bias_part], axis=1
    ).reshape(line, 2, -1)
    load = pick(small_part, 1 - side, 1).astype(jnp.bfloat16)
    total = pick(small_part, side, 1) + swap(load, "fsdp", 1).astype(jnp.float32)
    low_total = total.astype(jnp.bfloat16)
    mine = pick(total, here, 0)
    for r in range(1, line):
        mine = mine + swap(pick(low_total, here ^ r, 0), "dp", r).astype(jnp.float32)
    bit = count // 2
    while bit >= 1:
        mine = mine + swap(mine, "ctx", bit)
        bit //= 2

    return (
        mixed[None],
        input_grad[None],
        mine[:depth],
        mine[depth : 2 * depth],
        qkv_out,
        mine[4 * depth :],
        out_out,
        mine[2 * depth : 3 * depth],
        mine[3 * depth : 4 * depth],
        gate_out,
        down_out,
    )


def fits(mesh):
    count, shards = mesh.shape["ctx"], mesh.shape["dp"] * mesh.shape["fsdp"]
    return (
        mesh.shape["fsdp"] == 2
        and count > 1
        and count & (count - 1) == 0
        and (H // shards) == count
        and (FF // shards) % (16 * count) == 0
        and (FF // count) % 128 == 0
        and (H // count) % 2 == 0
    )


def solution(mesh):
    shards = ("dp", "fsdp")
    row = P(shards, "ctx", None)
    vector = P(shards)
    matrix = P(shards, None)
    return jax.shard_map(
        fast_body if fits(mesh) else body,
        mesh=mesh,
        in_specs=(
            row,
            P(shards, "ctx"),
            row,
            vector,
            vector,
            matrix,
            vector,
            matrix,
            vector,
            vector,
            matrix,
            matrix,
        ),
        out_specs=(
            row,
            row,
            vector,
            vector,
            matrix,
            vector,
            matrix,
            vector,
            vector,
            matrix,
            matrix,
        ),
        check_vma=False,
    )
```

```python
import math

import jax
import jax.numpy as jnp
import numpy as np
from jax import lax
from jax.experimental import pallas as pl
from jax.experimental.pallas import tpu as pltpu
from jax.sharding import PartitionSpec as P

D = 2048
H = 32
E = 64
FF = 5632
ROT = 16

epsilon = 1e-05
masked_score = -1e30
scale = E ** (-0.5)


def swap(block, axis, bit):
    count = lax.axis_size(axis)
    return lax.ppermute(block, axis, [(i, i ^ bit) for i in range(count)])


def tie(value, *others):
    return lax.optimization_barrier((value, *others))[0]


def shard_index():
    return lax.axis_index("dp") * lax.axis_size("fsdp") + lax.axis_index("fsdp")


def gather_shards(block):
    near = [block] + [swap(block, "dp", r) for r in range(1, lax.axis_size("dp"))]
    blocks = []
    for part in near:
        blocks.append(part)
        for r in range(1, lax.axis_size("fsdp")):
            blocks.append(swap(part, "fsdp", r))
    return blocks


def scatter_shards(blocks):
    far = lax.axis_size("dp")
    wide = lax.axis_size("fsdp")
    parts = blocks.reshape((far, wide) + blocks.shape[1:])
    total = parts[:, 0]
    for r in range(1, wide):
        total = total + swap(parts[:, r].astype(jnp.bfloat16), "fsdp", r).astype(jnp.float32)
    mine = total[0]
    for r in range(1, far):
        mine = mine + swap(total[r].astype(jnp.bfloat16), "dp", r).astype(jnp.float32)
    return mine


def ctx_gather(block):
    count = lax.axis_size("ctx")
    found = {0: block}
    bit = count // 2
    while bit >= 1:
        for r in list(found):
            found[r | bit] = swap(found[r], "ctx", bit)
        bit //= 2
    return [found[r] for r in range(count)]


def ctx_scatter(rows):
    count = lax.axis_size("ctx")
    size = rows.shape[0] // count
    parts = {r: rows[r * size : (r + 1) * size] for r in range(count)}
    bit = 1
    while bit < count:
        parts = {
            r: parts[r]
            + swap(parts[r | bit].astype(jnp.bfloat16), "ctx", bit).astype(jnp.float32)
            for r in parts
            if not r & bit
        }
        bit *= 2
    return parts[0]


def reorder(array, index, axis):
    count = array.shape[axis]
    bit = 1
    while bit < count:
        shape = array.shape[:axis] + (count // (2 * bit), 2, bit) + array.shape[axis + 1 :]
        split = array.reshape(shape)
        first = lax.index_in_dim(split, 0, axis + 1, keepdims=True)
        second = lax.index_in_dim(split, 1, axis + 1, keepdims=True)
        flip = (index & bit) != 0
        split = jnp.concatenate(
            [jnp.where(flip, second, first), jnp.where(flip, first, second)], axis=axis + 1
        )
        array = split.reshape(array.shape)
        bit *= 2
    return array


def layer_stats(values):
    average = jnp.mean(values, axis=-1, keepdims=True)
    centred = values - average
    variance = jnp.mean(centred * centred, axis=-1, keepdims=True)
    inverse = lax.rsqrt(variance + epsilon)
    return (centred * inverse, inverse)


def layer_norm_back(grad_normed, normal, inverse, scale_gain):
    grad_scaled = grad_normed * scale_gain
    first_mean = jnp.mean(grad_scaled, axis=-1, keepdims=True)
    second_mean = jnp.mean(grad_scaled * normal, axis=-1, keepdims=True)
    return inverse * (grad_scaled - first_mean - normal * second_mean)


def rotary_tables(positions):
    half = ROT // 2
    freqs = 10000.0 ** (-jnp.arange(half, dtype=jnp.float32) * 2.0 / ROT)
    angles = positions.astype(jnp.float32)[:, None] * freqs[None, :]
    return (jnp.cos(angles)[:, None, :], jnp.sin(angles)[:, None, :])


def rotate(values, cosine, sine):
    half = ROT // 2
    first = values[..., :half]
    second = values[..., half:ROT]
    return jnp.concatenate(
        [first * cosine - second * sine, second * cosine + first * sine, values[..., ROT:]], axis=-1
    )


def mul(left, right):
    return jnp.dot(left, right, preferred_element_type=jnp.float32)


def contract_rows(left, right):
    return lax.dot_general(
        left, right, (((0,), (0,)), ((), ())), preferred_element_type=jnp.float32
    )


def contract_cols(left, right):
    return lax.dot_general(
        left, right, (((1,), (1,)), ((), ())), preferred_element_type=jnp.float32
    )


def pick(array, index, axis):
    return lax.dynamic_index_in_dim(array, index, axis, keepdims=False)


def body(
    tokens,
    segment_ids,
    cotangent,
    ln1_gain,
    ln1_bias,
    w_qkv,
    b_qkv,
    w_out,
    ln2_gain,
    ln2_bias,
    w_gate_up,
    w_down,
):
    rows = tokens.shape[1]
    count = lax.axis_size("ctx")
    ctx = lax.axis_index("ctx")
    shards = lax.axis_size("dp") * lax.axis_size("fsdp")
    shard = shard_index()
    length = rows * count
    depth = D // shards
    heads = H // count
    even = (H // shards) % count == 0

    if even:
        qkv_mine = pick(w_qkv.reshape(depth, 3, shards, count, -1), ctx, 3).reshape(depth, -1)
        out_mine = pick(w_out.reshape(count, -1, D), ctx, 0)
    else:
        qkv_mine = pick(w_qkv.reshape(depth, 3, count, -1), ctx, 2).reshape(depth, -1)
        out_mine = w_out
    gate_up_mine = pick(w_gate_up.reshape(depth, 2, shards, count, -1), ctx, 3).reshape(depth, -1)
    down_mine = pick(w_down.reshape(count, -1, D), ctx, 0)

    small = jnp.concatenate([ln1_gain, ln1_bias, ln2_gain, ln2_bias, b_qkv])
    small_all = reorder(jnp.stack(gather_shards(small)), shard, 0).astype(jnp.float32)
    gain_one = small_all[:, :depth].reshape(D)
    bias_one = small_all[:, depth : 2 * depth].reshape(D)
    gain_two = small_all[:, 2 * depth : 3 * depth].reshape(D)
    bias_two = small_all[:, 3 * depth : 4 * depth].reshape(D)
    qkv_bias = small_all[:, 4 * depth :].reshape(3 * D)
    if even:
        bias_mine = pick(qkv_bias.reshape(3, shards, count, -1), ctx, 2).reshape(-1)
    else:
        bias_mine = pick(qkv_bias.reshape(3, count, -1), ctx, 1).reshape(-1)

    token_rows = jnp.concatenate(ctx_gather(tokens[0]), axis=0)
    segments = jnp.concatenate(ctx_gather(segment_ids), axis=1)[0]
    positions = jnp.concatenate(
        [(ctx ^ r) * rows + jnp.arange(rows, dtype=jnp.int32) for r in range(count)]
    )
    cosine, sine = rotary_tables(positions)

    qkv_all = jnp.concatenate(gather_shards(qkv_mine), axis=0)
    out_all = jnp.stack(gather_shards(tie(out_mine, qkv_all)))
    out_all = reorder(out_all, shard, 0).reshape(-1, D)
    if not even:
        out_all = pick(out_all.reshape(count, -1, D), ctx, 0)
    gate_up_all = jnp.concatenate(gather_shards(tie(gate_up_mine, qkv_all)), axis=0)
    cot_rows = jnp.concatenate(ctx_gather(tie(cotangent[0], token_rows)), axis=0)
    down_all = jnp.stack(gather_shards(tie(down_mine, gate_up_all)))
    down_all = reorder(down_all, shard, 0).reshape(-1, D)

    def to_shard_order(array):
        n = array.shape[0]
        return reorder(array.reshape(n, shards, depth), shard, 1).reshape(n, D)

    normal_one, inverse_one = layer_stats(token_rows.astype(jnp.float32))
    normed_one = to_shard_order((normal_one * gain_one + bias_one).astype(jnp.bfloat16))
    projected = mul(normed_one, qkv_all) + bias_mine
    width = heads * E
    queries = rotate(projected[:, :width].reshape(length, heads, E), cosine, sine).astype(
        jnp.bfloat16
    )
    keys = rotate(projected[:, width : 2 * width].reshape(length, heads, E), cosine, sine).astype(
        jnp.bfloat16
    )
    values = projected[:, 2 * width :].reshape(length, heads, E).astype(jnp.bfloat16)
    allowed = (positions[None, :] <= positions[:, None]) & (segments[None, :] == segments[:, None])
    scores = jnp.einsum("qhe,khe->hqk", queries, keys, preferred_element_type=jnp.float32) * scale
    scores = jnp.where(allowed[None], scores, masked_score)
    top = jnp.max(scores, axis=-1, keepdims=True)
    weights = jnp.exp(scores - top)
    weights = weights / jnp.sum(weights, axis=-1, keepdims=True)
    low_weights = weights.astype(jnp.bfloat16)
    attended_f = jnp.einsum("hqk,khe->qhe", low_weights, values, preferred_element_type=jnp.float32)
    attended = attended_f.reshape(length, width).astype(jnp.bfloat16)

    hidden = tokens[0].astype(jnp.float32) + ctx_scatter(mul(attended, out_all))
    normal_two, inverse_two = layer_stats(hidden)
    normed_two = to_shard_order((normal_two * gain_two + bias_two).astype(jnp.bfloat16))
    normed_two = jnp.concatenate(ctx_gather(normed_two), axis=0)
    gate_up = mul(normed_two, gate_up_all)
    units = FF // count
    gate = gate_up[:, :units]
    upward = gate_up[:, units:]
    sigma = jax.nn.sigmoid(gate)
    swish = gate * sigma
    activ = (swish * upward).astype(jnp.bfloat16)
    mixed = hidden + ctx_scatter(mul(activ, down_all))

    grad_activ = contract_cols(cot_rows, down_all)
    grad_gate = grad_activ * upward * sigma * (1.0 + gate * (1.0 - sigma))
    grad_up = grad_activ * swish
    grad_gate_up = jnp.concatenate([grad_gate, grad_up], axis=1).astype(jnp.bfloat16)
    down_part = contract_rows(activ, cot_rows).reshape(shards, -1, D)
    down_grad = scatter_shards(reorder(down_part, shard, 0))
    gate_up_part = contract_rows(normed_two, grad_gate_up).reshape(shards, depth, 2 * units)
    gate_up_grad = scatter_shards(tie(gate_up_part, down_grad))

    grad_normed_two = ctx_scatter(contract_cols(grad_gate_up, gate_up_all))
    grad_normed_two = to_shard_order(grad_normed_two)
    gain_two_grad = jnp.sum(grad_normed_two * normal_two, axis=0)
    bias_two_grad = jnp.sum(grad_normed_two, axis=0)
    grad_hidden = cotangent[0].astype(jnp.float32) + layer_norm_back(
        grad_normed_two, normal_two, inverse_two, gain_two
    )
    grad_branch = jnp.concatenate(ctx_gather(grad_hidden.astype(jnp.bfloat16)), axis=0)

    grad_attended = contract_cols(grad_branch, out_all).astype(jnp.bfloat16)
    out_part = contract_rows(attended, grad_branch)
    grad_heads = grad_attended.reshape(length, heads, E)
    grad_weights = jnp.einsum("qhe,khe->hqk", grad_heads, values, preferred_element_type=jnp.float32)
    delta = jnp.sum(weights * grad_weights, axis=-1, keepdims=True)
    grad_scores = (weights * (grad_weights - delta)).astype(jnp.bfloat16)
    grad_queries = (
        jnp.einsum("hqk,khe->qhe", grad_scores, keys, preferred_element_type=jnp.float32) * scale
    )
    grad_keys = (
        jnp.einsum("hqk,qhe->khe", grad_scores, queries, preferred_element_type=jnp.float32) * scale
    )
    grad_values = jnp.einsum(
        "hqk,qhe->khe", low_weights, grad_heads, preferred_element_type=jnp.float32
    )
    grad_qkv = jnp.concatenate(
        [
            rotate(grad_queries, cosine, -sine).reshape(length, width),
            rotate(grad_keys, cosine, -sine).reshape(length, width),
            grad_values.reshape(length, width),
        ],
        axis=1,
    ).astype(jnp.bfloat16)
    qkv_bias_part = jnp.sum(grad_qkv.astype(jnp.float32), axis=0)
    qkv_part = contract_rows(normed_one, grad_qkv).reshape(shards, depth, 3 * width)

    grad_normed_one = to_shard_order(ctx_scatter(contract_cols(grad_qkv, qkv_all)))
    normal_mine = normal_one[:rows]
    gain_one_grad = jnp.sum(grad_normed_one * normal_mine, axis=0)
    bias_one_grad = jnp.sum(grad_normed_one, axis=0)
    input_grad = grad_hidden + layer_norm_back(
        grad_normed_one, normal_mine, inverse_one[:rows], gain_one
    )

    qkv_grad = scatter_shards(tie(qkv_part, gate_up_grad))

    def ctx_blocks(block):
        found = jnp.stack(ctx_gather(block.astype(jnp.bfloat16)))
        return reorder(found, ctx, 0).astype(jnp.float32)

    down_out = ctx_blocks(down_grad).reshape(-1, D)
    gate_up_out = ctx_blocks(gate_up_grad).reshape(count, depth, 2, shards, -1)
    gate_up_out = gate_up_out.transpose(1, 2, 3, 0, 4).reshape(depth, 2 * FF)
    if even:
        out_part = out_part.reshape(shards, -1, D)
        out_out = ctx_blocks(scatter_shards(reorder(out_part, shard, 0))).reshape(-1, D)
        qkv_out = ctx_blocks(qkv_grad).reshape(count, depth, 3, shards, -1)
        qkv_out = qkv_out.transpose(1, 2, 3, 0, 4).reshape(depth, 3 * D)
        qkv_bias_rows = ctx_blocks(qkv_bias_part).reshape(count, 3, shards, -1)
        qkv_bias_rows = qkv_bias_rows.transpose(1, 2, 0, 3).reshape(shards, -1)
    else:
        spread = jnp.zeros((count,) + out_part.shape, jnp.float32)
        spread = lax.dynamic_update_index_in_dim(spread, out_part, ctx, 0)
        out_part = spread.reshape(shards, depth, D)
        out_out = scatter_shards(reorder(out_part, shard, 0))
        out_out = lax.psum(out_out.astype(jnp.bfloat16), "ctx").astype(jnp.float32)
        qkv_out = ctx_blocks(qkv_grad).reshape(count, depth, 3, -1)
        qkv_out = qkv_out.transpose(1, 2, 0, 3).reshape(depth, 3 * D)
        qkv_bias_rows = ctx_blocks(qkv_bias_part).reshape(count, 3, -1)
        qkv_bias_rows = qkv_bias_rows.transpose(1, 0, 2).reshape(shards, -1)

    norm_parts = jnp.concatenate(
        [
            part.reshape(shards, depth)
            for part in (gain_one_grad, bias_one_grad, gain_two_grad, bias_two_grad)
        ],
        axis=1,
    )
    bit = 1
    while bit < count:
        norm_parts = norm_parts + swap(norm_parts, "ctx", bit)
        bit *= 2
    small_parts = jnp.concatenate([norm_parts, qkv_bias_rows], axis=1)
    small_grad = scatter_shards(reorder(small_parts, shard, 0))

    return (
        mixed.astype(jnp.bfloat16)[None],
        input_grad[None],
        small_grad[:depth],
        small_grad[depth : 2 * depth],
        qkv_out,
        small_grad[4 * depth :],
        out_out,
        small_grad[2 * depth : 3 * depth],
        small_grad[3 * depth : 4 * depth],
        gate_up_out,
        down_out,
    )


def call(kernel, grid, in_specs, out_specs, out_shape, scratch=(), limit=48, after=(), aliases=()):
    inputs = len(in_specs)

    def body_of(places_ref, *refs):
        kernel(places_ref, *refs[:inputs], *refs[inputs + len(after) :])

    run = pl.pallas_call(
        body_of,
        grid_spec=pltpu.PrefetchScalarGridSpec(
            num_scalar_prefetch=1,
            grid=grid,
            in_specs=in_specs + [anywhere()] * len(after),
            out_specs=out_specs,
            scratch_shapes=list(scratch),
        ),
        out_shape=out_shape,
        input_output_aliases=dict(aliases),
        compiler_params=pltpu.CompilerParams(vmem_limit_bytes=limit * 1024 * 1024),
        cost_estimate=pl.CostEstimate(flops=1, bytes_accessed=1, transcendentals=0),
    )
    return lambda *operands: run(*operands, *after)


def anywhere():
    return pl.BlockSpec(memory_space=pl.ANY)


def hold(places, value, *after):
    def kernel(places_ref, value_ref, o_ref):
        pass

    return call(
        kernel,
        (1,),
        [anywhere()],
        anywhere(),
        sds(value.shape, value.dtype),
        limit=1,
        after=after,
        aliases=((1, 0),),
    )(places, value)


def sds(shape, dtype):
    return jax.ShapeDtypeStruct(shape, dtype)


def whole(array):
    zeros = (0,) * array.ndim
    return pl.BlockSpec(array.shape, lambda *_: zeros)


def quarters(shape):
    if shape[0] % 64 == 0:
        return (shape[0] // 4, shape[1]), lambda m: (m, 0)
    return (shape[0], shape[1] // 4), lambda m: (0, m)


def add(places, terms, after=()):
    shape = terms[0][0].shape[len(terms[0][1]) :]
    steps = 4 if shape[0] % 64 == 0 else 1
    tile = shape[0] // steps

    def spec(at):
        return pl.BlockSpec((None,) * len(at) + (tile, shape[1]), lambda m, _: at + (m, 0))

    def kernel(places_ref, *refs):
        total = refs[0][...].astype(jnp.float32)
        for ref in refs[1:-1]:
            total = total + ref[...].astype(jnp.float32)
        refs[-1][...] = total.astype(jnp.bfloat16)

    return call(
        kernel,
        (steps,),
        [spec(at) for _, at in terms],
        spec(()),
        sds(shape, jnp.bfloat16),
        after=after,
    )(places, *[array for array, _ in terms])


def contract(left, right):
    return lax.dot_general(
        left, right, (((0,), (0,)), ((), ())), preferred_element_type=jnp.float32
    )


def take_columns(places, w, count, shards, groups, copies, pad, after=()):
    depth = w.shape[0]
    each = w.shape[1] // groups
    unit = each // (shards * count)
    tile = depth // 4

    def kernel(places_ref, w_ref, o_ref):
        for i in range(count):

            @pl.when(places_ref[0] == i)
            def _():
                block = jnp.concatenate(
                    [
                        w_ref[:, (s * count + i) * unit : (s * count + i + 1) * unit]
                        for s in range(shards)
                    ],
                    axis=1,
                )
                for copy in range(copies):
                    o_ref[copy] = block

    return call(
        kernel,
        (groups, 4),
        [pl.BlockSpec((tile, each), lambda g, m, _: (m, g))],
        pl.BlockSpec((copies, tile, each // count), lambda g, m, _: (0, m, g)),
        sds((copies, depth + pad, w.shape[1] // count), jnp.bfloat16),
        after=after,
    )(places, w)


def take_pairs(places, w, count, shards, after=()):
    depth = w.shape[0]
    each = w.shape[1] // 2
    unit = each // (shards * count)
    tile = depth // 4

    def kernel(places_ref, gate_ref, up_ref, o_ref):
        for i in range(count):

            @pl.when(places_ref[0] == i)
            def _():
                for part, ref in enumerate((gate_ref, up_ref)):
                    block = jnp.concatenate(
                        [
                            ref[:, (s * count + i) * unit : (s * count + i + 1) * unit]
                            for s in range(shards)
                        ],
                        axis=1,
                    )
                    for n in range(each // count // 128):
                        at = (2 * n + part) * 128
                        o_ref[:, at : at + 128] = block[:, n * 128 : (n + 1) * 128]

    return call(
        kernel,
        (4,),
        [
            pl.BlockSpec((tile, each), lambda m, _: (m, 0)),
            pl.BlockSpec((tile, each), lambda m, _: (m, 1)),
        ],
        pl.BlockSpec((tile, 2 * each // count), lambda m, _: (m, 0)),
        sds((depth, 2 * each // count), jnp.bfloat16),
        after=after,
    )(places, w, w)


def interleave(blocks, shards):
    unit = blocks[0].shape[1] // shards
    return [
        jnp.concatenate([block[:, s * unit : (s + 1) * unit] for block in blocks], axis=1)
        for s in range(shards)
    ]


def spread_pairs(places, gathered, count, shards, after=()):
    depth = gathered.shape[0] // count
    width = gathered.shape[1]
    each = width // 2
    unit = each // shards * count
    tile = depth // 8

    def kernel(places_ref, x_ref, o_ref):
        for part in range(2):
            blocks = []
            for i in range(count):
                tiles = [
                    x_ref[i][:, (2 * n + part) * 128 : (2 * n + part + 1) * 128]
                    for n in range(each // 128)
                ]
                blocks.append(jnp.concatenate(tiles, axis=1).astype(jnp.float32))
            for s, block in enumerate(interleave(blocks, shards)):
                at = part * each * count + s * unit
                o_ref[:, at : at + unit] = block

    return call(
        kernel,
        (8,),
        [pl.BlockSpec((count, tile, width), lambda m, _: (0, m, 0))],
        pl.BlockSpec((tile, width * count), lambda m, _: (m, 0)),
        sds((depth, width * count), jnp.float32),
        after=after,
    )(places, gathered.reshape(count, depth, width))


def spread_columns(places, pieces, count, shards, after=()):
    groups = len(pieces)
    depth, each = pieces[0][0].shape
    unit = each // shards * count
    tile = depth // 4
    flat = [piece for group in pieces for piece in group]

    def kernel(places_ref, *refs):
        o_ref = refs[-1]
        for g in range(groups):
            values = [refs[g * count + p][...].astype(jnp.float32) for p in range(count)]
            blocks = []
            for i in range(count):
                block = values[0]
                for p in range(1, count):
                    block = jnp.where(places_ref[1 + i] == p, values[p], block)
                blocks.append(block)
            for s, block in enumerate(interleave(blocks, shards)):
                at = g * each * count + s * unit
                o_ref[:, at : at + unit] = block

    spec = pl.BlockSpec((tile, each), lambda m, _: (m, 0))
    return call(
        kernel,
        (4,),
        [spec] * len(flat),
        pl.BlockSpec((tile, groups * each * count), lambda m, _: (m, 0)),
        sds((depth, groups * each * count), jnp.float32),
        after=after,
    )(places, *flat)


def norm_stats(values):
    average = jnp.mean(values, axis=-1, keepdims=True)
    centred = values - average
    inverse = lax.rsqrt(jnp.mean(centred * centred, axis=-1, keepdims=True) + epsilon)
    return centred * inverse, inverse


def norm_tokens(places, tokens, gain, bias, count, after=()):
    length = tokens.shape[0]
    tile = length // count // 2
    shards, depth = gain.shape

    def kernel(places_ref, x_ref, gain_ref, bias_ref, o_ref, plain_ref):
        plain_ref[...], _ = norm_stats(x_ref[...].astype(jnp.float32))
        for r in range(shards):
            start = pl.multiple_of(places_ref[1 + count + r] * depth, depth)
            block = plain_ref[:, pl.ds(start, depth)]
            o_ref[:, r * depth : (r + 1) * depth] = (
                block * gain_ref[r : r + 1] + bias_ref[r : r + 1]
            ).astype(jnp.bfloat16)

    return call(
        kernel,
        (count, 2),
        [
            pl.BlockSpec((tile, D), lambda b, h, p: (p[1 + b] * 2 + h, 0)),
            whole(gain),
            whole(bias),
        ],
        pl.BlockSpec((tile, D), lambda b, h, _: (b * 2 + h, 0)),
        sds((length, D), jnp.bfloat16),
        [pltpu.VMEM((tile, D), jnp.float32)],
        after=after,
    )(places, tokens, gain, bias)


def norm_hidden(places, tokens, pieces, gain, bias, after=()):
    rows = tokens.shape[0]
    tile = rows // 4

    def kernel(places_ref, x_ref, *refs):
        gain_ref, bias_ref, hidden_ref, o_ref = refs[-4:]
        hidden = x_ref[...].astype(jnp.float32)
        for ref in refs[:-4]:
            hidden = hidden + ref[...].astype(jnp.float32)
        hidden_ref[...] = hidden
        normal, _ = norm_stats(hidden)
        o_ref[...] = (normal * gain_ref[...] + bias_ref[...]).astype(jnp.bfloat16)

    spec = pl.BlockSpec((tile, D), lambda m, _: (m, 0))
    return call(
        kernel,
        (4,),
        [spec] * (1 + len(pieces)) + [whole(gain), whole(bias)],
        [spec, spec],
        [sds((rows, D), jnp.float32), sds((rows, D), jnp.bfloat16)],
        after=after,
    )(places, tokens, *pieces, gain, bias)


def norm_back(places, source, pieces, gain, added, first, low, after=()):
    rows = source.shape[0]
    tile = rows // 4
    shards, depth = gain.shape

    def kernel(places_ref, x_ref, added_ref, gain_ref, *refs):
        piece_refs = refs[: len(pieces)]
        out_refs = refs[len(pieces) : -2]
        sums_ref = out_refs[-1]
        grad_ref, gain_plain = refs[-2:]
        for r in range(shards):
            start = pl.multiple_of(places_ref[first + r] * depth, depth) if shards > 1 else 0
            at = slice(r * depth, (r + 1) * depth)
            block = piece_refs[0][:, at].astype(jnp.float32)
            for ref in piece_refs[1:]:
                block = block + ref[:, at].astype(jnp.float32)
            grad_ref[:, pl.ds(start, depth)] = block
            gain_plain[:, pl.ds(start, depth)] = jnp.broadcast_to(gain_ref[r : r + 1], (8, depth))
        normal, inverse = norm_stats(x_ref[...].astype(jnp.float32))
        grad = grad_ref[...]

        @pl.when(pl.program_id(0) == 0)
        def _():
            sums_ref[...] = jnp.zeros_like(sums_ref)

        sums_ref[0:1] += jnp.sum(grad * normal, axis=0, keepdims=True)
        sums_ref[1:2] += jnp.sum(grad, axis=0, keepdims=True)
        scaled = grad * gain_plain[0:1]
        mean = jnp.mean(scaled, axis=-1, keepdims=True)
        second = jnp.mean(scaled * normal, axis=-1, keepdims=True)
        total = added_ref[...].astype(jnp.float32) + inverse * (scaled - mean - normal * second)
        out_refs[0][...] = total
        if low:
            out_refs[1][...] = total.astype(jnp.bfloat16)

    spec = pl.BlockSpec((tile, D), lambda m, _: (m, 0))
    sums = pl.BlockSpec((2, D), lambda m, _: (0, 0))
    return call(
        kernel,
        (4,),
        [spec, spec, whole(gain)] + [spec] * len(pieces),
        [spec] + [spec] * low + [sums],
        [sds((rows, D), jnp.float32)]
        + [sds((rows, D), jnp.bfloat16)] * low
        + [sds((2, D), jnp.float32)],
        [pltpu.VMEM((tile, D), jnp.float32), pltpu.VMEM((8, D), jnp.float32)],
        after=after,
    )(places, source, added, gain, *pieces)


def project(places, normed, near, far, group, bias, tables, after=()):
    length = normed.shape[0]
    width = bias.shape[1]
    tile = min(width, 256)
    blocks = near.shape[0]
    depth = D // blocks // 2

    def kernel(places_ref, x_ref, near_ref, far_ref, bias_ref, *refs):
        o_ref = refs[-1]
        total = bias_ref[...]
        for i, ref in enumerate((near_ref, far_ref)):
            weight = ref[...].reshape(D // 2, tile)
            left = x_ref[:, i * (D // 2) : (i + 1) * (D // 2)]
            total = total + jnp.dot(left, weight, preferred_element_type=jnp.float32)
        if tables:
            cosine, low, high = (
                jnp.concatenate([ref[...]] * (tile // 128), axis=1) for ref in refs[:3]
            )
            total = (
                total * cosine
                + pltpu.roll(total, tile - ROT // 2, 1) * low
                + pltpu.roll(total, ROT // 2, 1) * high
            )
        o_ref[...] = total.astype(jnp.bfloat16)

    steps = width // tile
    weight = pl.BlockSpec((blocks, depth, tile), lambda n, _: (0, 0, group * steps + n))
    return call(
        kernel,
        (steps,),
        [whole(normed), weight, weight, pl.BlockSpec((1, tile), lambda n, _: (0, n))]
        + [whole(table) for table in tables],
        pl.BlockSpec((length, tile), lambda n, _: (0, n)),
        sds((length, width), jnp.bfloat16),
        after=after,
    )(places, normed, near, far, bias, *tables)


def head_lanes(values, head):
    lanes = lax.broadcasted_iota(jnp.int32, values.shape, 1)
    return jnp.where((lanes >= head * E) & (lanes < (head + 1) * E), values, jnp.zeros_like(values))


def to_plain_rows(places_ref, source_ref, target_ref, count):
    rows = target_ref.shape[0] // count
    for b in range(count):
        start = pl.multiple_of(places_ref[1 + b] * rows, rows)
        target_ref[b * rows : (b + 1) * rows] = source_ref[pl.ds(start, rows)]


def masked(shape, keys_seg, query_seg, first):
    ks = lax.broadcasted_iota(jnp.int32, shape, 0)
    qs = lax.broadcasted_iota(jnp.int32, shape, 1) + first
    return (ks <= qs) & (keys_seg == query_seg)


def attend(places, qkv, seg_col, seg_row, count, heads, after=()):
    length = qkv[0].shape[0]
    pairs = heads // 2
    step = math.gcd(length, 256)
    rows = length // count

    def kernel(places_ref, q_ref, k_ref, v_ref, col_ref, row_ref, o_ref, log_ref, vt, os):
        vt[...] = jnp.transpose(v_ref[...].astype(jnp.float32)).astype(jnp.bfloat16)
        for a in range(length // step):
            n = (a + 1) * step
            halves = []
            allowed = masked((n, step), col_ref[0:n], row_ref[:, a * step : n], a * step)
            for h in range(2):
                query = head_lanes(q_ref[a * step : n], h) * scale
                scores = lax.dot_general(
                    k_ref[0:n], query, (((1,), (1,)), ((), ())), preferred_element_type=jnp.float32
                )
                scores = jnp.where(allowed, scores, masked_score)
                top = jnp.max(scores, axis=0, keepdims=True)
                weights = jnp.exp(scores - top)
                total = jnp.sum(weights, axis=0, keepdims=True)
                out = jnp.dot(
                    vt[h * E : (h + 1) * E, 0:n],
                    weights.astype(jnp.bfloat16),
                    preferred_element_type=jnp.float32,
                )
                halves.append(out / total)
                log_ref[0, h : h + 1, a * step : n] = top + jnp.log(total)
            os[a * step : n] = jnp.transpose(jnp.concatenate(halves, axis=0)).astype(jnp.bfloat16)
        for b in range(count):
            start = pl.multiple_of(places_ref[1 + b] * rows, rows)
            o_ref[pl.ds(start, rows)] = os[b * rows : (b + 1) * rows]

    def columns(group):
        return pl.BlockSpec((length, 128), lambda p, _: (0, group * pairs + p))

    scratch = pltpu.VMEM((length, 128), jnp.bfloat16)
    return call(
        kernel,
        (pairs,),
        [columns(0), columns(0), columns(0), whole(seg_col), whole(seg_row)],
        [columns(0), pl.BlockSpec((1, 2, length), lambda p, _: (p, 0, 0))],
        [
            sds((length, heads * E), jnp.bfloat16),
            sds((pairs, 2, length), jnp.float32),
        ],
        [pltpu.VMEM((128, length), jnp.bfloat16), scratch],
        after=after,
    )(places, *qkv, seg_col, seg_row)


def attend_back(
    places, qkv, grad_attended, logs, seg_col, seg_row, tables, count, heads, after=()
):
    length = qkv[0].shape[0]
    pairs = heads // 2
    step = math.gcd(length, 256)
    rows = length // count

    def kernel(
        places_ref,
        q_ref,
        k_ref,
        v_ref,
        g_ref,
        log_ref,
        col_ref,
        row_ref,
        cos_ref,
        low_ref,
        high_ref,
        dq_ref,
        dk_ref,
        dv_ref,
        sums_ref,
        gs,
        kt,
        dq,
        dk,
        dv,
    ):
        to_plain_rows(places_ref, g_ref, gs, count)
        kt[...] = jnp.transpose(k_ref[...].astype(jnp.float32)).astype(jnp.bfloat16)
        dk[...] = jnp.zeros_like(dk)
        dv[...] = jnp.zeros_like(dv)
        for a in range(length // step):
            n = (a + 1) * step
            halves = []
            allowed = masked((n, step), col_ref[0:n], row_ref[:, a * step : n], a * step)
            for h in range(2):
                query = head_lanes(q_ref[a * step : n], h) * scale
                grad = head_lanes(gs[a * step : n], h)
                scores = lax.dot_general(
                    k_ref[0:n], query, (((1,), (1,)), ((), ())), preferred_element_type=jnp.float32
                )
                log = log_ref[0, h : h + 1, a * step : n]
                weights = jnp.exp(jnp.where(allowed, scores - log, masked_score))
                grad_weights = lax.dot_general(
                    v_ref[0:n], grad, (((1,), (1,)), ((), ())), preferred_element_type=jnp.float32
                )
                product = weights * grad_weights
                delta = jnp.sum(product, axis=0, keepdims=True)
                grad_scores = (product - weights * delta).astype(jnp.bfloat16)
                dv[0:n] += jnp.dot(
                    weights.astype(jnp.bfloat16), grad, preferred_element_type=jnp.float32
                )
                dk[0:n] += jnp.dot(grad_scores, query, preferred_element_type=jnp.float32)
                halves.append(
                    jnp.dot(
                        kt[h * E : (h + 1) * E, 0:n],
                        grad_scores,
                        preferred_element_type=jnp.float32,
                    )
                )
            dq[a * step : n] = jnp.transpose(jnp.concatenate(halves, axis=0))

        sums = [jnp.zeros((1, 128), jnp.float32)] * 3
        for b in range(count):
            at = slice(b * rows, (b + 1) * rows)
            cosine, low, high = cos_ref[at], low_ref[at], high_ref[at]
            for i, (part, out_ref) in enumerate(((dq, dq_ref), (dk, dk_ref), (dv, dv_ref))):
                block = part[at]
                if i == 0:
                    block = block * scale
                if i < 2:
                    block = (
                        block * cosine
                        - pltpu.roll(block, 128 - ROT // 2, 1) * low
                        - pltpu.roll(block, ROT // 2, 1) * high
                    )
                block = block.astype(jnp.bfloat16)
                sums[i] = sums[i] + jnp.sum(block.astype(jnp.float32), axis=0, keepdims=True)
                out_ref[at] = block
        for i in range(3):
            sums_ref[i] = sums[i]

    def columns(group):
        return pl.BlockSpec((length, 128), lambda p, _: (0, group * pairs + p))

    low_scratch = pltpu.VMEM((length, 128), jnp.bfloat16)
    scratch = pltpu.VMEM((length, 128), jnp.float32)
    width = heads * E
    return call(
        kernel,
        (pairs,),
        [
            columns(0),
            columns(0),
            columns(0),
            columns(0),
            pl.BlockSpec((1, 2, length), lambda p, _: (p, 0, 0)),
            whole(seg_col),
            whole(seg_row),
            whole(tables[0]),
            whole(tables[1]),
            whole(tables[2]),
        ],
        [columns(0)] * 3 + [pl.BlockSpec((3, 1, 128), lambda p, _: (0, 0, p))],
        [sds((length, width), jnp.bfloat16)] * 3 + [sds((3, 1, width), jnp.float32)],
        [low_scratch]
        + [pltpu.VMEM((128, length), jnp.bfloat16), scratch, scratch, scratch],
        after=after,
    )(places, *qkv, grad_attended, logs, seg_col, seg_row, *tables)


def join_rows(places_ref, first, refs, joined):
    halves = len(refs) // 2
    width = refs[0].shape[-1]
    for at, ref in enumerate(refs):
        blocks, size, _ = ref.shape
        columns = slice(at % halves * width, (at % halves + 1) * width)
        for i in range(blocks):
            place = places_ref[first + at // halves * blocks + i]
            joined[pl.ds(pl.multiple_of(place * size, size), size), columns] = ref[i]


def row_product(places, left, parts, count, after=()):
    length, depth = left.shape
    tile = D // 4

    def kernel(places_ref, x_ref, *refs):
        near_ref, far_ref, joined = refs[-3:]

        @pl.when(pl.program_id(0) == 0)
        def _():
            join_rows(places_ref, 1 + count, refs[:-3], joined)

        start = pl.multiple_of(pl.program_id(0) * tile, tile)
        total = jnp.dot(
            x_ref[...], joined[:, pl.ds(start, tile)], preferred_element_type=jnp.float32
        ).astype(jnp.bfloat16)
        near_ref[...] = total[: length // 2]
        far_ref[...] = total[length // 2 :]

    spec = pl.BlockSpec((length // 2, tile), lambda n, _: (0, n))
    shape = sds((length // 2, D), jnp.bfloat16)
    return call(
        kernel,
        (4,),
        [whole(left)] + [whole(part) for part in parts],
        [spec, spec],
        [shape, shape],
        [pltpu.VMEM((depth, D), jnp.bfloat16)],
        after=after,
    )(places, left, *parts)


def grad_out(places, pieces, near, far, count, after=()):
    rows = pieces[0].shape[0]
    width = near.shape[0] * near.shape[1] * 2
    tile = rows

    def kernel(places_ref, *refs):
        piece_refs = refs[:count]
        a_ref, b_ref, o_ref, all_ref, joined = refs[count:]

        @pl.when(pl.program_id(0) == 0)
        def _():
            join_rows(places_ref, 1 + count, (a_ref, b_ref), joined)

        for p, ref in enumerate(piece_refs):

            @pl.when(pl.program_id(0) == p)
            def _():
                all_ref[...] = ref[...]
                o_ref[...] = lax.dot_general(
                    ref[...],
                    joined[...],
                    (((1,), (1,)), ((), ())),
                    preferred_element_type=jnp.float32,
                ).astype(jnp.bfloat16)

    return call(
        kernel,
        (count,),
        [whole(piece) for piece in pieces] + [whole(near), whole(far)],
        [
            pl.BlockSpec((tile, width), lambda m, _: (m, 0)),
            pl.BlockSpec((tile, D), lambda m, _: (m, 0)),
        ],
        [sds((rows * count, width), jnp.bfloat16), sds((rows * count, D), jnp.bfloat16)],
        [pltpu.VMEM((width, D), jnp.bfloat16)],
        after=after,
    )(places, *pieces, near, far)


def gate_product(places, pieces, weight, after=()):
    rows = pieces[0].shape[0]
    length = rows * len(pieces)
    width = weight.shape[1]

    def kernel(places_ref, *refs):
        *piece_refs, w_ref, all_ref, both_ref, activ_ref = refs

        @pl.when(pl.program_id(0) == 0)
        def _():
            for p, ref in enumerate(piece_refs):
                all_ref[p * rows : (p + 1) * rows] = ref[...]

        both = jnp.dot(all_ref[...], w_ref[...], preferred_element_type=jnp.float32)
        gate = both[:, :128]
        both_ref[...] = both.astype(jnp.bfloat16)
        activ_ref[...] = (gate * jax.nn.sigmoid(gate) * both[:, 128:]).astype(jnp.bfloat16)

    return call(
        kernel,
        (width // 256,),
        [whole(piece) for piece in pieces] + [pl.BlockSpec((D, 256), lambda n, _: (0, n))],
        [
            pl.BlockSpec((length, D), lambda n, _: (0, 0)),
            pl.BlockSpec((length, 256), lambda n, _: (0, n)),
            pl.BlockSpec((length, 128), lambda n, _: (0, n)),
        ],
        [
            sds((length, D), jnp.bfloat16),
            sds((length, width), jnp.bfloat16),
            sds((length, width // 2), jnp.bfloat16),
        ],
        limit=56,
        after=after,
    )(places, *pieces, weight)


def gate_back(places, cotangent, parts, both, count, after=()):
    length, width = both.shape
    units = width // 2
    steps = -(-units // 256)

    def kernel(places_ref, x_ref, both_ref, *refs):
        o_ref, joined = refs[-2:]

        @pl.when(pl.program_id(0) == 0)
        def _():
            join_rows(places_ref, 1 + count, refs[:-2], joined)

        start = pl.multiple_of(pl.program_id(0) * 256, 256)
        grad = lax.dot_general(
            x_ref[...],
            joined[pl.ds(start, 256)],
            (((1,), (1,)), ((), ())),
            preferred_element_type=jnp.float32,
        )
        for i in range(2):
            part = grad[:, i * 128 : (i + 1) * 128]
            gate = both_ref[:, i * 256 : i * 256 + 128].astype(jnp.float32)
            upward = both_ref[:, i * 256 + 128 : (i + 1) * 256].astype(jnp.float32)
            sigma = jax.nn.sigmoid(gate)
            grad_gate = part * upward * sigma * (1.0 + gate * (1.0 - sigma))
            o_ref[:, i * 256 : i * 256 + 128] = grad_gate.astype(jnp.bfloat16)
            o_ref[:, i * 256 + 128 : (i + 1) * 256] = (part * (gate * sigma)).astype(jnp.bfloat16)

    spec = pl.BlockSpec((length, 512), lambda n, _: (0, n))
    return call(
        kernel,
        (steps,),
        [whole(cotangent), spec] + [whole(part) for part in parts],
        spec,
        sds((length, width), jnp.bfloat16),
        [pltpu.VMEM((steps * 256, D), jnp.bfloat16)],
        limit=56,
        after=after,
    )(places, cotangent, both, *parts)


def normed_grad(places, left, weight, after=()):
    length, width = left.shape

    def kernel(places_ref, x_ref, w_ref, near_ref, far_ref):
        total = lax.dot_general(
            x_ref[...], w_ref[...], (((1,), (1,)), ((), ())), preferred_element_type=jnp.float32
        ).astype(jnp.bfloat16)
        near_ref[...] = total[: length // 2]
        far_ref[...] = total[length // 2 :]

    spec = pl.BlockSpec((length // 2, 256), lambda n, _: (0, n))
    shape = sds((length // 2, D), jnp.bfloat16)
    return call(
        kernel,
        (D // 256,),
        [whole(left), pl.BlockSpec((256, width), lambda n, _: (n, 0))],
        [spec, spec],
        [shape, shape],
        limit=56,
        after=after,
    )(places, left, weight)


def normed_grad_parts(places, lefts, parts, count, after=()):
    length, width = lefts[0].shape
    rows = length // count
    blocks = parts[0].shape[0]
    depth = D // blocks // 2
    total_width = width * len(lefts)

    def kernel(places_ref, *refs):
        left_refs = refs[: len(lefts)]
        near_part, far_part, near_ref, far_ref, joined = refs[len(lefts) :]

        @pl.when(pl.program_id(0) == 0)
        def _():
            for b in range(count):
                start = pl.multiple_of(places_ref[1 + b] * rows, rows)
                for i, ref in enumerate(left_refs):
                    joined[pl.ds(start, rows), i * width : (i + 1) * width] = ref[
                        b * rows : (b + 1) * rows
                    ]

        def run(weight_ref):
            total = lax.dot_general(
                joined[...], weight_ref[0], (((1,), (1,)), ((), ())), preferred_element_type=jnp.float32
            ).astype(jnp.bfloat16)
            near_ref[...] = total[: length // 2]
            far_ref[...] = total[length // 2 :]

        @pl.when(pl.program_id(0) < blocks)
        def _():
            run(near_part)

        @pl.when(pl.program_id(0) >= blocks)
        def _():
            run(far_part)

    near_spec = pl.BlockSpec(
        (1, depth, total_width), lambda n, _: (jnp.minimum(n, blocks - 1), 0, 0)
    )
    far_spec = pl.BlockSpec(
        (1, depth, total_width), lambda n, _: (jnp.maximum(n - blocks, 0), 0, 0)
    )
    spec = pl.BlockSpec((length // 2, depth), lambda n, _: (0, n))
    shape = sds((length // 2, D), jnp.bfloat16)
    return call(
        kernel,
        (2 * blocks,),
        [whole(left) for left in lefts] + [near_spec, far_spec],
        [spec, spec],
        [shape, shape],
        [pltpu.VMEM((length, total_width), jnp.bfloat16)],
        after=after,
    )(places, *lefts, *parts)


def turn(source_ref, first, columns, target_ref):
    step = math.gcd(columns, 256)
    for at in range(0, columns, step):
        block = source_ref[:, first + at : first + at + step].astype(jnp.float32)
        target_ref[at : at + step] = jnp.transpose(block).astype(jnp.bfloat16)


def pairs_grad(places, normed, right, after=()):
    length, width = right.shape

    def kernel(places_ref, x_ref, g_ref, o_ref, turned):
        @pl.when(pl.program_id(0) == 0)
        def _():
            turn(x_ref, 0, D, turned)

        o_ref[...] = jnp.dot(
            turned[...], g_ref[...], preferred_element_type=jnp.float32
        ).astype(jnp.bfloat16)

    return call(
        kernel,
        (width // 256,),
        [whole(normed), pl.BlockSpec((length, 256), lambda n, _: (0, n))],
        pl.BlockSpec((D, 256), lambda n, _: (0, n)),
        sds((D, width), jnp.bfloat16),
        [pltpu.VMEM((D, length), jnp.bfloat16)],
        after=after,
    )(places, normed, right)


def column_loads(places, normed, rights, after=()):
    length, width = rights[0].shape
    count = len(rights)
    rows = D // 2

    def kernel(places_ref, x_ref, *refs):
        right_refs, out_refs = refs[:count], refs[count : 2 * count]
        turned_ref, turned = refs[2 * count :]
        step = pl.program_id(0)

        @pl.when(step == 0)
        def _():
            turn(x_ref, rows, rows, turned)

        for i in range(count):

            @pl.when(step == i)
            def _():
                out_refs[i][...] = jnp.dot(
                    turned[...], right_refs[i][...], preferred_element_type=jnp.float32
                ).astype(jnp.bfloat16)

        @pl.when(step == count - 1)
        def _():
            turn(x_ref, 0, rows, turned_ref)

    shape = sds((rows, width), jnp.bfloat16)
    own = sds((rows, length), jnp.bfloat16)
    return call(
        kernel,
        (count,),
        [whole(normed)] + [whole(right) for right in rights],
        [whole(shape)] * count + [whole(own)],
        [shape] * count + [own],
        [pltpu.VMEM((rows, length), jnp.bfloat16)],
        after=after,
    )(places, normed, *rights)


def column_keep(places, turned, right, arrived, after=()):
    rows, length = turned.shape
    width = right.shape[1]
    tile = width // 2

    def kernel(places_ref, x_ref, g_ref, arrived_ref, o_ref):
        total = jnp.dot(x_ref[...], g_ref[...], preferred_element_type=jnp.float32)
        o_ref[...] = (total + arrived_ref[...].astype(jnp.float32)).astype(jnp.bfloat16)

    spec = pl.BlockSpec((rows, tile), lambda n, _: (0, n))
    return call(
        kernel,
        (2,),
        [whole(turned), pl.BlockSpec((length, tile), lambda n, _: (0, n)), spec],
        spec,
        sds((rows, width), jnp.bfloat16),
        after=after,
    )(places, turned, right, arrived)


def row_grad(places, left, right, size, count, stacked, after=()):
    length, width = left.shape
    tile = D // 4
    blocks = width // size // 2

    def kernel(places_ref, x_ref, g_ref, *refs):
        total_ref = refs[-1]
        total_ref[...] = contract(x_ref[...], g_ref[...])
        halves = 1 if stacked else 2
        for half in range(halves):

            @pl.when(pl.program_id(0) // 2 == half if halves > 1 else pl.program_id(0) >= 0)
            def _():
                for side in range(2):
                    for r in range(blocks):
                        place = places_ref[1 + count + side * blocks + r]
                        start = pl.multiple_of(place * size, size)
                        block = total_ref[pl.ds(start, size)].astype(jnp.bfloat16)
                        refs[side * halves + half][r] = block

    block = (blocks, size, tile)
    if stacked:
        specs = [pl.BlockSpec(block, lambda n, _: (0, n, 0))] * 2
        shapes = [sds((blocks, 4 * size, tile), jnp.bfloat16)] * 2
    else:
        first = pl.BlockSpec(block, lambda n, _: (0, 0, jnp.minimum(n, 1)))
        second = pl.BlockSpec(block, lambda n, _: (0, 0, jnp.maximum(n - 2, 0)))
        specs = [first, second] * 2
        shapes = [sds((blocks, size, D // 2), jnp.bfloat16)] * 4
    return call(
        kernel,
        (4,),
        [whole(left), pl.BlockSpec((length, tile), lambda n, _: (0, n))],
        specs,
        shapes,
        [pltpu.VMEM((width, tile), jnp.float32)],
        after=after,
    )(places, left, right)


def to_line(blocks):
    return lax.all_to_all(blocks, "dp", split_axis=0, concat_axis=0)


def rows_gather(own):
    pieces = [own]
    bit = lax.axis_size("ctx") // 2
    while bit >= 1:
        pieces = pieces + [swap(piece, "ctx", bit) for piece in pieces]
        bit //= 2
    return pieces


def rows_scatter(places, near, far, after=()):
    count = lax.axis_size("ctx")
    pieces = [near, swap(far, "ctx", 1)]
    bit = 2
    while bit < count:
        pieces = [piece.reshape(2, -1, D) for piece in pieces]
        load = add(places, [(piece, (1,)) for piece in pieces], after if 2 * bit == count else ())
        pieces = [piece[0] for piece in pieces] if 2 * bit < count else [
            piece.reshape(-1, D) for piece in pieces
        ]
        pieces.append(swap(load, "ctx", bit))
        bit *= 2
    return pieces


def fast_body(
    tokens,
    segment_ids,
    cotangent,
    ln1_gain,
    ln1_bias,
    w_qkv,
    b_qkv,
    w_out,
    ln2_gain,
    ln2_bias,
    w_gate_up,
    w_down,
):
    rows = tokens.shape[1]
    count = lax.axis_size("ctx")
    ctx = lax.axis_index("ctx")
    line = lax.axis_size("dp")
    here = lax.axis_index("dp")
    side = lax.axis_index("fsdp")
    shards = 2 * line
    depth = D // shards
    heads = H // count
    width = heads * E
    length = rows * count

    def reversed_bits(value):
        return sum(
            ((value >> i) & 1) * (count >> (i + 1)) for i in range(count.bit_length() - 1)
        )

    shard_of = [(r % line) * 2 + (side ^ (r // line)) for r in range(shards)]
    index = jnp.arange(1 + count + shards, dtype=jnp.int32)
    r = jnp.maximum(index - 1 - count, 0)
    places = jnp.where(
        index <= count,
        reversed_bits(jnp.clip(index - 1, 0, count - 1) ^ ctx),
        lax.rem(r, line) * 2 + (side ^ lax.div(r, line)),
    )
    places = jnp.where(index == 0, ctx, places).astype(jnp.int32)

    small = jnp.concatenate([ln1_gain, ln1_bias, ln2_gain, ln2_bias, b_qkv])
    pad = 16
    qkv_mine = take_columns(places, w_qkv, count, shards, 3, line, pad)
    lead = jnp.pad(small, (0, 2 * 3 * width - small.shape[0])).reshape(1, 2, 3 * width)
    lead = jnp.pad(lead, ((0, 0), (0, pad - 2), (0, 0)))
    qkv_mine = lax.dynamic_update_slice(
        qkv_mine, jnp.broadcast_to(lead, (line, pad, 3 * width)), (0, depth, 0)
    )

    def weight(blocks):
        near = to_line(blocks)
        return near, swap(near, "fsdp", 1)

    def row_copies(w, *after):
        block = hold(places, pick(w.reshape(count, -1, D), ctx, 0), *after)
        return jnp.broadcast_to(block[None], (line,) + block.shape)

    token_rows = jnp.concatenate(rows_gather(tokens[0]), axis=0)
    cot_rows = jnp.concatenate(
        rows_gather(hold(places, cotangent[0], token_rows)), axis=0
    )
    qkv_parts = weight(qkv_mine)
    gate_mine = take_pairs(places, w_gate_up, count, shards, (qkv_parts[0], token_rows))
    gate_up = lax.all_gather(gate_mine, ("dp", "fsdp"), axis=0, tiled=True)
    out_parts = weight(row_copies(w_out, qkv_parts[0], cot_rows))
    seg_row = lax.all_gather(segment_ids, "ctx", axis=1, tiled=True)
    seg_col = seg_row.reshape(length, 1)

    half = ROT // 2
    angles = np.arange(length)[:, None] * 10000.0 ** (-np.arange(half) * 2.0 / ROT)[None, :]
    cosine, sine = np.cos(angles), np.sin(angles)
    flat = np.zeros((length, E - ROT))
    zero = np.zeros((length, half))
    tables = [
        jnp.asarray(np.concatenate(parts * 2, axis=1), jnp.float32)
        for parts in ([cosine, cosine, flat + 1.0], [-sine, zero, flat], [zero, sine, flat])
    ]

    small_rows = [part[:, depth : depth + 2] for part in qkv_parts]
    small_all = jnp.concatenate(small_rows, axis=0).reshape(shards, -1)[:, : small.shape[0]]
    small_all = small_all.astype(jnp.float32)
    small_plain = sum(
        (jnp.arange(shards)[:, None] == shard_of[r]) * small_all[r][None, :] for r in range(shards)
    )
    gain_one, bias_one = small_all[:, :depth], small_all[:, depth : 2 * depth]
    gain_two = small_plain[:, 2 * depth : 3 * depth].reshape(1, D)
    bias_two = small_plain[:, 3 * depth : 4 * depth].reshape(1, D)
    bias_plain = small_plain[:, 4 * depth :]
    bias_mine = pick(bias_plain.reshape(3, shards, count, E), ctx, 2).reshape(3, 1, width)

    normed_one = norm_tokens(places, token_rows, gain_one, bias_one, count, (seg_row,))
    qkv = []
    for i in range(3):
        turns = tables if i < 2 else []
        qkv.append(
            project(places, normed_one, *qkv_parts, i, bias_mine[i], turns, qkv[-1:])
        )
    down_copies = row_copies(w_down, out_parts[0])
    size = down_copies.shape[1]
    down_left = to_line(down_copies[..., : D // 2])
    down_right = to_line(hold(places, down_copies[..., D // 2 :], down_left))
    attended, logs = attend(places, qkv, seg_col, seg_row, count, heads)
    product = row_product(places, attended, out_parts, count)
    pieces = rows_scatter(places, *product)
    hidden, normed_two = norm_hidden(places, tokens[0], pieces, gain_two, bias_two)
    normed_pieces = rows_gather(normed_two)
    down_left = hold(places, down_left, product[0])
    down_right = hold(places, down_right, normed_pieces[1])
    down_parts = (
        down_left,
        down_right,
        swap(down_left, "fsdp", 1),
        swap(down_right, "fsdp", 1),
    )
    normed_two, both, activ = gate_product(places, normed_pieces, gate_up)

    def line_sum(blocks, after=()):
        arrived = to_line(blocks).reshape(line, -1, blocks.shape[-1])
        return add(places, [(arrived, (i,)) for i in range(line)], after)

    def both_sides(kept, arrived):
        return (kept.astype(jnp.float32) + arrived.astype(jnp.float32)).astype(jnp.bfloat16)

    keep_left, keep_right, load_left, load_right = row_grad(
        places, activ, cot_rows, size, count, False
    )
    left_arrived = swap(load_left, "fsdp", 1)
    right_arrived = swap(load_right, "fsdp", 1)
    grad_both = gate_back(places, cot_rows, down_parts, both, count, (load_right,))
    gate_part = pairs_grad(places, normed_two, grad_both)
    gate_grad = lax.psum_scatter(gate_part, ("dp", "fsdp"), scatter_dimension=0, tiled=True)
    pieces = rows_scatter(places, *normed_grad(places, grad_both, gate_up, (gate_part,)))
    down_pieces = row_product(places, activ, down_parts, count, (pieces[1],))
    left_total = both_sides(keep_left, hold(places, left_arrived, down_pieces[0]))
    grad_hidden, grad_branch, sums_two = norm_back(
        places, hidden, pieces, gain_two, cotangent[0], 0, True, (down_pieces[0], left_total,)
    )
    down_pieces = rows_scatter(places, *down_pieces, (grad_branch,))
    branch_pieces = rows_gather(grad_branch)
    down_total = both_sides(keep_right, hold(places, right_arrived, branch_pieces[1]))
    grad_attended, grad_branch = grad_out(
        places, branch_pieces, *out_parts, count, ( down_total,)
    )
    out_keep, out_load = row_grad(
        places, attended, grad_branch, out_parts[0].shape[1], count, True, ()
    )
    out_arrived = swap(out_load, "fsdp", 1)
    grads = attend_back(
        places,
        qkv,
        grad_attended,
        logs,
        seg_col,
        seg_row,
        tables,
        count,
        heads,
        (out_load, down_pieces[-1]),
    )
    grads, bias_sums = grads[:3], grads[3]
    out_total = both_sides(out_keep, out_arrived)
    *loads, turned = column_loads(places, normed_one, grads, ())
    arrivals = [swap(load, "fsdp", 1) for load in loads]
    mixed = hidden + sum(piece[:rows].astype(jnp.float32) for piece in down_pieces)
    mixed = mixed.astype(jnp.bfloat16)
    left_grad = line_sum(left_total, (loads[2],))
    down_grad = jnp.concatenate([left_grad, line_sum(down_total, (loads[2],))], axis=1)

    def ctx_rows(block):
        return lax.all_gather(block, "ctx", axis=0, tiled=True)

    def keep(i, *after):
        total = column_keep(places, turned, grads[i], arrivals[i], after)
        return total.reshape(line, depth, width)

    totals = [jnp.concatenate([keep(0, down_grad), out_total], axis=1)]
    near, far = normed_grad_parts(places, grads, qkv_parts, count, (totals[0],))
    gate_grad = hold(places, gate_grad, loads[0])
    gate_rows = ctx_rows(gate_grad)
    gate_out = spread_pairs(places, gate_rows, count, shards)
    down_out = ctx_rows(hold(places, down_grad, totals[0])).astype(jnp.float32)
    totals.append(keep(1, gate_out))
    pieces = rows_scatter(places, near, far, (totals[0],))
    q_sum = line_sum(totals[0], (mixed,))
    totals.append(keep(2, down_out))
    input_grad, sums_one = norm_back(
        places, tokens[0], pieces, gain_one, grad_hidden, 1 + count, False, ()
    )
    out_out = ctx_rows(q_sum[depth:]).reshape(count, 4, -1, D // 4)
    out_out = out_out.transpose(0, 2, 1, 3).reshape(-1, D).astype(jnp.float32)
    sums = [q_sum[:depth], line_sum(totals[1], ()), line_sum(totals[2], (out_out, down_out, gate_out))]
    qkv_grads = [rows_gather(total) for total in sums]
    qkv_out = spread_columns(places, qkv_grads, count, shards)

    bias_part = jnp.where(
        jnp.arange(count)[None, None, :, None] == ctx, bias_sums.reshape(3, shards, 1, E), 0.0
    ).reshape(shards, 3 * depth)
    small_part = jnp.concatenate(
        [part.reshape(shards, depth) for part in (*sums_one, *sums_two)] + [bias_part], axis=1
    ).reshape(line, 2, -1)
    load = pick(small_part, 1 - side, 1).astype(jnp.bfloat16)
    total = pick(small_part, side, 1) + swap(load, "fsdp", 1).astype(jnp.float32)
    low_total = total.astype(jnp.bfloat16)
    mine = pick(total, here, 0)
    for r in range(1, line):
        mine = mine + swap(pick(low_total, here ^ r, 0), "dp", r).astype(jnp.float32)
    bit = count // 2
    while bit >= 1:
        mine = mine + swap(mine, "ctx", bit)
        bit //= 2

    return (
        mixed[None],
        input_grad[None],
        mine[:depth],
        mine[depth : 2 * depth],
        qkv_out,
        mine[4 * depth :],
        out_out,
        mine[2 * depth : 3 * depth],
        mine[3 * depth : 4 * depth],
        gate_out,
        down_out,
    )


def fits(mesh):
    count, shards = mesh.shape["ctx"], mesh.shape["dp"] * mesh.shape["fsdp"]
    return (
        mesh.shape["fsdp"] == 2
        and count > 1
        and count & (count - 1) == 0
        and (H // shards) == count
        and (FF // shards) % (16 * count) == 0
        and (FF // count) % 128 == 0
        and (H // count) % 2 == 0
    )


def solution(mesh):
    shards = ("dp", "fsdp")
    row = P(shards, "ctx", None)
    vector = P(shards)
    matrix = P(shards, None)
    return jax.shard_map(
        fast_body if fits(mesh) else body,
        mesh=mesh,
        in_specs=(
            row,
            P(shards, "ctx"),
            row,
            vector,
            vector,
            matrix,
            vector,
            matrix,
            vector,
            vector,
            matrix,
            matrix,
        ),
        out_specs=(
            row,
            row,
            vector,
            vector,
            matrix,
            vector,
            matrix,
            vector,
            vector,
            matrix,
            matrix,
        ),
        check_vma=False,
    )
```
